32 devices in a mesh: prow: 8 (over y, x, core), pcol: 4 (over z).
Axes of the slice: x: 2, y: 2, z: 4, core: 2. Of those that a mesh axis runs over, the one named last changes fastest.
Arguments:
- slab: float32 [8192, 1024], P('prow', 'pcol'), may hold values from -6 to 6
- panel: float32 [8192, 256], P('prow', 'pcol'), may hold values from -0.1875 to 0.1875
- pivots: int32 [256], replicated, may hold values from 256 to 8191, as said below
Outputs:
- result: float32 [8192, 1024], P('prow', 'pcol')
The draws below stay inside these ranges and needn't reach their ends.
Inputs may be any that keep to these rules, and one draw needn't show every extreme that they name: `pivots`: 256 distinct rows, none among the first 256; at most 32 of them lie in the 1024 rows of one process row, and some process row holds exactly 32.
All inputs are finite; a program needn't handle non-finite values.
Results may differ from the reference program's by a relative error of at most 0.00005.
Values sent between devices are 32-bit elements; how exact they have to be, the bound alone decides.
No kernel may reach another device: no remote copies, remote signals or barrier semaphores. Data moves between devices by JAX's collectives and lax.ppermute only.
A program may use at most 64 MiB of HBM per device.

```python
import jax
import jax.numpy as jnp
from jax import lax

NB = 256
ROWS = 1024
CAP = 32
M = 8192
NS = 1024
N_PROW = 8


def draw_pivots(key, part):
    total_slots = N_PROW * CAP
    heavy_row = jax.random.randint(jax.random.fold_in(key, 11), (), 0, N_PROW)
    slot_order = jax.random.permutation(jax.random.fold_in(key, 12), total_slots)
    slot_owner = slot_order // CAP
    slot_score = jnp.where(slot_owner == heavy_row, 0, total_slots) + jnp.arange(total_slots)
    ranked = slot_order[jnp.argsort(slot_score, stable=True)]
    chosen = jax.random.permutation(jax.random.fold_in(key, 13), ranked[:NB])
    owner_row = chosen // CAP
    slot_index = chosen % CAP
    stride = (ROWS - NB) // CAP
    jitter = jax.random.randint(jax.random.fold_in(key, 14), (NB,), 0, stride)
    return (owner_row * ROWS + NB + slot_index * stride + jitter).astype(jnp.int32)


def shard_levels(rng, shape, pieces, low, high):
    level = 1.0
    for dim, shards_of in pieces:
        steps = jax.random.uniform(jax.random.fold_in(jax.random.fold_in(rng, 6), dim), (shards_of,), jnp.float32, low / len(pieces), high / len(pieces))
        level = level * jnp.repeat(jnp.exp(steps), shape[dim] // shards_of).reshape((-1,) + (1,) * (len(shape) - 1 - dim))
    return level


def scatter_about(rng, extent, deviation, most, cuts=(), dtype=jnp.bfloat16):
    drawn = jax.random.normal(rng, extent, jnp.float32) * deviation
    if len(cuts) > 0:
        drawn = shard_levels(rng, extent, cuts, -0.22, 0.18) * drawn
    return jnp.clip(drawn, min=-most, max=most).astype(dtype)


def setup_inputs(seed: int = 0) -> dict:
    keys = jax.random.split(jax.random.key(seed), 4)
    return {
        "slab": scatter_about(keys[0], (M, NS), 1.0, 6.0, ((0, 8), (1, 4)), jnp.float32),
        "panel": scatter_about(keys[1], (M, NB), (4 * NB) ** -0.5, 0.1875, ((0, 8), (1, 4)), jnp.float32),
        "pivots": draw_pivots(jax.random.fold_in(keys[3], 71), 0),
    }


def reference(slab, panel, pivots):
    leading = slab[:NB]
    pivot_rows = slab[pivots]
    swapped = slab.at[pivots].set(leading)
    diag_block = panel[:NB]
    upper_rows = jax.scipy.linalg.solve_triangular(diag_block, pivot_rows, lower=True, unit_diagonal=True)
    update = jnp.dot(panel.astype(jnp.float32), upper_rows.astype(jnp.float32), precision=lax.Precision.HIGHEST, preferred_element_type=jnp.float32)
    result = swapped - update
    return result.at[:NB].set(upper_rows)
```

```python
import functools

import jax
import jax.numpy as jnp
from jax import lax
from jax.experimental import pallas as pl
from jax.experimental.pallas import tpu as pltpu
from jax.sharding import PartitionSpec as P

CAP = 32
BLOCK = 32
F32 = jnp.float32
BF16 = jnp.bfloat16
VMEM = pl.BlockSpec(memory_space=pltpu.VMEM)
PARAMS = pltpu.CompilerParams(vmem_limit_bytes=24 * 1024 * 1024)


def split3(x):
    high = x.astype(BF16)
    rest = x - high.astype(F32)
    mid = rest.astype(BF16)
    low = (rest - mid.astype(F32)).astype(BF16)
    return high, mid, low


def split2(x):
    high = x.astype(BF16)
    return high, (x - high.astype(F32)).astype(BF16)


def select_rows(one_hot, x):
    return sum(jnp.dot(one_hot, part, preferred_element_type=F32) for part in split3(x))


def dot_full(a, b):
    return jnp.dot(a, b, precision=lax.Precision.HIGHEST, preferred_element_type=F32)


def tree_partner(r, span):
    if span == 1 or r % span > 1:
        return r ^ 1
    if r % 2 == 0:
        return r + 1 if r & span else r + span
    return r - span if r & span else r - 1


def lead_place(owner, n):
    bits = n.bit_length() - 1
    return sum((lax.shift_right_logical(owner, bit) & 1) * (1 << (bits - 1 - bit)) for bit in range(bits))


def slots(pivot_row, rows):
    width = pivot_row.shape[1]
    by_sublane = jnp.broadcast_to(pivot_row, (width, width)).T
    shift = rows.bit_length() - 1
    owner_row = jnp.broadcast_to(lax.shift_right_logical(pivot_row, shift), (width, width))
    owner_col = lax.shift_right_logical(by_sublane, shift)
    sub = lax.broadcasted_iota(jnp.int32, (width, width), 0)
    lane = lax.broadcasted_iota(jnp.int32, (width, width), 1)
    same = owner_row == owner_col
    rank_row = jnp.sum(jnp.where(same & (sub < lane), 1, 0), axis=0, keepdims=True)
    rank_col = jnp.sum(jnp.where(same & (lane < sub), 1, 0), axis=1, keepdims=True)
    return owner_row[:1], rank_row, owner_col[:, :1], rank_col


def pack_kernel(pivot_ref, slab_ref, packed_ref, lead_ref, local_ref):
    rows = slab_ref.shape[0]
    width = pivot_ref.shape[1]
    count = lead_ref.shape[0]
    lanes = local_ref.shape[1]
    me = lax.axis_index("prow")
    pivot_row = pivot_ref[...]
    owner_row, rank_row, owner_col, rank_col = slots(pivot_row, rows)
    pivot_col = jnp.broadcast_to(pivot_row, (lanes, width)).T
    slot = lax.broadcasted_iota(jnp.int32, (width, lanes), 1)
    mine = (owner_col == me) & (rank_col == slot)
    local = jnp.sum(jnp.where(mine, pivot_col - (me + 1) * rows, 0), axis=0, keepdims=True) + rows
    local_ref[...] = local
    slot = lax.broadcasted_iota(jnp.int32, (CAP, width), 0)
    mine = (owner_row == me) & (rank_row == slot)
    local = jnp.sum(jnp.where(mine, pivot_row - (me + 1) * rows, 0), axis=1, keepdims=True) + rows
    one_hot = (lax.broadcasted_iota(jnp.int32, (CAP, rows), 1) == local).astype(F32).astype(BF16)
    packed_ref[...] = select_rows(one_hot, slab_ref[...])
    slot = lax.broadcasted_iota(jnp.int32, (count, width), 0)
    one_hot = (slot == lead_place(owner_row, count // CAP) * CAP + rank_row).astype(F32).astype(BF16)
    lead_ref[...] = select_rows(one_hot, slab_ref[:width, :])


def block_inverses(lower):
    width = lower.shape[0]
    lane = lax.broadcasted_iota(jnp.int32, (BLOCK, width), 1)
    sub = lax.broadcasted_iota(jnp.int32, (BLOCK, width), 0)
    block = lane // BLOCK
    within = lane % BLOCK
    diag = jnp.zeros((BLOCK, width), F32)
    for b in range(width // BLOCK):
        diag = jnp.where(block == b, lower[b * BLOCK : (b + 1) * BLOCK], diag)
    diag = jnp.where(within < sub, diag, 0.0)
    inv = jnp.where(within == sub, 1.0, 0.0).astype(F32)
    half = 128
    first = (lax.broadcasted_iota(jnp.int32, (BLOCK, half), 1) // BLOCK) * BLOCK
    outs = []
    for h in range(0, width, half):
        d, x = diag[:, h : h + half], inv[:, h : h + half]
        for k in range(BLOCK - 1):
            column = jnp.take_along_axis(d, first + k, axis=1)
            x = x - column * x[k : k + 1, :]
        outs.append(x)
    return outs


def order_kernel(n, rows, pivot_ref, gathered_ref, out_ref, gathered):
    width = pivot_ref.shape[1]
    me = lax.axis_index("prow")
    for q in range(n):
        source = jnp.bitwise_xor(me, q)
        gathered[pl.ds(pl.multiple_of(source * CAP, CAP), CAP), :] = gathered_ref[q * CAP : (q + 1) * CAP, :]
    _, _, owner_col, rank_col = slots(pivot_ref[...], rows)
    slot = lax.broadcasted_iota(jnp.int32, (width, gathered.shape[0]), 1)
    one_hot = (slot == owner_col * CAP + rank_col).astype(F32).astype(BF16)
    out_ref[...] = select_rows(one_hot, gathered[...])


def top_order(m):
    return [0, 1, *range(m - 1, 1, -1)]


def cut_kernel(panel_ref, top_ref, rest_ref, sems):
    width = top_ref.shape[1]
    copies = []
    for c in range(sems.shape[0]):
        target = rest_ref.at[:, pl.ds((c - 1) * width, width)] if c else top_ref
        copies.append(pltpu.make_async_copy(panel_ref.at[:, pl.ds(c * width, width)], target, sems.at[c]))
        copies[-1].start()
    for copy in copies:
        copy.wait()


def assemble_kernel(m, *refs):
    *pieces, out_ref, lower_t = refs
    width = lower_t.shape[0]
    piece = width // m
    half = width // 2
    z = lax.axis_index("pcol")
    for d, ref in zip(top_order(m), pieces):
        lower_t[pl.ds(pl.multiple_of(jnp.bitwise_xor(z, d) * piece, piece), piece), :] = ref[...]
    out_ref[:half, :] = lower_t[:half, :]
    out_ref[half:, :half] = lower_t[half : half + half // 2, half:]
    out_ref[half:, half:] = lower_t[half + half // 2 :, half:]


def pick_kernel(span, moved_ref, held_ref, out_ref):
    child = lax.rem(lax.axis_index("prow"), 2 * span) == span

    @pl.when(child)
    def _():
        out_ref[...] = moved_ref[...]

    @pl.when(jnp.logical_not(child))
    def _():
        out_ref[...] = held_ref[...]


def invert_kernel(lower_ref, out_ref, lower_t):
    width = lower_t.shape[0]
    half = width // 2
    lower_t[:half, :] = lower_ref[:half, :]
    lower_t[half:, :half] = jnp.zeros((half, half), F32)
    lower_t[half : half + half // 2, half:] = lower_ref[half:, :half]
    lower_t[half + half // 2 :, half:] = lower_ref[half:, half:]
    lower = lower_t[...].T
    blocks = block_inverses(lower)
    row = lax.broadcasted_iota(jnp.int32, (half, half), 0)
    col = lax.broadcasted_iota(jnp.int32, (half, half), 1)
    for h, strip in enumerate(blocks):
        corner = lower[h * half : (h + 1) * half, h * half : (h + 1) * half]
        inv = jnp.where(row // BLOCK == col // BLOCK, jnp.concatenate([strip] * (half // BLOCK), axis=0), 0.0)
        size = BLOCK
        while size < half:
            off = (row // (2 * size) == col // (2 * size)) & (row // size > col // size)
            inv = inv - dot_full(dot_full(inv, jnp.where(off, corner, 0.0)), inv)
            size *= 2
        out_ref[:half, h * half : (h + 1) * half] = inv
    out_ref[half:, :half] = lower[half : half + half // 2, :half]
    out_ref[half:, half:] = lower[half + half // 2 :, :half]


def solve_kernel(inverse_ref, pivot_rows_ref, x_ref):
    half = pivot_rows_ref.shape[0] // 2
    quarter = jnp.concatenate([inverse_ref[half:, :half], inverse_ref[half:, half:]], axis=0)
    first = dot_full(inverse_ref[:half, :half], pivot_rows_ref[:half, :])
    x_ref[:half, :] = first
    x_ref[half:, :] = dot_full(inverse_ref[:half, half:], pivot_rows_ref[half:, :] - dot_full(quarter, first))


def product(piece, upper):
    high, low = split2(piece)
    upper_high, upper_low = split2(upper)
    left = jnp.concatenate([high, high, low], axis=0)
    right = jnp.concatenate([upper_high, upper_low, upper_high], axis=0)
    return lax.dot_general(left, right, (((0,), (0,)), ((), ())), preferred_element_type=F32)


def piece_rows(x_ref, m, d):
    piece = x_ref.shape[0] // m
    source = jnp.bitwise_xor(lax.axis_index("pcol"), d)
    return x_ref[pl.ds(pl.multiple_of(source * piece, piece), piece), :]


def update_kernel(m, local_ref, lead_ref, x_ref, slab_ref, *refs):
    *pieces, out_ref, result, sems = refs
    tops, rests = dict(zip(top_order(m), pieces[:m])), pieces[m:]
    rows, cols = slab_ref.shape
    width = x_ref.shape[0]
    result[:rows, :] = slab_ref[...]
    for s in range(CAP):
        result[pl.ds(local_ref[0, s], 1), :] = lead_ref[pl.ds(s, 1), :]
    uppers = [piece_rows(x_ref, m, d) for d in range(m)]
    copies = []
    for c in range(rows // width):
        part = pl.ds(c * width, width)
        total = result[part, :]
        for d, upper in enumerate(uppers):
            piece = rests[d][:, (c - 1) * width : c * width] if c else tops[d][...]
            total = total - product(piece, upper)
        result[part, :] = total
        if c == 0:

            @pl.when(lax.axis_index("prow") == 0)
            def _():
                result[part, :] = x_ref[...]

        copy = pltpu.make_async_copy(result.at[part], out_ref.at[part], sems.at[c])
        copy.start()
        copies.append(copy)
    for copy in copies:
        copy.wait()


def unit(held, steps, *operands):
    shapes = jax.eval_shape(steps, *operands)
    return lax.cond(held, steps, lambda *_: jax.tree.map(lambda s: jnp.zeros(s.shape, s.dtype), shapes), *operands)


def call(kernel, outs, operands, in_specs=None, out_specs=None, scratch=()):
    return pl.pallas_call(
        kernel,
        out_shape=outs,
        in_specs=in_specs or [VMEM] * len(operands),
        out_specs=out_specs or jax.tree.map(lambda _: VMEM, outs),
        scratch_shapes=list(scratch),
        compiler_params=PARAMS,
        cost_estimate=pl.CostEstimate(flops=1, bytes_accessed=1, transcendentals=0),
    )(*operands)


def local(n, m, slab, panel, pivots):
    rows, cols = slab.shape
    width = pivots.shape[0]
    piece = panel.shape[1]
    me = lax.axis_index("prow")
    panel_t = panel.T
    pivot_row = pivots.reshape(1, width)

    def spread(block, order):
        return [block] + [lax.ppermute(block, "pcol", [(c, c ^ d) for c in range(m)]) for d in order]

    top, rest = call(
        cut_kernel,
        (jax.ShapeDtypeStruct((piece, width), F32), jax.ShapeDtypeStruct((piece, rows - width), F32)),
        (panel_t,),
        in_specs=[pl.BlockSpec(memory_space=pl.ANY)],
        scratch=[pltpu.SemaphoreType.DMA((rows // width,))],
    )
    tops, rests = spread(top, top_order(m)[1:]), spread(rest, range(1, m))

    gathered, leading, local_rows = call(
        pack_kernel,
        (
            jax.ShapeDtypeStruct((CAP, cols), F32),
            jax.ShapeDtypeStruct((n * CAP, cols), F32),
            jax.ShapeDtypeStruct((1, 128), jnp.int32),
        ),
        (pivot_row, slab),
    )
    lower = call(
        functools.partial(assemble_kernel, m),
        jax.ShapeDtypeStruct((width * 3 // 4, width), F32),
        tops,
        scratch=[pltpu.VMEM((width, width), F32)],
    )

    def split(leading):
        blocks = leading.reshape(2, -1, cols)
        return blocks[0], blocks[1]

    def levels(lower, gathered, leading):
        kept, sent = split(leading)
        moved = lax.ppermute(sent, "prow", [(r, r ^ 1) for r in range(n)])
        leading = jnp.where(me & 1 != 0, moved, kept)
        span, other = n // 2, 2
        while span > 1:
            moved = lax.ppermute(lower, "prow", [(r, tree_partner(r, span)) for r in range(n)])
            lower = call(
                functools.partial(pick_kernel, span),
                jax.ShapeDtypeStruct(lower.shape, F32),
                (moved, lower),
            )
            kept, sent = split(leading)
            count = gathered.shape[0]
            message = jnp.concatenate([gathered, sent], axis=0)
            moved = lax.ppermute(message, "prow", [(r, r ^ other) for r in range(n)])
            gathered = jnp.concatenate([gathered, moved[:count]], axis=0)
            leading = jnp.where(me & other != 0, moved[count:], kept)
            span, other = span // 2, other * 2
        pivot_rows = call(
            functools.partial(order_kernel, n, rows),
            jax.ShapeDtypeStruct((width, cols), F32),
            (pivot_row, gathered),
            scratch=[pltpu.VMEM((n * CAP, cols), F32)],
        )
        inverse = call(
            invert_kernel,
            jax.ShapeDtypeStruct(lower.shape, F32),
            (lower,),
            scratch=[pltpu.VMEM((width, width), F32)],
        )
        moved = lax.ppermute(inverse, "prow", [(r, r ^ 1) for r in range(n)])
        inverse = jnp.where(me & 1 != 0, moved, inverse)
        return leading, call(solve_kernel, jax.ShapeDtypeStruct((width, cols), F32), (inverse, pivot_rows))

    gathered, lower = lax.optimization_barrier((gathered, lower))
    moved = lax.ppermute(jnp.concatenate([gathered, gathered], axis=0), "prow", [(r, r ^ 1) for r in range(n)])
    gathered = jnp.concatenate([gathered, moved[:CAP]], axis=0)
    leading, upper_rows = unit(me < n, levels, lower, gathered, leading)
    return call(
        functools.partial(update_kernel, m),
        jax.ShapeDtypeStruct((rows, cols), F32),
        (local_rows, leading, upper_rows, slab, *tops, *rests),
        in_specs=[pl.BlockSpec(memory_space=pltpu.SMEM)] + [VMEM] * (2 * m + 3),
        out_specs=pl.BlockSpec(memory_space=pl.ANY),
        scratch=[pltpu.VMEM((rows + 8, cols), F32), pltpu.SemaphoreType.DMA((rows // width,))],
    )


def solution(mesh):
    return jax.shard_map(
        functools.partial(local, mesh.shape["prow"], mesh.shape["pcol"]),
        mesh=mesh,
        in_specs=(P("prow", "pcol"), P("prow", "pcol"), P()),
        out_specs=P("prow", "pcol"),
        check_vma=False,
    )
```

```python
import functools

import jax
import jax.numpy as jnp
from jax import lax
from jax.experimental import pallas as pl
from jax.experimental.pallas import tpu as pltpu
from jax.sharding import PartitionSpec as P

CAP = 32
BLOCK = 32
F32 = jnp.float32
BF16 = jnp.bfloat16
VMEM = pl.BlockSpec(memory_space=pltpu.VMEM)
PARAMS = pltpu.CompilerParams(vmem_limit_bytes=24 * 1024 * 1024)


def split3(x):
    high = x.astype(BF16)
    rest = x - high.astype(F32)
    mid = rest.astype(BF16)
    low = (rest - mid.astype(F32)).astype(BF16)
    return high, mid, low


def split2(x):
    high = x.astype(BF16)
    return high, (x - high.astype(F32)).astype(BF16)


def select_rows(one_hot, x):
    return sum(jnp.dot(one_hot, part, preferred_element_type=F32) for part in split3(x))


def dot_full(a, b):
    return jnp.dot(a, b, precision=lax.Precision.HIGHEST, preferred_element_type=F32)


def tree_partner(r, span):
    if span == 1 or r % span > 1:
        return r ^ 1
    if r % 2 == 0:
        return r + 1 if r & span else r + span
    return r - span if r & span else r - 1


def lead_place(owner, n):
    bits = n.bit_length() - 1
    return sum((lax.shift_right_logical(owner, bit) & 1) * (1 << (bits - 1 - bit)) for bit in range(bits))


def slots(pivot_row, rows):
    width = pivot_row.shape[1]
    by_sublane = jnp.broadcast_to(pivot_row, (width, width)).T
    shift = rows.bit_length() - 1
    owner_row = jnp.broadcast_to(lax.shift_right_logical(pivot_row, shift), (width, width))
    owner_col = lax.shift_right_logical(by_sublane, shift)
    sub = lax.broadcasted_iota(jnp.int32, (width, width), 0)
    lane = lax.broadcasted_iota(jnp.int32, (width, width), 1)
    same = owner_row == owner_col
    rank_row = jnp.sum(jnp.where(same & (sub < lane), 1, 0), axis=0, keepdims=True)
    rank_col = jnp.sum(jnp.where(same & (lane < sub), 1, 0), axis=1, keepdims=True)
    return owner_row[:1], rank_row, owner_col[:, :1], rank_col


def pack_kernel(pivot_ref, slab_ref, packed_ref, lead_ref, local_ref, held, sems):
    parts = sems.shape[0]
    copies = []
    for p in range(parts):
        part = pl.ds(p * (slab_ref.shape[0] // parts), slab_ref.shape[0] // parts)
        copies.append(pltpu.make_async_copy(slab_ref.at[part], held.at[part], sems.at[p]))
        copies[-1].start()
    rows = slab_ref.shape[0]
    width = pivot_ref.shape[1]
    count = lead_ref.shape[0]
    lanes = local_ref.shape[1]
    me = lax.axis_index("prow")
    pivot_row = pivot_ref[...]
    owner_row, rank_row, owner_col, rank_col = slots(pivot_row, rows)
    pivot_col = jnp.broadcast_to(pivot_row, (lanes, width)).T
    slot = lax.broadcasted_iota(jnp.int32, (width, lanes), 1)
    mine = (owner_col == me) & (rank_col == slot)
    local = jnp.sum(jnp.where(mine, pivot_col - (me + 1) * rows, 0), axis=0, keepdims=True) + rows
    local_ref[...] = local
    slot = lax.broadcasted_iota(jnp.int32, (CAP, width), 0)
    mine = (owner_row == me) & (rank_row == slot)
    local = jnp.sum(jnp.where(mine, pivot_row - (me + 1) * rows, 0), axis=1, keepdims=True) + rows
    mine = (lax.broadcasted_iota(jnp.int32, (CAP, rows), 1) == local).astype(F32).astype(BF16)
    slot = lax.broadcasted_iota(jnp.int32, (count, width), 0)
    lead = (slot == lead_place(owner_row, count // CAP) * CAP + rank_row).astype(F32).astype(BF16)
    for copy in copies:
        copy.wait()
    packed_ref[...] = select_rows(mine, held[...])
    lead_ref[...] = select_rows(lead, held[:width, :])


def block_inverses(lower):
    width = lower.shape[0]
    lane = lax.broadcasted_iota(jnp.int32, (BLOCK, width), 1)
    sub = lax.broadcasted_iota(jnp.int32, (BLOCK, width), 0)
    block = lane // BLOCK
    within = lane % BLOCK
    diag = jnp.zeros((BLOCK, width), F32)
    for b in range(width // BLOCK):
        diag = jnp.where(block == b, lower[b * BLOCK : (b + 1) * BLOCK], diag)
    diag = jnp.where(within < sub, diag, 0.0)
    inv = jnp.where(within == sub, 1.0, 0.0).astype(F32)
    half = 128
    first = (lax.broadcasted_iota(jnp.int32, (BLOCK, half), 1) // BLOCK) * BLOCK
    outs = []
    for h in range(0, width, half):
        d, x = diag[:, h : h + half], inv[:, h : h + half]
        for k in range(BLOCK - 1):
            column = jnp.take_along_axis(d, first + k, axis=1)
            x = x - column * x[k : k + 1, :]
        outs.append(x)
    return outs


def order_kernel(n, rows, pivot_ref, gathered_ref, out_ref, gathered):
    width = pivot_ref.shape[1]
    me = lax.axis_index("prow")
    for q in range(n):
        source = jnp.bitwise_xor(me, q)
        gathered[pl.ds(pl.multiple_of(source * CAP, CAP), CAP), :] = gathered_ref[q * CAP : (q + 1) * CAP, :]
    _, _, owner_col, rank_col = slots(pivot_ref[...], rows)
    slot = lax.broadcasted_iota(jnp.int32, (width, gathered.shape[0]), 1)
    one_hot = (slot == owner_col * CAP + rank_col).astype(F32).astype(BF16)
    out_ref[...] = select_rows(one_hot, gathered[...])


def top_order(m):
    return [0, 1, *range(m - 1, 1, -1)]


def cut_kernel(panel_ref, top_ref, rest_ref, sems):
    width = top_ref.shape[1]
    copies = []
    for c in range(sems.shape[0]):
        target = rest_ref.at[:, pl.ds((c - 1) * width, width)] if c else top_ref
        copies.append(pltpu.make_async_copy(panel_ref.at[:, pl.ds(c * width, width)], target, sems.at[c]))
        copies[-1].start()
    for copy in copies:
        copy.wait()


def assemble_kernel(m, *refs):
    *pieces, out_ref, lower_t = refs
    width = lower_t.shape[0]
    piece = width // m
    half = width // 2
    z = lax.axis_index("pcol")
    for d, ref in zip(top_order(m), pieces):
        lower_t[pl.ds(pl.multiple_of(jnp.bitwise_xor(z, d) * piece, piece), piece), :] = ref[...]
    out_ref[:half, :] = lower_t[:half, :]
    out_ref[half:, :half] = lower_t[half : half + half // 2, half:]
    out_ref[half:, half:] = lower_t[half + half // 2 :, half:]


def pick_kernel(span, moved_ref, held_ref, out_ref):
    child = lax.rem(lax.axis_index("prow"), 2 * span) == span

    @pl.when(child)
    def _():
        out_ref[...] = moved_ref[...]

    @pl.when(jnp.logical_not(child))
    def _():
        out_ref[...] = held_ref[...]


def invert_kernel(lower_ref, out_ref, lower_t):
    width = lower_t.shape[0]
    half = width // 2
    lower_t[:half, :] = lower_ref[:half, :]
    lower_t[half:, :half] = jnp.zeros((half, half), F32)
    lower_t[half : half + half // 2, half:] = lower_ref[half:, :half]
    lower_t[half + half // 2 :, half:] = lower_ref[half:, half:]
    lower = lower_t[...].T
    blocks = block_inverses(lower)
    row = lax.broadcasted_iota(jnp.int32, (half, half), 0)
    col = lax.broadcasted_iota(jnp.int32, (half, half), 1)
    for h, strip in enumerate(blocks):
        corner = lower[h * half : (h + 1) * half, h * half : (h + 1) * half]
        inv = jnp.where(row // BLOCK == col // BLOCK, jnp.concatenate([strip] * (half // BLOCK), axis=0), 0.0)
        size = BLOCK
        while size < half:
            off = (row // (2 * size) == col // (2 * size)) & (row // size > col // size)
            inv = inv - dot_full(dot_full(inv, jnp.where(off, corner, 0.0)), inv)
            size *= 2
        out_ref[:half, h * half : (h + 1) * half] = inv
    out_ref[half:, :half] = lower[half : half + half // 2, :half]
    out_ref[half:, half:] = lower[half + half // 2 :, :half]


def solve_kernel(inverse_ref, pivot_rows_ref, x_ref):
    half = pivot_rows_ref.shape[0] // 2
    quarter = jnp.concatenate([inverse_ref[half:, :half], inverse_ref[half:, half:]], axis=0)
    first = dot_full(inverse_ref[:half, :half], pivot_rows_ref[:half, :])
    x_ref[:half, :] = first
    x_ref[half:, :] = dot_full(inverse_ref[:half, half:], pivot_rows_ref[half:, :] - dot_full(quarter, first))


def product(piece, upper):
    high, low = split2(piece)
    upper_high, upper_low = split2(upper)
    left = jnp.concatenate([high, high, low], axis=0)
    right = jnp.concatenate([upper_high, upper_low, upper_high], axis=0)
    return lax.dot_general(left, right, (((0,), (0,)), ((), ())), preferred_element_type=F32)


def piece_rows(x_ref, m, d):
    piece = x_ref.shape[0] // m
    source = jnp.bitwise_xor(lax.axis_index("pcol"), d)
    return x_ref[pl.ds(pl.multiple_of(source * piece, piece), piece), :]


def update_kernel(m, local_ref, lead_ref, x_ref, slab_ref, *refs):
    *pieces, out_ref, result, sems = refs
    tops, rests = dict(zip(top_order(m), pieces[:m])), pieces[m:]
    rows, cols = slab_ref.shape
    width = x_ref.shape[0]
    result[:rows, :] = slab_ref[...]
    for s in range(CAP):
        result[pl.ds(local_ref[0, s], 1), :] = lead_ref[pl.ds(s, 1), :]
    uppers = [piece_rows(x_ref, m, d) for d in range(m)]
    copies = []
    for c in range(rows // width):
        part = pl.ds(c * width, width)
        total = result[part, :]
        for d, upper in enumerate(uppers):
            piece = rests[d][:, (c - 1) * width : c * width] if c else tops[d][...]
            total = total - product(piece, upper)
        result[part, :] = total
        if c == 0:

            @pl.when(lax.axis_index("prow") == 0)
            def _():
                result[part, :] = x_ref[...]

        copy = pltpu.make_async_copy(result.at[part], out_ref.at[part], sems.at[c])
        copy.start()
        copies.append(copy)
    for copy in copies:
        copy.wait()


def unit(held, steps, *operands):
    shapes = jax.eval_shape(steps, *operands)
    return lax.cond(held, steps, lambda *_: jax.tree.map(lambda s: jnp.zeros(s.shape, s.dtype), shapes), *operands)


def call(kernel, outs, operands, in_specs=None, out_specs=None, scratch=()):
    return pl.pallas_call(
        kernel,
        out_shape=outs,
        in_specs=in_specs or [VMEM] * len(operands),
        out_specs=out_specs or jax.tree.map(lambda _: VMEM, outs),
        scratch_shapes=list(scratch),
        compiler_params=PARAMS,
        cost_estimate=pl.CostEstimate(flops=1, bytes_accessed=1, transcendentals=0),
    )(*operands)


def local(n, m, slab, panel, pivots):
    rows, cols = slab.shape
    width = pivots.shape[0]
    piece = panel.shape[1]
    me = lax.axis_index("prow")
    panel_t = panel.T
    pivot_row = pivots.reshape(1, width)

    def spread(block, order):
        return [block] + [lax.ppermute(block, "pcol", [(c, c ^ d) for c in range(m)]) for d in order]

    def cut(panel_t):
        return call(
            cut_kernel,
            (jax.ShapeDtypeStruct((piece, width), F32), jax.ShapeDtypeStruct((piece, rows - width), F32)),
            (panel_t,),
            in_specs=[pl.BlockSpec(memory_space=pl.ANY)],
            scratch=[pltpu.SemaphoreType.DMA((rows // width,))],
        )

    top, rest = unit(me < n, cut, panel_t)
    tops, rests = spread(top, top_order(m)[1:]), spread(rest, range(1, m))

    def pack(pivot_row, slab):
        return call(
            pack_kernel,
            (
                jax.ShapeDtypeStruct((CAP, cols), F32),
                jax.ShapeDtypeStruct((n * CAP, cols), F32),
                jax.ShapeDtypeStruct((1, 128), jnp.int32),
            ),
            (pivot_row, slab),
            in_specs=[VMEM, pl.BlockSpec(memory_space=pl.ANY)],
            scratch=[pltpu.VMEM((rows, cols), F32), pltpu.SemaphoreType.DMA((8,))],
        )

    gathered, leading, local_rows = unit(me < n, pack, pivot_row, slab)
    lower = call(
        functools.partial(assemble_kernel, m),
        jax.ShapeDtypeStruct((width * 3 // 4, width), F32),
        tops,
        scratch=[pltpu.VMEM((width, width), F32)],
    )

    def split(leading):
        blocks = leading.reshape(2, -1, cols)
        return blocks[0], blocks[1]

    def levels(lower, gathered, leading):
        kept, sent = split(leading)
        moved = lax.ppermute(sent, "prow", [(r, r ^ 1) for r in range(n)])
        leading = jnp.where(me & 1 != 0, moved, kept)
        span, other = n // 2, 2
        while span > 1:
            moved = lax.ppermute(lower, "prow", [(r, tree_partner(r, span)) for r in range(n)])
            lower = call(
                functools.partial(pick_kernel, span),
                jax.ShapeDtypeStruct(lower.shape, F32),
                (moved, lower),
            )
            kept, sent = split(leading)
            count = gathered.shape[0]
            message = jnp.concatenate([gathered, sent], axis=0)
            moved = lax.ppermute(message, "prow", [(r, r ^ other) for r in range(n)])
            gathered = jnp.concatenate([gathered, moved[:count]], axis=0)
            leading = jnp.where(me & other != 0, moved[count:], kept)
            span, other = span // 2, other * 2
        pivot_rows = call(
            functools.partial(order_kernel, n, rows),
            jax.ShapeDtypeStruct((width, cols), F32),
            (pivot_row, gathered),
            scratch=[pltpu.VMEM((n * CAP, cols), F32)],
        )
        inverse = call(
            invert_kernel,
            jax.ShapeDtypeStruct(lower.shape, F32),
            (lower,),
            scratch=[pltpu.VMEM((width, width), F32)],
        )
        moved = lax.ppermute(inverse, "prow", [(r, r ^ 1) for r in range(n)])
        inverse = jnp.where(me & 1 != 0, moved, inverse)
        return leading, call(solve_kernel, jax.ShapeDtypeStruct((width, cols), F32), (inverse, pivot_rows))

    gathered, lower = lax.optimization_barrier((gathered, lower))
    moved = lax.ppermute(jnp.concatenate([gathered, gathered], axis=0), "prow", [(r, r ^ 1) for r in range(n)])
    gathered = jnp.concatenate([gathered, moved[:CAP]], axis=0)
    leading, upper_rows = unit(me < n, levels, lower, gathered, leading)
    return call(
        functools.partial(update_kernel, m),
        jax.ShapeDtypeStruct((rows, cols), F32),
        (local_rows, leading, upper_rows, slab, *tops, *rests),
        in_specs=[pl.BlockSpec(memory_space=pltpu.SMEM)] + [VMEM] * (2 * m + 3),
        out_specs=pl.BlockSpec(memory_space=pl.ANY),
        scratch=[pltpu.VMEM((rows + 8, cols), F32), pltpu.SemaphoreType.DMA((rows // width,))],
    )


def solution(mesh):
    return jax.shard_map(
        functools.partial(local, mesh.shape["prow"], mesh.shape["pcol"]),
        mesh=mesh,
        in_specs=(P("prow", "pcol"), P("prow", "pcol"), P()),
        out_specs=P("prow", "pcol"),
        check_vma=False,
    )
```

```python
import functools

import jax
import jax.numpy as jnp
from jax import lax
from jax.experimental import pallas as pl
from jax.experimental.pallas import tpu as pltpu
from jax.sharding import PartitionSpec as P

CAP = 32
BLOCK = 32
F32 = jnp.float32
BF16 = jnp.bfloat16
VMEM = pl.BlockSpec(memory_space=pltpu.VMEM)
PARAMS = pltpu.CompilerParams(vmem_limit_bytes=24 * 1024 * 1024)


def split3(x):
    high = x.astype(BF16)
    rest = x - high.astype(F32)
    mid = rest.astype(BF16)
    low = (rest - mid.astype(F32)).astype(BF16)
    return high, mid, low


def split2(x):
    high = x.astype(BF16)
    return high, (x - high.astype(F32)).astype(BF16)


def select_rows(one_hot, x):
    return sum(jnp.dot(one_hot, part, preferred_element_type=F32) for part in split3(x))


def dot_full(a, b):
    high, mid, low = split3(a)
    left = jnp.concatenate([low, mid, high, mid, high, high], axis=1)
    high, mid, low = split3(b)
    right = jnp.concatenate([high, mid, low, high, mid, high], axis=0)
    return jnp.dot(left, right, preferred_element_type=F32)


def tree_partner(r, span):
    if span == 1 or r % span > 1:
        return r ^ 1
    if r % 2 == 0:
        return r + 1 if r & span else r + span
    return r - span if r & span else r - 1


def lead_place(owner, n):
    bits = n.bit_length() - 1
    return sum((lax.shift_right_logical(owner, bit) & 1) * (1 << (bits - 1 - bit)) for bit in range(bits))


def slots(pivot_row, rows):
    width = pivot_row.shape[1]
    by_sublane = jnp.broadcast_to(pivot_row, (width, width)).T
    shift = rows.bit_length() - 1
    owner_row = jnp.broadcast_to(lax.shift_right_logical(pivot_row, shift), (width, width))
    owner_col = lax.shift_right_logical(by_sublane, shift)
    sub = lax.broadcasted_iota(jnp.int32, (width, width), 0)
    lane = lax.broadcasted_iota(jnp.int32, (width, width), 1)
    same = owner_row == owner_col
    rank_row = jnp.sum(jnp.where(same & (sub < lane), 1, 0), axis=0, keepdims=True)
    rank_col = jnp.sum(jnp.where(same & (lane < sub), 1, 0), axis=1, keepdims=True)
    return owner_row[:1], rank_row, owner_col[:, :1], rank_col


def pack_kernel(pivot_ref, slab_ref, packed_ref, lead_ref, local_ref):
    rows = slab_ref.shape[0]
    width = pivot_ref.shape[1]
    count = lead_ref.shape[0]
    lanes = local_ref.shape[1]
    me = lax.axis_index("prow")
    pivot_row = pivot_ref[...]
    owner_row, rank_row, owner_col, rank_col = slots(pivot_row, rows)
    pivot_col = jnp.broadcast_to(pivot_row, (lanes, width)).T
    slot = lax.broadcasted_iota(jnp.int32, (width, lanes), 1)
    mine = (owner_col == me) & (rank_col == slot)
    local = jnp.sum(jnp.where(mine, pivot_col - (me + 1) * rows, 0), axis=0, keepdims=True) + rows
    local_ref[...] = local
    slot = lax.broadcasted_iota(jnp.int32, (CAP, width), 0)
    mine = (owner_row == me) & (rank_row == slot)
    local = jnp.sum(jnp.where(mine, pivot_row - (me + 1) * rows, 0), axis=1, keepdims=True) + rows
    one_hot = (lax.broadcasted_iota(jnp.int32, (CAP, rows), 1) == local).astype(F32).astype(BF16)
    packed_ref[...] = select_rows(one_hot, slab_ref[...])
    slot = lax.broadcasted_iota(jnp.int32, (count, width), 0)
    one_hot = (slot == lead_place(owner_row, count // CAP) * CAP + rank_row).astype(F32).astype(BF16)
    lead_ref[...] = select_rows(one_hot, slab_ref[:width, :])


def block_inverses(lower):
    width = lower.shape[0]
    lane = lax.broadcasted_iota(jnp.int32, (BLOCK, width), 1)
    sub = lax.broadcasted_iota(jnp.int32, (BLOCK, width), 0)
    block = lane // BLOCK
    within = lane % BLOCK
    diag = jnp.zeros((BLOCK, width), F32)
    for b in range(width // BLOCK):
        diag = jnp.where(block == b, lower[b * BLOCK : (b + 1) * BLOCK], diag)
    diag = jnp.where(within < sub, diag, 0.0)
    inv = jnp.where(within == sub, 1.0, 0.0).astype(F32)
    half = 128
    first = (lax.broadcasted_iota(jnp.int32, (BLOCK, half), 1) // BLOCK) * BLOCK
    outs = []
    for h in range(0, width, half):
        d, x = diag[:, h : h + half], inv[:, h : h + half]
        for k in range(BLOCK - 1):
            column = jnp.take_along_axis(d, first + k, axis=1)
            x = x - column * x[k : k + 1, :]
        outs.append(x)
    return outs


def order_kernel(n, rows, pivot_ref, gathered_ref, out_ref, gathered):
    width = pivot_ref.shape[1]
    me = lax.axis_index("prow")
    for q in range(n):
        source = jnp.bitwise_xor(me, q)
        gathered[pl.ds(pl.multiple_of(source * CAP, CAP), CAP), :] = gathered_ref[q * CAP : (q + 1) * CAP, :]
    _, _, owner_col, rank_col = slots(pivot_ref[...], rows)
    slot = lax.broadcasted_iota(jnp.int32, (width, gathered.shape[0]), 1)
    one_hot = (slot == owner_col * CAP + rank_col).astype(F32).astype(BF16)
    out_ref[...] = select_rows(one_hot, gathered[...])


def top_order(m):
    return [0, 1, *range(m - 1, 1, -1)]


def cut_kernel(panel_ref, top_ref, rest_ref, sems):
    width = top_ref.shape[1]
    copies = []
    for c in range(sems.shape[0]):
        target = rest_ref.at[:, pl.ds((c - 1) * width, width)] if c else top_ref
        copies.append(pltpu.make_async_copy(panel_ref.at[:, pl.ds(c * width, width)], target, sems.at[c]))
        copies[-1].start()
    for copy in copies:
        copy.wait()


def assemble_kernel(m, *refs):
    *pieces, out_ref, lower_t = refs
    width = lower_t.shape[0]
    piece = width // m
    half = width // 2
    z = lax.axis_index("pcol")
    for d, ref in zip(top_order(m), pieces):
        lower_t[pl.ds(pl.multiple_of(jnp.bitwise_xor(z, d) * piece, piece), piece), :] = ref[...]
    out_ref[:half, :] = lower_t[:half, :]
    out_ref[half:, :half] = lower_t[half : half + half // 2, half:]
    out_ref[half:, half:] = lower_t[half + half // 2 :, half:]


def pick_kernel(span, moved_ref, held_ref, out_ref):
    child = lax.rem(lax.axis_index("prow"), 2 * span) == span

    @pl.when(child)
    def _():
        out_ref[...] = moved_ref[...]

    @pl.when(jnp.logical_not(child))
    def _():
        out_ref[...] = held_ref[...]


def invert_kernel(lower_ref, out_ref, lower_t):
    width = lower_t.shape[0]
    half = width // 2
    lower_t[:half, :] = lower_ref[:half, :]
    lower_t[half:, :half] = jnp.zeros((half, half), F32)
    lower_t[half : half + half // 2, half:] = lower_ref[half:, :half]
    lower_t[half + half // 2 :, half:] = lower_ref[half:, half:]
    lower = lower_t[...].T
    blocks = block_inverses(lower)
    row = lax.broadcasted_iota(jnp.int32, (half, half), 0)
    col = lax.broadcasted_iota(jnp.int32, (half, half), 1)
    for h, strip in enumerate(blocks):
        corner = lower[h * half : (h + 1) * half, h * half : (h + 1) * half]
        inv = jnp.where(row // BLOCK == col // BLOCK, jnp.concatenate([strip] * (half // BLOCK), axis=0), 0.0)
        size = BLOCK
        while size < half:
            off = (row // (2 * size) == col // (2 * size)) & (row // size > col // size)
            inv = inv - dot_full(dot_full(inv, jnp.where(off, corner, 0.0)), inv)
            size *= 2
        out_ref[:half, h * half : (h + 1) * half] = inv
    out_ref[half:, :half] = lower[half : half + half // 2, :half]
    out_ref[half:, half:] = lower[half + half // 2 :, :half]


def solve_kernel(inverse_ref, pivot_rows_ref, x_ref):
    half = pivot_rows_ref.shape[0] // 2
    quarter = jnp.concatenate([inverse_ref[half:, :half], inverse_ref[half:, half:]], axis=0)
    first = dot_full(inverse_ref[:half, :half], pivot_rows_ref[:half, :])
    x_ref[:half, :] = first
    x_ref[half:, :] = dot_full(inverse_ref[:half, half:], pivot_rows_ref[half:, :] - dot_full(quarter, first))


def update_kernel(m, local_ref, lead_ref, x_ref, slab_ref, *refs):
    *pieces, out_ref, result, high_t, low_t, sems = refs
    tops, rests = zip(top_order(m), pieces[:m]), zip(range(m), pieces[m:])
    rows, cols = slab_ref.shape
    width = x_ref.shape[0]
    piece = width // m
    z = lax.axis_index("pcol")
    for blocks, columns in ((tops, pl.ds(0, width)), (rests, pl.ds(width, rows - width))):
        for d, ref in blocks:
            place = pl.ds(pl.multiple_of(jnp.bitwise_xor(z, d) * piece, piece), piece)
            high_t[place, columns], low_t[place, columns] = split2(ref[...])
    upper_high, upper_low = split2(x_ref[...])
    upper = jnp.concatenate([upper_high, upper_low], axis=1)
    result[:rows, :] = slab_ref[...]
    for s in range(CAP):
        result[pl.ds(local_ref[0, s], 1), :] = lead_ref[pl.ds(s, 1), :]

    def product(part_t, factor):
        return lax.dot_general(part_t, factor, (((0,), (0,)), ((), ())), preferred_element_type=F32)

    copies = []
    for c in range(rows // width):
        part = pl.ds(c * width, width)
        both = product(high_t[:, part], upper)
        low = product(low_t[:, part], upper_high)
        result[part, :] = result[part, :] - (both[:, :cols] + (both[:, cols:] + low))
        if c == 0:

            @pl.when(lax.axis_index("prow") == 0)
            def _():
                result[part, :] = x_ref[...]

        copy = pltpu.make_async_copy(result.at[part], out_ref.at[part], sems.at[c])
        copy.start()
        copies.append(copy)
    for copy in copies:
        copy.wait()


def unit(held, steps, *operands):
    shapes = jax.eval_shape(steps, *operands)
    return lax.cond(held, steps, lambda *_: jax.tree.map(lambda s: jnp.zeros(s.shape, s.dtype), shapes), *operands)


def call(kernel, outs, operands, in_specs=None, out_specs=None, scratch=()):
    return pl.pallas_call(
        kernel,
        out_shape=outs,
        in_specs=in_specs or [VMEM] * len(operands),
        out_specs=out_specs or jax.tree.map(lambda _: VMEM, outs),
        scratch_shapes=list(scratch),
        compiler_params=PARAMS,
        cost_estimate=pl.CostEstimate(flops=1, bytes_accessed=1, transcendentals=0),
    )(*operands)


def local(n, m, slab, panel, pivots):
    rows, cols = slab.shape
    width = pivots.shape[0]
    piece = panel.shape[1]
    me = lax.axis_index("prow")
    panel_t = panel.T
    pivot_row = pivots.reshape(1, width)

    def spread(block, order):
        return [block] + [lax.ppermute(block, "pcol", [(c, c ^ d) for c in range(m)]) for d in order]

    top, rest = call(
        cut_kernel,
        (jax.ShapeDtypeStruct((piece, width), F32), jax.ShapeDtypeStruct((piece, rows - width), F32)),
        (panel_t,),
        in_specs=[pl.BlockSpec(memory_space=pl.ANY)],
        scratch=[pltpu.SemaphoreType.DMA((rows // width,))],
    )
    tops, rests = spread(top, top_order(m)[1:]), spread(rest, range(1, m))

    gathered, leading, local_rows = call(
        pack_kernel,
        (
            jax.ShapeDtypeStruct((CAP, cols), F32),
            jax.ShapeDtypeStruct((n * CAP, cols), F32),
            jax.ShapeDtypeStruct((1, 128), jnp.int32),
        ),
        (pivot_row, slab),
    )
    lower = call(
        functools.partial(assemble_kernel, m),
        jax.ShapeDtypeStruct((width * 3 // 4, width), F32),
        tops,
        scratch=[pltpu.VMEM((width, width), F32)],
    )

    def split(leading):
        blocks = leading.reshape(2, -1, cols)
        return blocks[0], blocks[1]

    def levels(lower, gathered, leading):
        kept, sent = split(leading)
        moved = lax.ppermute(sent, "prow", [(r, r ^ 1) for r in range(n)])
        leading = jnp.where(me & 1 != 0, moved, kept)
        span, other = n // 2, 2
        while span > 1:
            moved = lax.ppermute(lower, "prow", [(r, tree_partner(r, span)) for r in range(n)])
            lower = call(
                functools.partial(pick_kernel, span),
                jax.ShapeDtypeStruct(lower.shape, F32),
                (moved, lower),
            )
            kept, sent = split(leading)
            count = gathered.shape[0]
            message = jnp.concatenate([gathered, sent], axis=0)
            moved = lax.ppermute(message, "prow", [(r, r ^ other) for r in range(n)])
            gathered = jnp.concatenate([gathered, moved[:count]], axis=0)
            leading = jnp.where(me & other != 0, moved[count:], kept)
            span, other = span // 2, other * 2
        pivot_rows = call(
            functools.partial(order_kernel, n, rows),
            jax.ShapeDtypeStruct((width, cols), F32),
            (pivot_row, gathered),
            scratch=[pltpu.VMEM((n * CAP, cols), F32)],
        )
        inverse = call(
            invert_kernel,
            jax.ShapeDtypeStruct(lower.shape, F32),
            (lower,),
            scratch=[pltpu.VMEM((width, width), F32)],
        )
        moved = lax.ppermute(inverse, "prow", [(r, r ^ 1) for r in range(n)])
        inverse = jnp.where(me & 1 != 0, moved, inverse)
        return leading, call(solve_kernel, jax.ShapeDtypeStruct((width, cols), F32), (inverse, pivot_rows))

    gathered, lower = lax.optimization_barrier((gathered, lower))
    moved = lax.ppermute(jnp.concatenate([gathered, gathered], axis=0), "prow", [(r, r ^ 1) for r in range(n)])
    gathered = jnp.concatenate([gathered, moved[:CAP]], axis=0)
    leading, upper_rows = unit(me < n, levels, lower, gathered, leading)
    return call(
        functools.partial(update_kernel, m),
        jax.ShapeDtypeStruct((rows, cols), F32),
        (local_rows, leading, upper_rows, slab, *tops, *rests),
        in_specs=[pl.BlockSpec(memory_space=pltpu.SMEM)] + [VMEM] * (2 * m + 3),
        out_specs=pl.BlockSpec(memory_space=pl.ANY),
        scratch=[
            pltpu.VMEM((rows + 8, cols), F32),
            pltpu.VMEM((width, rows), BF16),
            pltpu.VMEM((width, rows), BF16),
            pltpu.SemaphoreType.DMA((rows // width,)),
        ],
    )


def solution(mesh):
    return jax.shard_map(
        functools.partial(local, mesh.shape["prow"], mesh.shape["pcol"]),
        mesh=mesh,
        in_specs=(P("prow", "pcol"), P("prow", "pcol"), P()),
        out_specs=P("prow", "pcol"),
        check_vma=False,
    )
```

```python
import functools

import jax
import jax.numpy as jnp
from jax import lax
from jax.experimental import pallas as pl
from jax.experimental.pallas import tpu as pltpu
from jax.sharding import PartitionSpec as P

CAP = 32
BLOCK = 32
F32 = jnp.float32
BF16 = jnp.bfloat16
VMEM = pl.BlockSpec(memory_space=pltpu.VMEM)
PARAMS = pltpu.CompilerParams(vmem_limit_bytes=24 * 1024 * 1024)


def split3(x):
    high = x.astype(BF16)
    rest = x - high.astype(F32)
    mid = rest.astype(BF16)
    low = (rest - mid.astype(F32)).astype(BF16)
    return high, mid, low


def split2(x):
    high = x.astype(BF16)
    return high, (x - high.astype(F32)).astype(BF16)


def select_rows(one_hot, x):
    return sum(jnp.dot(one_hot, part, preferred_element_type=F32) for part in split3(x))


def dot_full(a, b):
    high, mid, low = split3(a)
    left = jnp.concatenate([low, mid, high, mid, high, high], axis=1)
    high, mid, low = split3(b)
    right = jnp.concatenate([high, mid, low, high, mid, high], axis=0)
    return jnp.dot(left, right, preferred_element_type=F32)


def tree_partner(r, span):
    if span == 1 or r % span > 1:
        return r ^ 1
    if r % 2 == 0:
        return r + 1 if r & span else r + span
    return r - span if r & span else r - 1


def lead_place(owner, n):
    bits = n.bit_length() - 1
    return sum((lax.shift_right_logical(owner, bit) & 1) * (1 << (bits - 1 - bit)) for bit in range(bits))


def slots(pivot_row, rows):
    width = pivot_row.shape[1]
    by_sublane = jnp.broadcast_to(pivot_row, (width, width)).T
    shift = rows.bit_length() - 1
    owner_row = jnp.broadcast_to(lax.shift_right_logical(pivot_row, shift), (width, width))
    owner_col = lax.shift_right_logical(by_sublane, shift)
    sub = lax.broadcasted_iota(jnp.int32, (width, width), 0)
    lane = lax.broadcasted_iota(jnp.int32, (width, width), 1)
    same = owner_row == owner_col
    rank_row = jnp.sum(jnp.where(same & (sub < lane), 1, 0), axis=0, keepdims=True)
    rank_col = jnp.sum(jnp.where(same & (lane < sub), 1, 0), axis=1, keepdims=True)
    return owner_row[:1], rank_row, owner_col[:, :1], rank_col


def pack_kernel(pivot_ref, slab_ref, packed_ref, lead_ref, local_ref):
    rows = slab_ref.shape[0]
    width = pivot_ref.shape[1]
    count = lead_ref.shape[0]
    lanes = local_ref.shape[1]
    me = lax.axis_index("prow")
    pivot_row = pivot_ref[...]
    owner_row, rank_row, owner_col, rank_col = slots(pivot_row, rows)
    pivot_col = jnp.broadcast_to(pivot_row, (lanes, width)).T
    slot = lax.broadcasted_iota(jnp.int32, (width, lanes), 1)
    mine = (owner_col == me) & (rank_col == slot)
    local = jnp.sum(jnp.where(mine, pivot_col - (me + 1) * rows, 0), axis=0, keepdims=True) + rows
    local_ref[...] = local
    slot = lax.broadcasted_iota(jnp.int32, (CAP, width), 0)
    mine = (owner_row == me) & (rank_row == slot)
    local = jnp.sum(jnp.where(mine, pivot_row - (me + 1) * rows, 0), axis=1, keepdims=True) + rows
    one_hot = (lax.broadcasted_iota(jnp.int32, (CAP, rows), 1) == local).astype(F32).astype(BF16)
    packed_ref[...] = select_rows(one_hot, slab_ref[...])
    slot = lax.broadcasted_iota(jnp.int32, (count, width), 0)
    one_hot = (slot == lead_place(owner_row, count // CAP) * CAP + rank_row).astype(F32).astype(BF16)
    lead_ref[...] = select_rows(one_hot, slab_ref[:width, :])


def block_inverses(lower):
    width = lower.shape[0]
    lane = lax.broadcasted_iota(jnp.int32, (BLOCK, width), 1)
    sub = lax.broadcasted_iota(jnp.int32, (BLOCK, width), 0)
    block = lane // BLOCK
    within = lane % BLOCK
    diag = jnp.zeros((BLOCK, width), F32)
    for b in range(width // BLOCK):
        diag = jnp.where(block == b, lower[b * BLOCK : (b + 1) * BLOCK], diag)
    diag = jnp.where(within < sub, diag, 0.0)
    inv = jnp.where(within == sub, 1.0, 0.0).astype(F32)
    half = 128
    first = (lax.broadcasted_iota(jnp.int32, (BLOCK, half), 1) // BLOCK) * BLOCK
    outs = []
    for h in range(0, width, half):
        d, x = diag[:, h : h + half], inv[:, h : h + half]
        for k in range(BLOCK - 1):
            column = jnp.take_along_axis(d, first + k, axis=1)
            x = x - column * x[k : k + 1, :]
        outs.append(x)
    return outs


def order_kernel(n, rows, pivot_ref, gathered_ref, mark_ref, out_ref, gathered):
    width = pivot_ref.shape[1]
    me = lax.axis_index("prow")
    for q in range(n):
        source = jnp.bitwise_xor(me, q)
        gathered[pl.ds(pl.multiple_of(source * CAP, CAP), CAP), :] = gathered_ref[q * CAP : (q + 1) * CAP, :]
    _, _, owner_col, rank_col = slots(pivot_ref[...], rows)
    slot = lax.broadcasted_iota(jnp.int32, (width, gathered.shape[0]), 1)
    one_hot = (slot == owner_col * CAP + rank_col).astype(F32).astype(BF16)
    out_ref[...] = select_rows(one_hot, gathered[...])


def top_order(m):
    return [0, 1, *range(m - 1, 1, -1)]


def cut_kernel(panel_ref, slab_ref, top_ref, rest_ref, held_ref, sems):
    width = top_ref.shape[1]
    blocks = sems.shape[0] // 2
    copies = []
    for c in range(blocks):
        target = rest_ref.at[:, pl.ds((c - 1) * width, width)] if c else top_ref
        copies.append(pltpu.make_async_copy(panel_ref.at[:, pl.ds(c * width, width)], target, sems.at[c]))
    for c in range(blocks):
        block = pl.ds(c * width, width)
        copies.append(pltpu.make_async_copy(slab_ref.at[block], held_ref.at[block], sems.at[blocks + c]))
    for copy in copies:
        copy.start()
    for copy in copies:
        copy.wait()


def assemble_kernel(m, *refs):
    *pieces, out_ref, lower_t = refs
    width = lower_t.shape[0]
    piece = width // m
    half = width // 2
    z = lax.axis_index("pcol")
    for d, ref in zip(top_order(m), pieces):
        lower_t[pl.ds(pl.multiple_of(jnp.bitwise_xor(z, d) * piece, piece), piece), :] = ref[...]
    out_ref[:half, :] = lower_t[:half, :]
    out_ref[half:, :half] = lower_t[half : half + half // 2, half:]
    out_ref[half:, half:] = lower_t[half + half // 2 :, half:]


def pick_kernel(span, moved_ref, held_ref, out_ref):
    child = lax.rem(lax.axis_index("prow"), 2 * span) == span

    @pl.when(child)
    def _():
        out_ref[...] = moved_ref[...]

    @pl.when(jnp.logical_not(child))
    def _():
        out_ref[...] = held_ref[...]


def invert_kernel(lower_ref, out_ref, lower_t):
    width = lower_t.shape[0]
    half = width // 2
    lower_t[:half, :] = lower_ref[:half, :]
    lower_t[half:, :half] = jnp.zeros((half, half), F32)
    lower_t[half : half + half // 2, half:] = lower_ref[half:, :half]
    lower_t[half + half // 2 :, half:] = lower_ref[half:, half:]
    lower = lower_t[...].T
    blocks = block_inverses(lower)
    row = lax.broadcasted_iota(jnp.int32, (half, half), 0)
    col = lax.broadcasted_iota(jnp.int32, (half, half), 1)
    for h, strip in enumerate(blocks):
        corner = lower[h * half : (h + 1) * half, h * half : (h + 1) * half]
        inv = jnp.where(row // BLOCK == col // BLOCK, jnp.concatenate([strip] * (half // BLOCK), axis=0), 0.0)
        size = BLOCK
        while size < half:
            off = (row // (2 * size) == col // (2 * size)) & (row // size > col // size)
            inv = inv - dot_full(dot_full(inv, jnp.where(off, corner, 0.0)), inv)
            size *= 2
        out_ref[:half, h * half : (h + 1) * half] = inv
    out_ref[half:, :half] = lower[half : half + half // 2, :half]
    out_ref[half:, half:] = lower[half + half // 2 :, :half]


def solve_kernel(inverse_ref, pivot_rows_ref, x_ref):
    half = pivot_rows_ref.shape[0] // 2
    quarter = jnp.concatenate([inverse_ref[half:, :half], inverse_ref[half:, half:]], axis=0)
    first = dot_full(inverse_ref[:half, :half], pivot_rows_ref[:half, :])
    x_ref[:half, :] = first
    x_ref[half:, :] = dot_full(inverse_ref[:half, half:], pivot_rows_ref[half:, :] - dot_full(quarter, first))


def product(piece, upper):
    high, low = split2(piece)
    upper_high, upper_low = split2(upper)
    left = jnp.concatenate([high, high, low], axis=0)
    right = jnp.concatenate([upper_high, upper_low, upper_high], axis=0)
    return lax.dot_general(left, right, (((0,), (0,)), ((), ())), preferred_element_type=F32)


def piece_rows(x_ref, m, d):
    piece = x_ref.shape[0] // m
    source = jnp.bitwise_xor(lax.axis_index("pcol"), d)
    return x_ref[pl.ds(pl.multiple_of(source * piece, piece), piece), :]


def update_kernel(m, local_ref, lead_ref, x_ref, slab_ref, *refs):
    *pieces, out_ref, result, sems = refs
    tops, rests = dict(zip(top_order(m), pieces[:m])), pieces[m:]
    rows, cols = slab_ref.shape
    width = x_ref.shape[0]
    result[:rows, :] = slab_ref[...]
    for s in range(CAP):
        result[pl.ds(local_ref[0, s], 1), :] = lead_ref[pl.ds(s, 1), :]
    uppers = [piece_rows(x_ref, m, d) for d in range(m)]
    copies = []
    for c in range(rows // width):
        part = pl.ds(c * width, width)
        total = result[part, :]
        for d, upper in enumerate(uppers):
            piece = rests[d][:, (c - 1) * width : c * width] if c else tops[d][...]
            total = total - product(piece, upper)
        result[part, :] = total
        if c == 0:

            @pl.when(lax.axis_index("prow") == 0)
            def _():
                result[part, :] = x_ref[...]

        copy = pltpu.make_async_copy(result.at[part], out_ref.at[part], sems.at[c])
        copy.start()
        copies.append(copy)
    for copy in copies:
        copy.wait()


def unit(held, steps, *operands):
    shapes = jax.eval_shape(steps, *operands)
    return lax.cond(held, steps, lambda *_: jax.tree.map(lambda s: jnp.zeros(s.shape, s.dtype), shapes), *operands)


def call(kernel, outs, operands, in_specs=None, out_specs=None, scratch=()):
    return pl.pallas_call(
        kernel,
        out_shape=outs,
        in_specs=in_specs or [VMEM] * len(operands),
        out_specs=out_specs or jax.tree.map(lambda _: VMEM, outs),
        scratch_shapes=list(scratch),
        compiler_params=PARAMS,
        cost_estimate=pl.CostEstimate(flops=1, bytes_accessed=1, transcendentals=0),
    )(*operands)


def local(n, m, slab, panel, pivots):
    rows, cols = slab.shape
    width = pivots.shape[0]
    piece = panel.shape[1]
    me = lax.axis_index("prow")
    panel_t = panel.T
    pivot_row = pivots.reshape(1, width)

    def spread(block, order):
        return [block] + [lax.ppermute(block, "pcol", [(c, c ^ d) for c in range(m)]) for d in order]

    def cut(panel_t, slab):
        return call(
            cut_kernel,
            (
                jax.ShapeDtypeStruct((piece, width), F32),
                jax.ShapeDtypeStruct((piece, rows - width), F32),
                jax.ShapeDtypeStruct((rows, cols), F32),
            ),
            (panel_t, slab),
            in_specs=[pl.BlockSpec(memory_space=pl.ANY)] * 2,
            scratch=[pltpu.SemaphoreType.DMA((2 * (rows // width),))],
        )

    top, rest, slab = unit(me < n, cut, panel_t, slab)
    tops, rests = spread(top, top_order(m)[1:]), spread(rest, range(1, m))

    lower = call(
        functools.partial(assemble_kernel, m),
        jax.ShapeDtypeStruct((width * 3 // 4, width), F32),
        tops,
        scratch=[pltpu.VMEM((width, width), F32)],
    )

    def split(leading):
        blocks = leading.reshape(2, -1, cols)
        return blocks[0], blocks[1]

    def levels(lower, gathered, leading, mark):
        span, other = n // 2, 1
        while other < n:
            if span > 1:
                moved = lax.ppermute(lower, "prow", [(r, tree_partner(r, span)) for r in range(n)])
                lower = call(
                    functools.partial(pick_kernel, span),
                    jax.ShapeDtypeStruct(lower.shape, F32),
                    (moved, lower),
                )
            kept, sent = split(leading)
            count = gathered.shape[0]
            message = jnp.concatenate([gathered, sent], axis=0)
            moved = lax.ppermute(message, "prow", [(r, r ^ other) for r in range(n)])
            gathered = jnp.concatenate([gathered, moved[:count]], axis=0)
            leading = jnp.where(me & other != 0, moved[count:], kept)
            span, other = span // 2, other * 2
        pivot_rows = call(
            functools.partial(order_kernel, n, rows),
            jax.ShapeDtypeStruct((width, cols), F32),
            (pivot_row, gathered, mark),
            scratch=[pltpu.VMEM((n * CAP, cols), F32)],
        )
        inverse = call(
            invert_kernel,
            jax.ShapeDtypeStruct(lower.shape, F32),
            (lower,),
            scratch=[pltpu.VMEM((width, width), F32)],
        )
        moved = lax.ppermute(inverse, "prow", [(r, r ^ 1) for r in range(n)])
        inverse = jnp.where(me & 1 != 0, moved, inverse)
        return leading, call(solve_kernel, jax.ShapeDtypeStruct((width, cols), F32), (inverse, pivot_rows))

    mark = lax.ppermute(lower[: 4 * CAP], "prow", [(r, r ^ 1) for r in range(n)])
    pivot_row, lower = lax.optimization_barrier((pivot_row, lower))
    gathered, leading, local_rows = call(
        pack_kernel,
        (
            jax.ShapeDtypeStruct((CAP, cols), F32),
            jax.ShapeDtypeStruct((n * CAP, cols), F32),
            jax.ShapeDtypeStruct((1, 128), jnp.int32),
        ),
        (pivot_row, slab),
    )

    leading, upper_rows = unit(me < n, levels, lower, gathered, leading, mark)
    return call(
        functools.partial(update_kernel, m),
        jax.ShapeDtypeStruct((rows, cols), F32),
        (local_rows, leading, upper_rows, slab, *tops, *rests),
        in_specs=[pl.BlockSpec(memory_space=pltpu.SMEM)] + [VMEM] * (2 * m + 3),
        out_specs=pl.BlockSpec(memory_space=pl.ANY),
        scratch=[pltpu.VMEM((rows + 8, cols), F32), pltpu.SemaphoreType.DMA((rows // width,))],
    )


def solution(mesh):
    return jax.shard_map(
        functools.partial(local, mesh.shape["prow"], mesh.shape["pcol"]),
        mesh=mesh,
        in_specs=(P("prow", "pcol"), P("prow", "pcol"), P()),
        out_specs=P("prow", "pcol"),
        check_vma=False,
    )
```

```python
import functools

import jax
import jax.numpy as jnp
from jax import lax
from jax.experimental import pallas as pl
from jax.experimental.pallas import tpu as pltpu
from jax.sharding import PartitionSpec as P

CAP = 32
BLOCK = 32
EXTRA = 32
F32 = jnp.float32
BF16 = jnp.bfloat16
VMEM = pl.BlockSpec(memory_space=pltpu.VMEM)
PARAMS = pltpu.CompilerParams(vmem_limit_bytes=24 * 1024 * 1024)


def split3(x):
    high = x.astype(BF16)
    rest = x - high.astype(F32)
    mid = rest.astype(BF16)
    low = (rest - mid.astype(F32)).astype(BF16)
    return high, mid, low


def split2(x):
    high = x.astype(BF16)
    return high, (x - high.astype(F32)).astype(BF16)


def select_rows(one_hot, x):
    return sum(jnp.dot(one_hot, part, preferred_element_type=F32) for part in split3(x))


def dot_full(a, b):
    high, mid, low = split3(a)
    left = jnp.concatenate([low, mid, high, mid, high, high], axis=1)
    high, mid, low = split3(b)
    right = jnp.concatenate([high, mid, low, high, mid, high], axis=0)
    return jnp.dot(left, right, preferred_element_type=F32)


def lead_place(owner, n):
    bits = n.bit_length() - 1
    return sum((lax.shift_right_logical(owner, bit) & 1) * (1 << (bits - 1 - bit)) for bit in range(bits))


def slots(pivot_row, rows):
    width = pivot_row.shape[1]
    by_sublane = jnp.broadcast_to(pivot_row, (width, width)).T
    shift = rows.bit_length() - 1
    owner_row = jnp.broadcast_to(lax.shift_right_logical(pivot_row, shift), (width, width))
    owner_col = lax.shift_right_logical(by_sublane, shift)
    sub = lax.broadcasted_iota(jnp.int32, (width, width), 0)
    lane = lax.broadcasted_iota(jnp.int32, (width, width), 1)
    same = owner_row == owner_col
    rank_row = jnp.sum(jnp.where(same & (sub < lane), 1, 0), axis=0, keepdims=True)
    rank_col = jnp.sum(jnp.where(same & (lane < sub), 1, 0), axis=1, keepdims=True)
    return owner_row[:1], rank_row, owner_col[:, :1], rank_col


def pack_kernel(pivot_ref, slab_ref, packed_ref, lead_ref, local_ref):
    rows = slab_ref.shape[0]
    width = pivot_ref.shape[1]
    count = lead_ref.shape[0]
    lanes = local_ref.shape[1]
    me = lax.axis_index("prow")
    pivot_row = pivot_ref[...]
    owner_row, rank_row, owner_col, rank_col = slots(pivot_row, rows)
    pivot_col = jnp.broadcast_to(pivot_row, (lanes, width)).T
    slot = lax.broadcasted_iota(jnp.int32, (width, lanes), 1)
    mine = (owner_col == me) & (rank_col == slot)
    local = jnp.sum(jnp.where(mine, pivot_col - (me + 1) * rows, 0), axis=0, keepdims=True) + rows
    local_ref[...] = local
    slot = lax.broadcasted_iota(jnp.int32, (CAP, width), 0)
    mine = (owner_row == me) & (rank_row == slot)
    local = jnp.sum(jnp.where(mine, pivot_row - (me + 1) * rows, 0), axis=1, keepdims=True) + rows
    one_hot = (lax.broadcasted_iota(jnp.int32, (CAP, rows), 1) == local).astype(F32).astype(BF16)
    packed_ref[...] = select_rows(one_hot, slab_ref[...])
    slot = lax.broadcasted_iota(jnp.int32, (count, width), 0)
    one_hot = (slot == lead_place(owner_row, count // CAP) * CAP + rank_row).astype(F32).astype(BF16)
    lead_ref[...] = select_rows(one_hot, slab_ref[:width, :])


def block_inverses(lower):
    width = lower.shape[0]
    lane = lax.broadcasted_iota(jnp.int32, (BLOCK, width), 1)
    sub = lax.broadcasted_iota(jnp.int32, (BLOCK, width), 0)
    block = lane // BLOCK
    within = lane % BLOCK
    diag = jnp.zeros((BLOCK, width), F32)
    for b in range(width // BLOCK):
        diag = jnp.where(block == b, lower[b * BLOCK : (b + 1) * BLOCK], diag)
    diag = jnp.where(within < sub, diag, 0.0)
    inv = jnp.where(within == sub, 1.0, 0.0).astype(F32)
    half = 128
    first = (lax.broadcasted_iota(jnp.int32, (BLOCK, half), 1) // BLOCK) * BLOCK
    outs = []
    for h in range(0, width, half):
        d, x = diag[:, h : h + half], inv[:, h : h + half]
        for k in range(BLOCK - 1):
            column = jnp.take_along_axis(d, first + k, axis=1)
            x = x - column * x[k : k + 1, :]
        outs.append(x)
    return outs


def order_kernel(n, rows, pivot_ref, gathered_ref, out_ref, gathered):
    width = pivot_ref.shape[1]
    me = lax.axis_index("prow")
    for q in range(n):
        source = jnp.bitwise_xor(me, q)
        gathered[pl.ds(pl.multiple_of(source * CAP, CAP), CAP), :] = gathered_ref[q * CAP : (q + 1) * CAP, :]
    _, _, owner_col, rank_col = slots(pivot_ref[...], rows)
    slot = lax.broadcasted_iota(jnp.int32, (width, gathered.shape[0]), 1)
    one_hot = (slot == owner_col * CAP + rank_col).astype(F32).astype(BF16)
    out_ref[...] = select_rows(one_hot, gathered[...])


def top_order(m):
    return [0, 1, *range(m - 1, 1, -1)]


def cut_kernel(panel_ref, top_ref, rest_ref, sems):
    width = top_ref.shape[1]
    copies = []
    for c in range(sems.shape[0]):
        target = rest_ref.at[:, pl.ds((c - 1) * width, width)] if c else top_ref
        copies.append(pltpu.make_async_copy(panel_ref.at[:, pl.ds(c * width, width)], target, sems.at[c]))
        copies[-1].start()
    for copy in copies:
        copy.wait()


def assemble_kernel(m, *refs):
    *pieces, out_ref, lower_t = refs
    width = lower_t.shape[0]
    piece = width // m
    half = width // 2
    z = lax.axis_index("pcol")
    for d, ref in zip(top_order(m), pieces):
        lower_t[pl.ds(pl.multiple_of(jnp.bitwise_xor(z, d) * piece, piece), piece), :] = ref[...]
    out_ref[:half, :] = lower_t[:half, :]
    out_ref[half:, :half] = lower_t[half : half + half // 2, half:]
    out_ref[half:, half:] = lower_t[half + half // 2 :, half:]


def pick_kernel(span, moved_ref, held_ref, out_ref):
    reached = lax.rem(lax.axis_index("prow") // 2 * 2, 2 * span) == span

    @pl.when(reached)
    def _():
        out_ref[...] = moved_ref[...]

    @pl.when(jnp.logical_not(reached))
    def _():
        out_ref[...] = held_ref[...]


def invert_kernel(own_ref, twin_ref, out_ref, packed, lower_t):
    width = lower_t.shape[0]
    half = width // 2
    count = own_ref.shape[0]
    odd = lax.axis_index("prow") & 1
    packed[pl.ds(pl.multiple_of(odd * count, count), count), :] = own_ref[...]
    packed[pl.ds(pl.multiple_of((1 - odd) * count, count), count), :] = twin_ref[...]
    lower_t[:half, :] = packed[:half, :]
    lower_t[half:, :half] = jnp.zeros((half, half), F32)
    lower_t[half : half + half // 2, half:] = packed[half:, :half]
    lower_t[half + half // 2 :, half:] = packed[half:, half:]
    lower = lower_t[...].T
    blocks = block_inverses(lower)
    row = lax.broadcasted_iota(jnp.int32, (half, half), 0)
    col = lax.broadcasted_iota(jnp.int32, (half, half), 1)
    for h, strip in enumerate(blocks):
        corner = lower[h * half : (h + 1) * half, h * half : (h + 1) * half]
        inv = jnp.where(row // BLOCK == col // BLOCK, jnp.concatenate([strip] * (half // BLOCK), axis=0), 0.0)
        size = BLOCK
        while size < half:
            off = (row // (2 * size) == col // (2 * size)) & (row // size > col // size)
            inv = inv - dot_full(dot_full(inv, jnp.where(off, corner, 0.0)), inv)
            size *= 2
        out_ref[:half, h * half : (h + 1) * half] = inv
    out_ref[half:, :half] = lower[half : half + half // 2, :half]
    out_ref[half:, half:] = lower[half + half // 2 :, :half]


def solve_kernel(inverse_ref, pivot_rows_ref, x_ref):
    half = pivot_rows_ref.shape[0] // 2
    quarter = jnp.concatenate([inverse_ref[half:, :half], inverse_ref[half:, half:]], axis=0)
    first = dot_full(inverse_ref[:half, :half], pivot_rows_ref[:half, :])
    x_ref[:half, :] = first
    x_ref[half:, :] = dot_full(inverse_ref[:half, half:], pivot_rows_ref[half:, :] - dot_full(quarter, first))


def product(piece, upper):
    high, low = split2(piece)
    upper_high, upper_low = split2(upper)
    left = jnp.concatenate([high, high, low], axis=0)
    right = jnp.concatenate([upper_high, upper_low, upper_high], axis=0)
    return lax.dot_general(left, right, (((0,), (0,)), ((), ())), preferred_element_type=F32)


def piece_rows(x_ref, m, d):
    piece = x_ref.shape[0] // m
    source = jnp.bitwise_xor(lax.axis_index("pcol"), d)
    return x_ref[pl.ds(pl.multiple_of(source * piece, piece), piece), :]


def update_kernel(m, local_ref, lead_ref, x_ref, slab_ref, *refs):
    *pieces, out_ref, result, swaps, sems = refs
    tops, rests = dict(zip(top_order(m), pieces[:m])), pieces[m:]
    rows = slab_ref.shape[0]
    width = x_ref.shape[0]
    blocks = rows // width
    fetch = pltpu.make_async_copy(local_ref, swaps, sems.at[blocks])
    fetch.start()
    result[:rows, :] = slab_ref[...]
    uppers = [piece_rows(x_ref, m, d) for d in range(m)]
    copies = []
    for c in range(blocks):
        part = pl.ds(c * width, width)
        if c:
            total = sum(product(rests[d][:, (c - 1) * width : c * width], uppers[d]) for d in range(m))
        else:
            total = sum(product(tops[d][...], uppers[d]) for d in range(m))
            fetch.wait()
            for s in range(CAP):
                result[pl.ds(swaps[0, s], 1), :] = lead_ref[pl.ds(s, 1), :]
        result[part, :] = result[part, :] - total
        if c == 0:

            @pl.when(lax.axis_index("prow") == 0)
            def _():
                result[part, :] = x_ref[...]

        copy = pltpu.make_async_copy(result.at[part], out_ref.at[part], sems.at[c])
        copy.start()
        copies.append(copy)
    for copy in copies:
        copy.wait()


def unit(held, steps, *operands):
    shapes = jax.eval_shape(steps, *operands)
    return lax.cond(held, steps, lambda *_: jax.tree.map(lambda s: jnp.zeros(s.shape, s.dtype), shapes), *operands)


def call(kernel, outs, operands, in_specs=None, out_specs=None, scratch=()):
    return pl.pallas_call(
        kernel,
        out_shape=outs,
        in_specs=in_specs or [VMEM] * len(operands),
        out_specs=out_specs or jax.tree.map(lambda _: VMEM, outs),
        scratch_shapes=list(scratch),
        compiler_params=PARAMS,
        cost_estimate=pl.CostEstimate(flops=1, bytes_accessed=1, transcendentals=0),
    )(*operands)


def local(n, m, slab, panel, pivots):
    rows, cols = slab.shape
    width = pivots.shape[0]
    piece = panel.shape[1]
    me = lax.axis_index("prow")
    panel_t = panel.T
    pivot_row = pivots.reshape(1, width)

    def spread(block, order):
        return [block] + [lax.ppermute(block, "pcol", [(c, c ^ d) for c in range(m)]) for d in order]

    top, rest = call(
        cut_kernel,
        (jax.ShapeDtypeStruct((piece, width), F32), jax.ShapeDtypeStruct((piece, rows - width), F32)),
        (panel_t,),
        in_specs=[pl.BlockSpec(memory_space=pl.ANY)],
        scratch=[pltpu.SemaphoreType.DMA((rows // width,))],
    )
    tops, rests = spread(top, top_order(m)[1:]), spread(rest, range(1, m))

    gathered, leading, local_rows = call(
        pack_kernel,
        (
            jax.ShapeDtypeStruct((CAP, cols), F32),
            jax.ShapeDtypeStruct((n * CAP, cols), F32),
            jax.ShapeDtypeStruct((1, 128), jnp.int32),
        ),
        (pivot_row, slab),
    )
    lower = call(
        functools.partial(assemble_kernel, m),
        jax.ShapeDtypeStruct((width * 3 // 4, width), F32),
        tops,
        scratch=[pltpu.VMEM((width, width), F32)],
    )

    def split(leading):
        blocks = leading.reshape(2, -1, cols)
        return blocks[0], blocks[1]

    def levels(block, gathered, leading):
        kept, sent = split(leading)
        moved = lax.ppermute(jnp.concatenate([gathered, sent], axis=0), "prow", twins)
        gathered = jnp.concatenate([gathered, moved[:CAP]], axis=0)
        leading = jnp.where(me & 1 != 0, moved[CAP:], kept)
        span, other = n // 2, 2
        while span > 1:
            moved = lax.ppermute(block, "prow", [(r, r ^ span) for r in range(n)])
            block = call(
                functools.partial(pick_kernel, span),
                jax.ShapeDtypeStruct(block.shape, F32),
                (moved, block),
            )
            kept, sent = split(leading)
            count = gathered.shape[0]
            message = jnp.concatenate([gathered, sent], axis=0)
            moved = lax.ppermute(message, "prow", [(r, r ^ other) for r in range(n)])
            gathered = jnp.concatenate([gathered, moved[:count]], axis=0)
            leading = jnp.where(me & other != 0, moved[count:], kept)
            span, other = span // 2, other * 2
        twin = lax.ppermute(block, "prow", [(r, r ^ 1) for r in range(n)])
        inverse = call(
            invert_kernel,
            jax.ShapeDtypeStruct(lower.shape, F32),
            (block, twin),
            scratch=[pltpu.VMEM(lower.shape, F32), pltpu.VMEM((width, width), F32)],
        )
        gathered, inverse = lax.optimization_barrier((gathered, inverse))
        pivot_rows = call(
            functools.partial(order_kernel, n, rows),
            jax.ShapeDtypeStruct((width, cols), F32),
            (pivot_row, gathered),
            scratch=[pltpu.VMEM((n * CAP, cols), F32)],
        )
        return leading, call(solve_kernel, jax.ShapeDtypeStruct((width, cols), F32), (inverse, pivot_rows))

    half = lower.shape[0] // 2
    twins = [(r, r ^ 1) for r in range(n)]
    lower, gathered = lax.optimization_barrier((lower, gathered))
    moved = lax.ppermute(lower[half - EXTRA :], "prow", twins)
    block = jnp.where(me & 1 != 0, moved[EXTRA:], lower[:half])
    leading, upper_rows = unit(me < n, levels, block, gathered, leading)
    return call(
        functools.partial(update_kernel, m),
        jax.ShapeDtypeStruct((rows, cols), F32),
        (local_rows, leading, upper_rows, slab, *tops, *rests),
        in_specs=[VMEM] * (2 * m + 4),
        out_specs=pl.BlockSpec(memory_space=pl.ANY),
        scratch=[
            pltpu.VMEM((rows + 8, cols), F32),
            pltpu.SMEM((1, 128), jnp.int32),
            pltpu.SemaphoreType.DMA((rows // width + 1,)),
        ],
    )


def solution(mesh):
    return jax.shard_map(
        functools.partial(local, mesh.shape["prow"], mesh.shape["pcol"]),
        mesh=mesh,
        in_specs=(P("prow", "pcol"), P("prow", "pcol"), P()),
        out_specs=P("prow", "pcol"),
        check_vma=False,
    )
```

```python
import functools

import jax
import jax.numpy as jnp
from jax import lax
from jax.experimental import pallas as pl
from jax.experimental.pallas import tpu as pltpu
from jax.sharding import PartitionSpec as P

CAP = 32
BLOCK = 32
F32 = jnp.float32
BF16 = jnp.bfloat16
VMEM = pl.BlockSpec(memory_space=pltpu.VMEM)
PARAMS = pltpu.CompilerParams(vmem_limit_bytes=24 * 1024 * 1024)


def split3(x):
    high = x.astype(BF16)
    rest = x - high.astype(F32)
    mid = rest.astype(BF16)
    low = (rest - mid.astype(F32)).astype(BF16)
    return high, mid, low


def split2(x):
    high = x.astype(BF16)
    return high, (x - high.astype(F32)).astype(BF16)


def select_rows(one_hot, x):
    return sum(jnp.dot(one_hot, part, preferred_element_type=F32) for part in split3(x))


def dot_full(a, b):
    high, mid, low = split3(a)
    left = jnp.concatenate([low, mid, high, mid, high, high], axis=1)
    high, mid, low = split3(b)
    right = jnp.concatenate([high, mid, low, high, mid, high], axis=0)
    return jnp.dot(left, right, preferred_element_type=F32)


def tree_partner(r, span):
    if span == 1 or r % span > 1:
        return r ^ 1
    if r % 2 == 0:
        return r + 1 if r & span else r + span
    return r - span if r & span else r - 1


def lead_place(owner, n):
    bits = n.bit_length() - 1
    return sum((lax.shift_right_logical(owner, bit) & 1) * (1 << (bits - 1 - bit)) for bit in range(bits))


def slots(pivot_row, rows):
    width = pivot_row.shape[1]
    by_sublane = jnp.broadcast_to(pivot_row, (width, width)).T
    shift = rows.bit_length() - 1
    owner_row = jnp.broadcast_to(lax.shift_right_logical(pivot_row, shift), (width, width))
    owner_col = lax.shift_right_logical(by_sublane, shift)
    sub = lax.broadcasted_iota(jnp.int32, (width, width), 0)
    lane = lax.broadcasted_iota(jnp.int32, (width, width), 1)
    same = owner_row == owner_col
    rank_row = jnp.sum(jnp.where(same & (sub < lane), 1, 0), axis=0, keepdims=True)
    rank_col = jnp.sum(jnp.where(same & (lane < sub), 1, 0), axis=1, keepdims=True)
    return owner_row[:1], rank_row, owner_col[:, :1], rank_col


def pack_kernel(pivot_ref, slab_ref, packed_ref, lead_ref, local_ref):
    rows = slab_ref.shape[0]
    width = pivot_ref.shape[1]
    count = lead_ref.shape[0]
    lanes = local_ref.shape[1]
    me = lax.axis_index("prow")
    pivot_row = pivot_ref[...]
    owner_row, rank_row, owner_col, rank_col = slots(pivot_row, rows)
    pivot_col = jnp.broadcast_to(pivot_row, (lanes, width)).T
    slot = lax.broadcasted_iota(jnp.int32, (width, lanes), 1)
    mine = (owner_col == me) & (rank_col == slot)
    local = jnp.sum(jnp.where(mine, pivot_col - (me + 1) * rows, 0), axis=0, keepdims=True) + rows
    local_ref[...] = local
    slot = lax.broadcasted_iota(jnp.int32, (CAP, width), 0)
    mine = (owner_row == me) & (rank_row == slot)
    local = jnp.sum(jnp.where(mine, pivot_row - (me + 1) * rows, 0), axis=1, keepdims=True) + rows
    one_hot = (lax.broadcasted_iota(jnp.int32, (CAP, rows), 1) == local).astype(F32).astype(BF16)
    packed_ref[...] = select_rows(one_hot, slab_ref[...])
    slot = lax.broadcasted_iota(jnp.int32, (count, width), 0)
    one_hot = (slot == lead_place(owner_row, count // CAP) * CAP + rank_row).astype(F32).astype(BF16)
    lead_ref[...] = select_rows(one_hot, slab_ref[:width, :])


def block_inverses(lower):
    width = lower.shape[0]
    lane = lax.broadcasted_iota(jnp.int32, (BLOCK, width), 1)
    sub = lax.broadcasted_iota(jnp.int32, (BLOCK, width), 0)
    block = lane // BLOCK
    within = lane % BLOCK
    diag = jnp.zeros((BLOCK, width), F32)
    for b in range(width // BLOCK):
        diag = jnp.where(block == b, lower[b * BLOCK : (b + 1) * BLOCK], diag)
    diag = jnp.where(within < sub, diag, 0.0)
    inv = jnp.where(within == sub, 1.0, 0.0).astype(F32)
    half = 128
    first = (lax.broadcasted_iota(jnp.int32, (BLOCK, half), 1) // BLOCK) * BLOCK
    outs = []
    for h in range(0, width, half):
        d, x = diag[:, h : h + half], inv[:, h : h + half]
        for k in range(BLOCK - 1):
            column = jnp.take_along_axis(d, first + k, axis=1)
            x = x - column * x[k : k + 1, :]
        outs.append(x)
    return outs


def order_kernel(n, rows, pivot_ref, gathered_ref, out_ref, gathered):
    width = pivot_ref.shape[1]
    me = lax.axis_index("prow")
    for q in range(n):
        source = jnp.bitwise_xor(me, q)
        gathered[pl.ds(pl.multiple_of(source * CAP, CAP), CAP), :] = gathered_ref[q * CAP : (q + 1) * CAP, :]
    _, _, owner_col, rank_col = slots(pivot_ref[...], rows)
    slot = lax.broadcasted_iota(jnp.int32, (width, gathered.shape[0]), 1)
    one_hot = (slot == owner_col * CAP + rank_col).astype(F32).astype(BF16)
    out_ref[...] = select_rows(one_hot, gathered[...])


def top_order(m):
    return [0, *range(m - 1, 0, -1)]


def cut_kernel(panel_ref, top_ref, rest_ref, sems):
    width = top_ref.shape[1]
    copies = []
    for c in range(sems.shape[0]):
        target = rest_ref.at[:, pl.ds((c - 1) * width, width)] if c else top_ref
        copies.append(pltpu.make_async_copy(panel_ref.at[:, pl.ds(c * width, width)], target, sems.at[c]))
        copies[-1].start()
    for copy in copies:
        copy.wait()


def assemble_kernel(m, *refs):
    *pieces, out_ref, lower_t = refs
    width = lower_t.shape[0]
    piece = width // m
    half = width // 2
    z = lax.axis_index("pcol")
    for d, ref in zip(top_order(m), pieces):
        lower_t[pl.ds(pl.multiple_of(jnp.bitwise_xor(z, d) * piece, piece), piece), :] = ref[...]
    out_ref[:half, :] = lower_t[:half, :]
    out_ref[half:, :half] = lower_t[half : half + half // 2, half:]
    out_ref[half:, half:] = lower_t[half + half // 2 :, half:]


def pick_kernel(span, moved_ref, held_ref, out_ref):
    child = lax.rem(lax.axis_index("prow"), 2 * span) == span

    @pl.when(child)
    def _():
        out_ref[...] = moved_ref[...]

    @pl.when(jnp.logical_not(child))
    def _():
        out_ref[...] = held_ref[...]


def invert_kernel(lower_ref, out_ref, lower_t):
    width = lower_t.shape[0]
    half = width // 2
    lower_t[:half, :] = lower_ref[:half, :]
    lower_t[half:, :half] = jnp.zeros((half, half), F32)
    lower_t[half : half + half // 2, half:] = lower_ref[half:, :half]
    lower_t[half + half // 2 :, half:] = lower_ref[half:, half:]
    lower = lower_t[...].T
    blocks = block_inverses(lower)
    row = lax.broadcasted_iota(jnp.int32, (half, half), 0)
    col = lax.broadcasted_iota(jnp.int32, (half, half), 1)
    for h, strip in enumerate(blocks):
        corner = lower[h * half : (h + 1) * half, h * half : (h + 1) * half]
        inv = jnp.where(row // BLOCK == col // BLOCK, jnp.concatenate([strip] * (half // BLOCK), axis=0), 0.0)
        size = BLOCK
        while size < half:
            off = (row // (2 * size) == col // (2 * size)) & (row // size > col // size)
            inv = inv - dot_full(dot_full(inv, jnp.where(off, corner, 0.0)), inv)
            size *= 2
        out_ref[:half, h * half : (h + 1) * half] = inv
    out_ref[half:, :half] = lower[half : half + half // 2, :half]
    out_ref[half:, half:] = lower[half + half // 2 :, :half]


def solve_kernel(inverse_ref, pivot_rows_ref, x_ref):
    half = pivot_rows_ref.shape[0] // 2
    quarter = jnp.concatenate([inverse_ref[half:, :half], inverse_ref[half:, half:]], axis=0)
    first = dot_full(inverse_ref[:half, :half], pivot_rows_ref[:half, :])
    x_ref[:half, :] = first
    x_ref[half:, :] = dot_full(inverse_ref[:half, half:], pivot_rows_ref[half:, :] - dot_full(quarter, first))


def product(piece, upper):
    high, low = split2(piece)
    upper_high, upper_low = split2(upper)
    left = jnp.concatenate([high, high, low], axis=0)
    right = jnp.concatenate([upper_high, upper_low, upper_high], axis=0)
    return lax.dot_general(left, right, (((0,), (0,)), ((), ())), preferred_element_type=F32)


def piece_rows(x_ref, m, d):
    piece = x_ref.shape[0] // m
    source = jnp.bitwise_xor(lax.axis_index("pcol"), d)
    return x_ref[pl.ds(pl.multiple_of(source * piece, piece), piece), :]


def update_kernel(m, local_ref, lead_ref, x_ref, slab_ref, *refs):
    *pieces, out_ref, result, swaps, sems = refs
    tops, rests = dict(zip(top_order(m), pieces[:m])), pieces[m:]
    rows = slab_ref.shape[0]
    width = x_ref.shape[0]
    blocks = rows // width
    fetch = pltpu.make_async_copy(local_ref, swaps, sems.at[blocks])
    fetch.start()
    result[:rows, :] = slab_ref[...]
    uppers = [piece_rows(x_ref, m, d) for d in range(m)]
    copies = []
    for c in range(blocks):
        part = pl.ds(c * width, width)
        if c:
            total = sum(product(rests[d][:, (c - 1) * width : c * width], uppers[d]) for d in range(m))
        else:
            total = sum(product(tops[d][...], uppers[d]) for d in range(m))
            fetch.wait()
            for s in range(CAP):
                result[pl.ds(swaps[0, s], 1), :] = lead_ref[pl.ds(s, 1), :]
        result[part, :] = result[part, :] - total
        if c == 0:

            @pl.when(lax.axis_index("prow") == 0)
            def _():
                result[part, :] = x_ref[...]

        copy = pltpu.make_async_copy(result.at[part], out_ref.at[part], sems.at[c])
        copy.start()
        copies.append(copy)
    for copy in copies:
        copy.wait()


def unit(held, steps, *operands):
    shapes = jax.eval_shape(steps, *operands)
    return lax.cond(held, steps, lambda *_: jax.tree.map(lambda s: jnp.zeros(s.shape, s.dtype), shapes), *operands)


def call(kernel, outs, operands, in_specs=None, out_specs=None, scratch=()):
    return pl.pallas_call(
        kernel,
        out_shape=outs,
        in_specs=in_specs or [VMEM] * len(operands),
        out_specs=out_specs or jax.tree.map(lambda _: VMEM, outs),
        scratch_shapes=list(scratch),
        compiler_params=PARAMS,
        cost_estimate=pl.CostEstimate(flops=1, bytes_accessed=1, transcendentals=0),
    )(*operands)


def local(n, m, slab, panel, pivots):
    rows, cols = slab.shape
    width = pivots.shape[0]
    piece = panel.shape[1]
    me = lax.axis_index("prow")
    panel_t = panel.T
    pivot_row = pivots.reshape(1, width)

    def spread(block, order):
        return [block] + [lax.ppermute(block, "pcol", [(c, c ^ d) for c in range(m)]) for d in order]

    top, rest = call(
        cut_kernel,
        (jax.ShapeDtypeStruct((piece, width), F32), jax.ShapeDtypeStruct((piece, rows - width), F32)),
        (panel_t,),
        in_specs=[pl.BlockSpec(memory_space=pl.ANY)],
        scratch=[pltpu.SemaphoreType.DMA((rows // width,))],
    )
    tops, rests = spread(top, top_order(m)[1:]), spread(rest, range(1, m))

    gathered, leading, local_rows = call(
        pack_kernel,
        (
            jax.ShapeDtypeStruct((CAP, cols), F32),
            jax.ShapeDtypeStruct((n * CAP, cols), F32),
            jax.ShapeDtypeStruct((1, 128), jnp.int32),
        ),
        (pivot_row, slab),
    )
    lower = call(
        functools.partial(assemble_kernel, m),
        jax.ShapeDtypeStruct((width * 3 // 4, width), F32),
        tops,
        scratch=[pltpu.VMEM((width, width), F32)],
    )

    def split(leading):
        blocks = leading.reshape(2, -1, cols)
        return blocks[0], blocks[1]

    def levels(lower, gathered, leading):
        kept, sent = split(leading)
        moved = lax.ppermute(sent, "prow", [(r, r ^ 1) for r in range(n)])
        leading = jnp.where(me & 1 != 0, moved, kept)
        span, other = n // 2, 2
        while span > 1:
            moved = lax.ppermute(lower, "prow", [(r, tree_partner(r, span)) for r in range(n)])
            lower = call(
                functools.partial(pick_kernel, span),
                jax.ShapeDtypeStruct(lower.shape, F32),
                (moved, lower),
            )
            kept, sent = split(leading)
            count = gathered.shape[0]
            message = jnp.concatenate([gathered, sent], axis=0)
            moved = lax.ppermute(message, "prow", [(r, r ^ other) for r in range(n)])
            gathered = jnp.concatenate([gathered, moved[:count]], axis=0)
            leading = jnp.where(me & other != 0, moved[count:], kept)
            span, other = span // 2, other * 2
        pivot_rows = call(
            functools.partial(order_kernel, n, rows),
            jax.ShapeDtypeStruct((width, cols), F32),
            (pivot_row, gathered),
            scratch=[pltpu.VMEM((n * CAP, cols), F32)],
        )
        inverse = call(
            invert_kernel,
            jax.ShapeDtypeStruct(lower.shape, F32),
            (lower,),
            scratch=[pltpu.VMEM((width, width), F32)],
        )
        moved = lax.ppermute(inverse, "prow", [(r, r ^ 1) for r in range(n)])
        inverse = jnp.where(me & 1 != 0, moved, inverse)
        return leading, call(solve_kernel, jax.ShapeDtypeStruct((width, cols), F32), (inverse, pivot_rows))

    gathered, lower = lax.optimization_barrier((gathered, lower))
    moved = lax.ppermute(jnp.concatenate([gathered, gathered], axis=0), "prow", [(r, r ^ 1) for r in range(n)])
    gathered = jnp.concatenate([gathered, moved[:CAP]], axis=0)
    leading, upper_rows = unit(me < n, levels, lower, gathered, leading)
    return call(
        functools.partial(update_kernel, m),
        jax.ShapeDtypeStruct((rows, cols), F32),
        (local_rows, leading, upper_rows, slab, *tops, *rests),
        in_specs=[VMEM] * (2 * m + 4),
        out_specs=pl.BlockSpec(memory_space=pl.ANY),
        scratch=[
            pltpu.VMEM((rows + 8, cols), F32),
            pltpu.SMEM((1, 128), jnp.int32),
            pltpu.SemaphoreType.DMA((rows // width + 1,)),
        ],
    )


def solution(mesh):
    return jax.shard_map(
        functools.partial(local, mesh.shape["prow"], mesh.shape["pcol"]),
        mesh=mesh,
        in_specs=(P("prow", "pcol"), P("prow", "pcol"), P()),
        out_specs=P("prow", "pcol"),
        check_vma=False,
    )
```

```python
import functools

import jax
import jax.numpy as jnp
from jax import lax
from jax.experimental import pallas as pl
from jax.experimental.pallas import tpu as pltpu
from jax.sharding import PartitionSpec as P

CAP = 32
BLOCK = 32
F32 = jnp.float32
BF16 = jnp.bfloat16
VMEM = pl.BlockSpec(memory_space=pltpu.VMEM)
PARAMS = pltpu.CompilerParams(vmem_limit_bytes=24 * 1024 * 1024)


def split3(x):
    high = x.astype(BF16)
    rest = x - high.astype(F32)
    mid = rest.astype(BF16)
    low = (rest - mid.astype(F32)).astype(BF16)
    return high, mid, low


def split2(x):
    high = x.astype(BF16)
    return high, (x - high.astype(F32)).astype(BF16)


def select_rows(one_hot, x):
    return sum(jnp.dot(one_hot, part, preferred_element_type=F32) for part in split3(x))


def dot_full(a, b):
    high, mid, low = split3(a)
    left = jnp.concatenate([low, mid, high, mid, high, high], axis=1)
    high, mid, low = split3(b)
    right = jnp.concatenate([high, mid, low, high, mid, high], axis=0)
    return jnp.dot(left, right, preferred_element_type=F32)


def tree_partner(r, span):
    if span == 1 or r % span > 1:
        return r ^ 1
    if r % 2 == 0:
        return r + 1 if r & span else r + span
    return r - span if r & span else r - 1


def lead_place(owner, n):
    bits = n.bit_length() - 1
    return sum((lax.shift_right_logical(owner, bit) & 1) * (1 << (bits - 1 - bit)) for bit in range(bits))


def slots(pivot_row, rows):
    width = pivot_row.shape[1]
    by_sublane = jnp.broadcast_to(pivot_row, (width, width)).T
    shift = rows.bit_length() - 1
    owner_row = jnp.broadcast_to(lax.shift_right_logical(pivot_row, shift), (width, width))
    owner_col = lax.shift_right_logical(by_sublane, shift)
    sub = lax.broadcasted_iota(jnp.int32, (width, width), 0)
    lane = lax.broadcasted_iota(jnp.int32, (width, width), 1)
    same = owner_row == owner_col
    rank_row = jnp.sum(jnp.where(same & (sub < lane), 1, 0), axis=0, keepdims=True)
    rank_col = jnp.sum(jnp.where(same & (lane < sub), 1, 0), axis=1, keepdims=True)
    return owner_row[:1], rank_row, owner_col[:, :1], rank_col


def pack_kernel(pivot_ref, slab_ref, packed_ref, lead_ref, local_ref):
    rows = slab_ref.shape[0]
    width = pivot_ref.shape[1]
    count = lead_ref.shape[0]
    lanes = local_ref.shape[1]
    me = lax.axis_index("prow")
    pivot_row = pivot_ref[...]
    owner_row, rank_row, owner_col, rank_col = slots(pivot_row, rows)
    pivot_col = jnp.broadcast_to(pivot_row, (lanes, width)).T
    slot = lax.broadcasted_iota(jnp.int32, (width, lanes), 1)
    mine = (owner_col == me) & (rank_col == slot)
    local = jnp.sum(jnp.where(mine, pivot_col - (me + 1) * rows, 0), axis=0, keepdims=True) + rows
    local_ref[...] = local
    slot = lax.broadcasted_iota(jnp.int32, (CAP, width), 0)
    mine = (owner_row == me) & (rank_row == slot)
    local = jnp.sum(jnp.where(mine, pivot_row - (me + 1) * rows, 0), axis=1, keepdims=True) + rows
    one_hot = (lax.broadcasted_iota(jnp.int32, (CAP, rows), 1) == local).astype(F32).astype(BF16)
    packed_ref[...] = select_rows(one_hot, slab_ref[...])
    slot = lax.broadcasted_iota(jnp.int32, (count, width), 0)
    one_hot = (slot == lead_place(owner_row, count // CAP) * CAP + rank_row).astype(F32).astype(BF16)
    lead_ref[...] = select_rows(one_hot, slab_ref[:width, :])


def block_inverses(lower):
    width = lower.shape[0]
    lane = lax.broadcasted_iota(jnp.int32, (BLOCK, width), 1)
    sub = lax.broadcasted_iota(jnp.int32, (BLOCK, width), 0)
    block = lane // BLOCK
    within = lane % BLOCK
    diag = jnp.zeros((BLOCK, width), F32)
    for b in range(width // BLOCK):
        diag = jnp.where(block == b, lower[b * BLOCK : (b + 1) * BLOCK], diag)
    diag = jnp.where(within < sub, diag, 0.0)
    inv = jnp.where(within == sub, 1.0, 0.0).astype(F32)
    half = 128
    first = (lax.broadcasted_iota(jnp.int32, (BLOCK, half), 1) // BLOCK) * BLOCK
    outs = []
    for h in range(0, width, half):
        d, x = diag[:, h : h + half], inv[:, h : h + half]
        for k in range(BLOCK - 1):
            column = jnp.take_along_axis(d, first + k, axis=1)
            x = x - column * x[k : k + 1, :]
        outs.append(x)
    return outs


def order_kernel(n, rows, pivot_ref, gathered_ref, out_ref, gathered):
    width = pivot_ref.shape[1]
    me = lax.axis_index("prow")
    for q in range(n):
        source = jnp.bitwise_xor(me, q)
        gathered[pl.ds(pl.multiple_of(source * CAP, CAP), CAP), :] = gathered_ref[q * CAP : (q + 1) * CAP, :]
    _, _, owner_col, rank_col = slots(pivot_ref[...], rows)
    slot = lax.broadcasted_iota(jnp.int32, (width, gathered.shape[0]), 1)
    one_hot = (slot == owner_col * CAP + rank_col).astype(F32).astype(BF16)
    out_ref[...] = select_rows(one_hot, gathered[...])


def top_order(m):
    return [0, 1, *range(m - 1, 1, -1)]


def cut_kernel(panel_ref, top_ref, rest_ref, sems):
    width = top_ref.shape[1]
    copies = []
    for c in range(sems.shape[0]):
        target = rest_ref.at[:, pl.ds((c - 1) * width, width)] if c else top_ref
        copies.append(pltpu.make_async_copy(panel_ref.at[:, pl.ds(c * width, width)], target, sems.at[c]))
        copies[-1].start()
    for copy in copies:
        copy.wait()


def assemble_kernel(m, *refs):
    *pieces, out_ref, lower_t = refs
    width = lower_t.shape[0]
    piece = width // m
    half = width // 2
    z = lax.axis_index("pcol")
    for d, ref in zip(top_order(m), pieces):
        lower_t[pl.ds(pl.multiple_of(jnp.bitwise_xor(z, d) * piece, piece), piece), :] = ref[...]
    out_ref[:half, :] = lower_t[:half, :]
    out_ref[half:, :half] = lower_t[half : half + half // 2, half:]
    out_ref[half:, half:] = lower_t[half + half // 2 :, half:]


def pick_kernel(span, moved_ref, held_ref, out_ref):
    child = lax.rem(lax.axis_index("prow"), 2 * span) == span

    @pl.when(child)
    def _():
        out_ref[...] = moved_ref[...]

    @pl.when(jnp.logical_not(child))
    def _():
        out_ref[...] = held_ref[...]


def invert_kernel(lower_ref, out_ref, lower_t):
    width = lower_t.shape[0]
    half = width // 2
    lower_t[:half, :] = lower_ref[:half, :]
    lower_t[half:, :half] = jnp.zeros((half, half), F32)
    lower_t[half : half + half // 2, half:] = lower_ref[half:, :half]
    lower_t[half + half // 2 :, half:] = lower_ref[half:, half:]
    lower = lower_t[...].T
    blocks = block_inverses(lower)
    row = lax.broadcasted_iota(jnp.int32, (half, half), 0)
    col = lax.broadcasted_iota(jnp.int32, (half, half), 1)
    for h, strip in enumerate(blocks):
        corner = lower[h * half : (h + 1) * half, h * half : (h + 1) * half]
        inv = jnp.where(row // BLOCK == col // BLOCK, jnp.concatenate([strip] * (half // BLOCK), axis=0), 0.0)
        size = BLOCK
        while size < half:
            off = (row // (2 * size) == col // (2 * size)) & (row // size > col // size)
            inv = inv - dot_full(dot_full(inv, jnp.where(off, corner, 0.0)), inv)
            size *= 2
        out_ref[:half, h * half : (h + 1) * half] = inv
    out_ref[half:, :half] = lower[half : half + half // 2, :half]
    out_ref[half:, half:] = lower[half + half // 2 :, :half]


def solve_kernel(inverse_ref, pivot_rows_ref, x_ref):
    half = pivot_rows_ref.shape[0] // 2
    quarter = jnp.concatenate([inverse_ref[half:, :half], inverse_ref[half:, half:]], axis=0)
    first = dot_full(inverse_ref[:half, :half], pivot_rows_ref[:half, :])
    x_ref[:half, :] = first
    x_ref[half:, :] = dot_full(inverse_ref[:half, half:], pivot_rows_ref[half:, :] - dot_full(quarter, first))


def product(piece, upper):
    high, low = split2(piece)
    upper_high, upper_low = split2(upper)
    left = jnp.concatenate([high, high, low], axis=0)
    right = jnp.concatenate([upper_high, upper_low, upper_high], axis=0)
    return lax.dot_general(left, right, (((0,), (0,)), ((), ())), preferred_element_type=F32)


def piece_rows(x_ref, m, d):
    piece = x_ref.shape[0] // m
    source = jnp.bitwise_xor(lax.axis_index("pcol"), d)
    return x_ref[pl.ds(pl.multiple_of(source * piece, piece), piece), :]


def update_kernel(m, local_ref, lead_ref, x_ref, slab_ref, *refs):
    *pieces, out_ref, result, swaps, sems = refs
    tops, rests = dict(zip(top_order(m), pieces[:m])), pieces[m:]
    rows = slab_ref.shape[0]
    width = x_ref.shape[0]
    blocks = rows // width
    fetch = pltpu.make_async_copy(local_ref, swaps, sems.at[blocks])
    fetch.start()
    result[:rows, :] = slab_ref[...]
    uppers = [piece_rows(x_ref, m, d) for d in range(m)]
    copies = []
    for c in range(blocks):
        part = pl.ds(c * width, width)
        if c:
            total = sum(product(rests[d][:, (c - 1) * width : c * width], uppers[d]) for d in range(m))
        else:
            total = sum(product(tops[d][...], uppers[d]) for d in range(m))
            fetch.wait()
            for s in range(CAP):
                result[pl.ds(swaps[0, s], 1), :] = lead_ref[pl.ds(s, 1), :]
        result[part, :] = result[part, :] - total
        if c == 0:

            @pl.when(lax.axis_index("prow") == 0)
            def _():
                result[part, :] = x_ref[...]

        copy = pltpu.make_async_copy(result.at[part], out_ref.at[part], sems.at[c])
        copy.start()
        copies.append(copy)
    for copy in copies:
        copy.wait()


def unit(held, steps, *operands):
    shapes = jax.eval_shape(steps, *operands)
    return lax.cond(held, steps, lambda *_: jax.tree.map(lambda s: jnp.zeros(s.shape, s.dtype), shapes), *operands)


def call(kernel, outs, operands, in_specs=None, out_specs=None, scratch=()):
    return pl.pallas_call(
        kernel,
        out_shape=outs,
        in_specs=in_specs or [VMEM] * len(operands),
        out_specs=out_specs or jax.tree.map(lambda _: VMEM, outs),
        scratch_shapes=list(scratch),
        compiler_params=PARAMS,
        cost_estimate=pl.CostEstimate(flops=1, bytes_accessed=1, transcendentals=0),
    )(*operands)


def local(n, m, slab, panel, pivots):
    rows, cols = slab.shape
    width = pivots.shape[0]
    piece = panel.shape[1]
    me = lax.axis_index("prow")
    panel_t = panel.T
    pivot_row = pivots.reshape(1, width)

    def spread(block, order):
        return [block] + [lax.ppermute(block, "pcol", [(c, c ^ d) for c in range(m)]) for d in order]

    top, rest = call(
        cut_kernel,
        (jax.ShapeDtypeStruct((piece, width), F32), jax.ShapeDtypeStruct((piece, rows - width), F32)),
        (panel_t,),
        in_specs=[pl.BlockSpec(memory_space=pl.ANY)],
        scratch=[pltpu.SemaphoreType.DMA((rows // width,))],
    )
    tops, rests = spread(top, top_order(m)[1:]), spread(rest, range(1, m))

    gathered, leading, local_rows = call(
        pack_kernel,
        (
            jax.ShapeDtypeStruct((CAP, cols), F32),
            jax.ShapeDtypeStruct((n * CAP, cols), F32),
            jax.ShapeDtypeStruct((1, 128), jnp.int32),
        ),
        (pivot_row, slab),
    )
    lower = call(
        functools.partial(assemble_kernel, m),
        jax.ShapeDtypeStruct((width * 3 // 4, width), F32),
        tops,
        scratch=[pltpu.VMEM((width, width), F32)],
    )

    def split(leading):
        blocks = leading.reshape(2, -1, cols)
        return blocks[0], blocks[1]

    def levels(lower, gathered, leading):
        kept, sent = split(leading)
        moved = lax.ppermute(sent, "prow", [(r, r ^ 1) for r in range(n)])
        leading = jnp.where(me & 1 != 0, moved, kept)
        span, other = n // 2, 2
        while span > 1:
            moved = lax.ppermute(lower, "prow", [(r, tree_partner(r, span)) for r in range(n)])
            lower = call(
                functools.partial(pick_kernel, span),
                jax.ShapeDtypeStruct(lower.shape, F32),
                (moved, lower),
            )
            kept, sent = split(leading)
            count = gathered.shape[0]
            message = jnp.concatenate([gathered, sent], axis=0)
            moved = lax.ppermute(message, "prow", [(r, r ^ other) for r in range(n)])
            gathered = jnp.concatenate([gathered, moved[:count]], axis=0)
            leading = jnp.where(me & other != 0, moved[count:], kept)
            span, other = span // 2, other * 2
        pivot_rows = call(
            functools.partial(order_kernel, n, rows),
            jax.ShapeDtypeStruct((width, cols), F32),
            (pivot_row, gathered),
            scratch=[pltpu.VMEM((n * CAP, cols), F32)],
        )
        inverse = call(
            invert_kernel,
            jax.ShapeDtypeStruct(lower.shape, F32),
            (lower,),
            scratch=[pltpu.VMEM((width, width), F32)],
        )
        moved = lax.ppermute(inverse, "prow", [(r, r ^ 1) for r in range(n)])
        inverse = jnp.where(me & 1 != 0, moved, inverse)
        return leading, call(solve_kernel, jax.ShapeDtypeStruct((width, cols), F32), (inverse, pivot_rows))

    gathered, lower = lax.optimization_barrier((gathered, lower))
    moved = lax.ppermute(jnp.concatenate([gathered, gathered], axis=0), "prow", [(r, r ^ 1) for r in range(n)])
    gathered = jnp.concatenate([gathered, moved[:CAP]], axis=0)
    leading, upper_rows = unit(me < n, levels, lower, gathered, leading)
    return call(
        functools.partial(update_kernel, m),
        jax.ShapeDtypeStruct((rows, cols), F32),
        (local_rows, leading, upper_rows, slab, *tops, *rests),
        in_specs=[VMEM] * (2 * m + 4),
        out_specs=pl.BlockSpec(memory_space=pl.ANY),
        scratch=[
            pltpu.VMEM((rows + 8, cols), F32),
            pltpu.SMEM((1, 128), jnp.int32),
            pltpu.SemaphoreType.DMA((rows // width + 1,)),
        ],
    )


def solution(mesh):
    return jax.shard_map(
        functools.partial(local, mesh.shape["prow"], mesh.shape["pcol"]),
        mesh=mesh,
        in_specs=(P("prow", "pcol"), P("prow", "pcol"), P()),
        out_specs=P("prow", "pcol"),
        check_vma=False,
    )
```

```python
import functools

import jax
import jax.numpy as jnp
from jax import lax
from jax.experimental import pallas as pl
from jax.experimental.pallas import tpu as pltpu
from jax.sharding import PartitionSpec as P

CAP = 32
BLOCK = 32
F32 = jnp.float32
BF16 = jnp.bfloat16
VMEM = pl.BlockSpec(memory_space=pltpu.VMEM)
PARAMS = pltpu.CompilerParams(vmem_limit_bytes=24 * 1024 * 1024)


def split3(x):
    high = x.astype(BF16)
    rest = x - high.astype(F32)
    mid = rest.astype(BF16)
    low = (rest - mid.astype(F32)).astype(BF16)
    return high, mid, low


def split2(x):
    high = x.astype(BF16)
    return high, (x - high.astype(F32)).astype(BF16)


def select_rows(one_hot, x):
    return sum(jnp.dot(one_hot, part, preferred_element_type=F32) for part in split3(x))


def dot_full(a, b):
    high, mid, low = split3(a)
    left = jnp.concatenate([low, mid, high, mid, high, high], axis=1)
    high, mid, low = split3(b)
    right = jnp.concatenate([high, mid, low, high, mid, high], axis=0)
    return jnp.dot(left, right, preferred_element_type=F32)


def tree_partner(r, span):
    if span == 1 or r % span > 1:
        return r ^ 1
    if r % 2 == 0:
        return r + 1 if r & span else r + span
    return r - span if r & span else r - 1


def lead_place(owner, n):
    bits = n.bit_length() - 1
    return sum((lax.shift_right_logical(owner, bit) & 1) * (1 << (bits - 1 - bit)) for bit in range(bits))


def slots(pivot_row, rows):
    width = pivot_row.shape[1]
    by_sublane = jnp.broadcast_to(pivot_row, (width, width)).T
    shift = rows.bit_length() - 1
    owner_row = jnp.broadcast_to(lax.shift_right_logical(pivot_row, shift), (width, width))
    owner_col = lax.shift_right_logical(by_sublane, shift)
    sub = lax.broadcasted_iota(jnp.int32, (width, width), 0)
    lane = lax.broadcasted_iota(jnp.int32, (width, width), 1)
    same = owner_row == owner_col
    rank_row = jnp.sum(jnp.where(same & (sub < lane), 1, 0), axis=0, keepdims=True)
    rank_col = jnp.sum(jnp.where(same & (lane < sub), 1, 0), axis=1, keepdims=True)
    return owner_row[:1], rank_row, owner_col[:, :1], rank_col


def pack_kernel(pivot_ref, slab_ref, packed_ref, lead_ref, local_ref):
    rows = slab_ref.shape[0]
    width = pivot_ref.shape[1]
    count = lead_ref.shape[0]
    lanes = local_ref.shape[1]
    me = lax.axis_index("prow")
    pivot_row = pivot_ref[...]
    owner_row, rank_row, owner_col, rank_col = slots(pivot_row, rows)
    pivot_col = jnp.broadcast_to(pivot_row, (lanes, width)).T
    slot = lax.broadcasted_iota(jnp.int32, (width, lanes), 1)
    mine = (owner_col == me) & (rank_col == slot)
    local = jnp.sum(jnp.where(mine, pivot_col - (me + 1) * rows, 0), axis=0, keepdims=True) + rows
    local_ref[...] = local
    slot = lax.broadcasted_iota(jnp.int32, (CAP, width), 0)
    mine = (owner_row == me) & (rank_row == slot)
    local = jnp.sum(jnp.where(mine, pivot_row - (me + 1) * rows, 0), axis=1, keepdims=True) + rows
    one_hot = (lax.broadcasted_iota(jnp.int32, (CAP, rows), 1) == local).astype(F32).astype(BF16)
    packed_ref[...] = select_rows(one_hot, slab_ref[...])
    slot = lax.broadcasted_iota(jnp.int32, (count, width), 0)
    one_hot = (slot == lead_place(owner_row, count // CAP) * CAP + rank_row).astype(F32).astype(BF16)
    lead_ref[...] = select_rows(one_hot, slab_ref[:width, :])


def block_inverses(lower):
    width = lower.shape[0]
    lane = lax.broadcasted_iota(jnp.int32, (BLOCK, width), 1)
    sub = lax.broadcasted_iota(jnp.int32, (BLOCK, width), 0)
    block = lane // BLOCK
    within = lane % BLOCK
    diag = jnp.zeros((BLOCK, width), F32)
    for b in range(width // BLOCK):
        diag = jnp.where(block == b, lower[b * BLOCK : (b + 1) * BLOCK], diag)
    diag = jnp.where(within < sub, diag, 0.0)
    inv = jnp.where(within == sub, 1.0, 0.0).astype(F32)
    half = 128
    first = (lax.broadcasted_iota(jnp.int32, (BLOCK, half), 1) // BLOCK) * BLOCK
    outs = []
    for h in range(0, width, half):
        d, x = diag[:, h : h + half], inv[:, h : h + half]
        for k in range(BLOCK - 1):
            column = jnp.take_along_axis(d, first + k, axis=1)
            x = x - column * x[k : k + 1, :]
        outs.append(x)
    return outs


def order_kernel(n, rows, pivot_ref, gathered_ref, out_ref, gathered):
    width = pivot_ref.shape[1]
    me = lax.axis_index("prow")
    for q in range(n):
        source = jnp.bitwise_xor(me, q)
        gathered[pl.ds(pl.multiple_of(source * CAP, CAP), CAP), :] = gathered_ref[q * CAP : (q + 1) * CAP, :]
    _, _, owner_col, rank_col = slots(pivot_ref[...], rows)
    slot = lax.broadcasted_iota(jnp.int32, (width, gathered.shape[0]), 1)
    one_hot = (slot == owner_col * CAP + rank_col).astype(F32).astype(BF16)
    out_ref[...] = select_rows(one_hot, gathered[...])


def top_order(m):
    return [0, 1, *range(m - 1, 1, -1)]


def cut_kernel(panel_ref, top_ref, rest_ref, sems):
    width = top_ref.shape[1]
    copies = []
    for c in range(sems.shape[0]):
        target = rest_ref.at[:, pl.ds((c - 1) * width, width)] if c else top_ref
        copies.append(pltpu.make_async_copy(panel_ref.at[:, pl.ds(c * width, width)], target, sems.at[c]))
        copies[-1].start()
    for copy in copies:
        copy.wait()


def assemble_kernel(m, *refs):
    *pieces, out_ref, lower_t = refs
    width = lower_t.shape[0]
    piece = width // m
    half = width // 2
    z = lax.axis_index("pcol")
    for d, ref in zip(top_order(m), pieces):
        lower_t[pl.ds(pl.multiple_of(jnp.bitwise_xor(z, d) * piece, piece), piece), :] = ref[...]
    out_ref[:half, :] = lower_t[:half, :]
    out_ref[half:, :half] = lower_t[half : half + half // 2, half:]
    out_ref[half:, half:] = lower_t[half + half // 2 :, half:]


def pick_kernel(span, moved_ref, held_ref, out_ref):
    child = lax.rem(lax.axis_index("prow"), 2 * span) == span

    @pl.when(child)
    def _():
        out_ref[...] = moved_ref[...]

    @pl.when(jnp.logical_not(child))
    def _():
        out_ref[...] = held_ref[...]


def invert_kernel(lower_ref, out_ref, lower_t):
    width = lower_t.shape[0]
    half = width // 2
    lower_t[:half, :] = lower_ref[:half, :]
    lower_t[half:, :half] = jnp.zeros((half, half), F32)
    lower_t[half : half + half // 2, half:] = lower_ref[half:, :half]
    lower_t[half + half // 2 :, half:] = lower_ref[half:, half:]
    lower = lower_t[...].T
    blocks = block_inverses(lower)
    row = lax.broadcasted_iota(jnp.int32, (half, half), 0)
    col = lax.broadcasted_iota(jnp.int32, (half, half), 1)
    for h, strip in enumerate(blocks):
        corner = lower[h * half : (h + 1) * half, h * half : (h + 1) * half]
        inv = jnp.where(row // BLOCK == col // BLOCK, jnp.concatenate([strip] * (half // BLOCK), axis=0), 0.0)
        size = BLOCK
        while size < half:
            off = (row // (2 * size) == col // (2 * size)) & (row // size > col // size)
            inv = inv - dot_full(dot_full(inv, jnp.where(off, corner, 0.0)), inv)
            size *= 2
        out_ref[:half, h * half : (h + 1) * half] = inv
    out_ref[half:, :half] = lower[half : half + half // 2, :half]
    out_ref[half:, half:] = lower[half + half // 2 :, :half]


def solve_kernel(inverse_ref, pivot_rows_ref, x_ref):
    half = pivot_rows_ref.shape[0] // 2
    quarter = jnp.concatenate([inverse_ref[half:, :half], inverse_ref[half:, half:]], axis=0)
    first = dot_full(inverse_ref[:half, :half], pivot_rows_ref[:half, :])
    x_ref[:half, :] = first
    x_ref[half:, :] = dot_full(inverse_ref[:half, half:], pivot_rows_ref[half:, :] - dot_full(quarter, first))


def product(piece, upper):
    high, low = split2(piece)
    upper_high, upper_low = split2(upper)
    left = jnp.concatenate([high, high, low], axis=0)
    right = jnp.concatenate([upper_high, upper_low, upper_high], axis=0)
    return lax.dot_general(left, right, (((0,), (0,)), ((), ())), preferred_element_type=F32)


def piece_rows(x_ref, m, d):
    piece = x_ref.shape[0] // m
    source = jnp.bitwise_xor(lax.axis_index("pcol"), d)
    return x_ref[pl.ds(pl.multiple_of(source * piece, piece), piece), :]


def update_kernel(m, local_ref, lead_ref, x_ref, slab_ref, *refs):
    *pieces, out_ref, result, swaps, sems = refs
    tops, rests = dict(zip(top_order(m), pieces[:m])), pieces[m:]
    rows = slab_ref.shape[0]
    width = x_ref.shape[0]
    blocks = rows // width
    fetch = pltpu.make_async_copy(local_ref, swaps, sems.at[blocks])
    fetch.start()
    result[:rows, :] = slab_ref[...]
    uppers = [piece_rows(x_ref, m, d) for d in range(m)]
    copies = []
    for c in range(blocks):
        part = pl.ds(c * width, width)
        if c:
            total = sum(product(rests[d][:, (c - 1) * width : c * width], uppers[d]) for d in range(m))
        else:
            total = sum(product(tops[d][...], uppers[d]) for d in range(m))
            fetch.wait()
            for s in range(CAP):
                result[pl.ds(swaps[0, s], 1), :] = lead_ref[pl.ds(s, 1), :]
        result[part, :] = result[part, :] - total
        if c == 0:

            @pl.when(lax.axis_index("prow") == 0)
            def _():
                result[part, :] = x_ref[...]

        copy = pltpu.make_async_copy(result.at[part], out_ref.at[part], sems.at[c])
        copy.start()
        copies.append(copy)
    for copy in copies:
        copy.wait()


def unit(held, steps, *operands):
    shapes = jax.eval_shape(steps, *operands)
    return lax.cond(held, steps, lambda *_: jax.tree.map(lambda s: jnp.zeros(s.shape, s.dtype), shapes), *operands)


def call(kernel, outs, operands, in_specs=None, out_specs=None, scratch=()):
    return pl.pallas_call(
        kernel,
        out_shape=outs,
        in_specs=in_specs or [VMEM] * len(operands),
        out_specs=out_specs or jax.tree.map(lambda _: VMEM, outs),
        scratch_shapes=list(scratch),
        compiler_params=PARAMS,
        cost_estimate=pl.CostEstimate(flops=1, bytes_accessed=1, transcendentals=0),
    )(*operands)


def local(n, m, slab, panel, pivots):
    rows, cols = slab.shape
    width = pivots.shape[0]
    piece = panel.shape[1]
    me = lax.axis_index("prow")
    panel_t = panel.T
    pivot_row = pivots.reshape(1, width)

    def exchange(block, d):
        return lax.ppermute(block, "pcol", [(c, c ^ d) for c in range(m)])

    top, rest = call(
        cut_kernel,
        (jax.ShapeDtypeStruct((piece, width), F32), jax.ShapeDtypeStruct((piece, rows - width), F32)),
        (panel_t,),
        in_specs=[pl.BlockSpec(memory_space=pl.ANY)],
        scratch=[pltpu.SemaphoreType.DMA((rows // width,))],
    )
    tops = [top] + [exchange(top, d) for d in top_order(m)[1:]]
    rests = [rest] + [exchange(rest, d) for d in range(1, m)]

    gathered, leading, local_rows = call(
        pack_kernel,
        (
            jax.ShapeDtypeStruct((CAP, cols), F32),
            jax.ShapeDtypeStruct((n * CAP, cols), F32),
            jax.ShapeDtypeStruct((1, 128), jnp.int32),
        ),
        (pivot_row, slab),
    )
    lower = call(
        functools.partial(assemble_kernel, m),
        jax.ShapeDtypeStruct((width * 3 // 4, width), F32),
        tops,
        scratch=[pltpu.VMEM((width, width), F32)],
    )

    def split(leading):
        blocks = leading.reshape(2, -1, cols)
        return blocks[0], blocks[1]

    def levels(lower, gathered, leading):
        span, other = n // 2, 2
        while span > 1:
            moved = lax.ppermute(lower, "prow", [(r, tree_partner(r, span)) for r in range(n)])
            lower = call(
                functools.partial(pick_kernel, span),
                jax.ShapeDtypeStruct(lower.shape, F32),
                (moved, lower),
            )
            kept, sent = split(leading)
            count = gathered.shape[0]
            message = jnp.concatenate([gathered, sent], axis=0)
            moved = lax.ppermute(message, "prow", [(r, r ^ other) for r in range(n)])
            gathered = jnp.concatenate([gathered, moved[:count]], axis=0)
            leading = jnp.where(me & other != 0, moved[count:], kept)
            span, other = span // 2, other * 2
        pivot_rows = call(
            functools.partial(order_kernel, n, rows),
            jax.ShapeDtypeStruct((width, cols), F32),
            (pivot_row, gathered),
            scratch=[pltpu.VMEM((n * CAP, cols), F32)],
        )
        inverse = call(
            invert_kernel,
            jax.ShapeDtypeStruct(lower.shape, F32),
            (lower,),
            scratch=[pltpu.VMEM((width, width), F32)],
        )
        moved = lax.ppermute(inverse, "prow", [(r, r ^ 1) for r in range(n)])
        inverse = jnp.where(me & 1 != 0, moved, inverse)
        return leading, call(solve_kernel, jax.ShapeDtypeStruct((width, cols), F32), (inverse, pivot_rows))

    gathered, lower = lax.optimization_barrier((gathered, lower))
    twins = [(r, r ^ 1) for r in range(n)]
    moved = lax.ppermute(gathered, "prow", twins)
    gathered = jnp.concatenate([gathered, moved], axis=0)
    kept, sent = split(leading)
    leading = jnp.where(me & 1 != 0, lax.ppermute(sent, "prow", twins), kept)
    leading, upper_rows = unit(me < n, levels, lower, gathered, leading)
    return call(
        functools.partial(update_kernel, m),
        jax.ShapeDtypeStruct((rows, cols), F32),
        (local_rows, leading, upper_rows, slab, *tops, *rests),
        in_specs=[VMEM] * (2 * m + 4),
        out_specs=pl.BlockSpec(memory_space=pl.ANY),
        scratch=[
            pltpu.VMEM((rows + 8, cols), F32),
            pltpu.SMEM((1, 128), jnp.int32),
            pltpu.SemaphoreType.DMA((rows // width + 1,)),
        ],
    )


def solution(mesh):
    return jax.shard_map(
        functools.partial(local, mesh.shape["prow"], mesh.shape["pcol"]),
        mesh=mesh,
        in_specs=(P("prow", "pcol"), P("prow", "pcol"), P()),
        out_specs=P("prow", "pcol"),
        check_vma=False,
    )
```

```python
import functools

import jax
import jax.numpy as jnp
from jax import lax
from jax.experimental import pallas as pl
from jax.experimental.pallas import tpu as pltpu
from jax.sharding import PartitionSpec as P

CAP = 32
BLOCK = 32
F32 = jnp.float32
BF16 = jnp.bfloat16
VMEM = pl.BlockSpec(memory_space=pltpu.VMEM)
PARAMS = pltpu.CompilerParams(vmem_limit_bytes=24 * 1024 * 1024)


def split3(x):
    high = x.astype(BF16)
    rest = x - high.astype(F32)
    mid = rest.astype(BF16)
    low = (rest - mid.astype(F32)).astype(BF16)
    return high, mid, low


def split2(x):
    high = x.astype(BF16)
    return high, (x - high.astype(F32)).astype(BF16)


def select_rows(one_hot, x):
    return sum(jnp.dot(one_hot, part, preferred_element_type=F32) for part in split3(x))


def dot_full(a, b):
    high, mid, low = split3(a)
    left = jnp.concatenate([low, mid, high, mid, high, high], axis=1)
    high, mid, low = split3(b)
    right = jnp.concatenate([high, mid, low, high, mid, high], axis=0)
    return jnp.dot(left, right, preferred_element_type=F32)


def tree_partner(r, span):
    if span == 1 or r % span > 1:
        return r ^ 1
    if r % 2 == 0:
        return r + 1 if r & span else r + span
    return r - span if r & span else r - 1


def lead_place(owner, n):
    bits = n.bit_length() - 1
    return sum((lax.shift_right_logical(owner, bit) & 1) * (1 << (bits - 1 - bit)) for bit in range(bits))


def slots(pivot_row, rows):
    width = pivot_row.shape[1]
    by_sublane = jnp.broadcast_to(pivot_row, (width, width)).T
    shift = rows.bit_length() - 1
    owner_row = jnp.broadcast_to(lax.shift_right_logical(pivot_row, shift), (width, width))
    owner_col = lax.shift_right_logical(by_sublane, shift)
    sub = lax.broadcasted_iota(jnp.int32, (width, width), 0)
    lane = lax.broadcasted_iota(jnp.int32, (width, width), 1)
    same = owner_row == owner_col
    rank_row = jnp.sum(jnp.where(same & (sub < lane), 1, 0), axis=0, keepdims=True)
    rank_col = jnp.sum(jnp.where(same & (lane < sub), 1, 0), axis=1, keepdims=True)
    return owner_row[:1], rank_row, owner_col[:, :1], rank_col


def pack_kernel(pivot_ref, slab_ref, packed_ref, lead_ref, local_ref):
    rows = slab_ref.shape[0]
    width = pivot_ref.shape[1]
    count = lead_ref.shape[0]
    lanes = local_ref.shape[1]
    me = lax.axis_index("prow")
    pivot_row = pivot_ref[...]
    owner_row, rank_row, owner_col, rank_col = slots(pivot_row, rows)
    pivot_col = jnp.broadcast_to(pivot_row, (lanes, width)).T
    slot = lax.broadcasted_iota(jnp.int32, (width, lanes), 1)
    mine = (owner_col == me) & (rank_col == slot)
    local = jnp.sum(jnp.where(mine, pivot_col - (me + 1) * rows, 0), axis=0, keepdims=True) + rows
    local_ref[...] = local
    slot = lax.broadcasted_iota(jnp.int32, (CAP, width), 0)
    mine = (owner_row == me) & (rank_row == slot)
    local = jnp.sum(jnp.where(mine, pivot_row - (me + 1) * rows, 0), axis=1, keepdims=True) + rows
    one_hot = (lax.broadcasted_iota(jnp.int32, (CAP, rows), 1) == local).astype(F32).astype(BF16)
    packed_ref[...] = select_rows(one_hot, slab_ref[...])
    slot = lax.broadcasted_iota(jnp.int32, (count, width), 0)
    one_hot = (slot == lead_place(owner_row, count // CAP) * CAP + rank_row).astype(F32).astype(BF16)
    lead_ref[...] = select_rows(one_hot, slab_ref[:width, :])


def block_inverses(lower):
    width = lower.shape[0]
    lane = lax.broadcasted_iota(jnp.int32, (BLOCK, width), 1)
    sub = lax.broadcasted_iota(jnp.int32, (BLOCK, width), 0)
    block = lane // BLOCK
    within = lane % BLOCK
    diag = jnp.zeros((BLOCK, width), F32)
    for b in range(width // BLOCK):
        diag = jnp.where(block == b, lower[b * BLOCK : (b + 1) * BLOCK], diag)
    diag = jnp.where(within < sub, diag, 0.0)
    inv = jnp.where(within == sub, 1.0, 0.0).astype(F32)
    half = 128
    first = (lax.broadcasted_iota(jnp.int32, (BLOCK, half), 1) // BLOCK) * BLOCK
    outs = []
    for h in range(0, width, half):
        d, x = diag[:, h : h + half], inv[:, h : h + half]
        for k in range(BLOCK - 1):
            column = jnp.take_along_axis(d, first + k, axis=1)
            x = x - column * x[k : k + 1, :]
        outs.append(x)
    return outs


def order_kernel(n, rows, pivot_ref, gathered_ref, out_ref, gathered):
    width = pivot_ref.shape[1]
    me = lax.axis_index("prow")
    for q in range(n):
        source = jnp.bitwise_xor(me, q)
        gathered[pl.ds(pl.multiple_of(source * CAP, CAP), CAP), :] = gathered_ref[q * CAP : (q + 1) * CAP, :]
    _, _, owner_col, rank_col = slots(pivot_ref[...], rows)
    slot = lax.broadcasted_iota(jnp.int32, (width, gathered.shape[0]), 1)
    one_hot = (slot == owner_col * CAP + rank_col).astype(F32).astype(BF16)
    out_ref[...] = select_rows(one_hot, gathered[...])


def top_order(m):
    return [0, 1, *range(m - 1, 1, -1)]


def cut_kernel(panel_ref, top_ref, rest_ref, sems):
    width = top_ref.shape[1]
    copies = []
    for c in range(sems.shape[0]):
        target = rest_ref.at[:, pl.ds((c - 1) * width, width)] if c else top_ref
        copies.append(pltpu.make_async_copy(panel_ref.at[:, pl.ds(c * width, width)], target, sems.at[c]))
        copies[-1].start()
    for copy in copies:
        copy.wait()


def assemble_kernel(m, *refs):
    *pieces, out_ref, lower_t = refs
    width = lower_t.shape[0]
    piece = width // m
    half = width // 2
    z = lax.axis_index("pcol")
    for d, ref in zip(top_order(m), pieces):
        lower_t[pl.ds(pl.multiple_of(jnp.bitwise_xor(z, d) * piece, piece), piece), :] = ref[...]
    out_ref[:half, :] = lower_t[:half, :]
    out_ref[half:, :half] = lower_t[half : half + half // 2, half:]
    out_ref[half:, half:] = lower_t[half + half // 2 :, half:]


def pick_kernel(span, moved_ref, held_ref, out_ref):
    child = lax.rem(lax.axis_index("prow"), 2 * span) == span

    @pl.when(child)
    def _():
        out_ref[...] = moved_ref[...]

    @pl.when(jnp.logical_not(child))
    def _():
        out_ref[...] = held_ref[...]


def invert_kernel(lower_ref, out_ref, lower_t):
    width = lower_t.shape[0]
    half = width // 2
    lower_t[:half, :] = lower_ref[:half, :]
    lower_t[half:, :half] = jnp.zeros((half, half), F32)
    lower_t[half : half + half // 2, half:] = lower_ref[half:, :half]
    lower_t[half + half // 2 :, half:] = lower_ref[half:, half:]
    lower = lower_t[...].T
    blocks = block_inverses(lower)
    row = lax.broadcasted_iota(jnp.int32, (half, half), 0)
    col = lax.broadcasted_iota(jnp.int32, (half, half), 1)
    for h, strip in enumerate(blocks):
        corner = lower[h * half : (h + 1) * half, h * half : (h + 1) * half]
        inv = jnp.where(row // BLOCK == col // BLOCK, jnp.concatenate([strip] * (half // BLOCK), axis=0), 0.0)
        size = BLOCK
        while size < half:
            off = (row // (2 * size) == col // (2 * size)) & (row // size > col // size)
            inv = inv - dot_full(dot_full(inv, jnp.where(off, corner, 0.0)), inv)
            size *= 2
        out_ref[:half, h * half : (h + 1) * half] = inv
    out_ref[half:, :half] = lower[half : half + half // 2, :half]
    out_ref[half:, half:] = lower[half + half // 2 :, :half]


def solve_kernel(inverse_ref, pivot_rows_ref, x_ref):
    half = pivot_rows_ref.shape[0] // 2
    quarter = jnp.concatenate([inverse_ref[half:, :half], inverse_ref[half:, half:]], axis=0)
    first = dot_full(inverse_ref[:half, :half], pivot_rows_ref[:half, :])
    x_ref[:half, :] = first
    x_ref[half:, :] = dot_full(inverse_ref[:half, half:], pivot_rows_ref[half:, :] - dot_full(quarter, first))


def product(piece, upper):
    high, low = split2(piece)
    upper_high, upper_low = split2(upper)
    left = jnp.concatenate([high, high, low], axis=0)
    right = jnp.concatenate([upper_high, upper_low, upper_high], axis=0)
    return lax.dot_general(left, right, (((0,), (0,)), ((), ())), preferred_element_type=F32)


def piece_rows(x_ref, m, d):
    piece = x_ref.shape[0] // m
    source = jnp.bitwise_xor(lax.axis_index("pcol"), d)
    return x_ref[pl.ds(pl.multiple_of(source * piece, piece), piece), :]


def update_kernel(m, local_ref, lead_ref, x_ref, slab_ref, *refs):
    *pieces, out_ref, result, swaps, sems = refs
    tops, rests = dict(zip(top_order(m), pieces[:m])), pieces[m:]
    rows = slab_ref.shape[0]
    width = x_ref.shape[0]
    blocks = rows // width
    fetch = pltpu.make_async_copy(local_ref, swaps, sems.at[blocks])
    fetch.start()
    result[:rows, :] = slab_ref[...]
    uppers = [piece_rows(x_ref, m, d) for d in range(m)]
    copies = []
    for c in range(blocks):
        part = pl.ds(c * width, width)
        if c:
            total = sum(product(rests[d][:, (c - 1) * width : c * width], uppers[d]) for d in range(m))
        else:
            total = sum(product(tops[d][...], uppers[d]) for d in range(m))
            fetch.wait()
            for s in range(CAP):
                result[pl.ds(swaps[0, s], 1), :] = lead_ref[pl.ds(s, 1), :]
        result[part, :] = result[part, :] - total
        if c == 0:

            @pl.when(lax.axis_index("prow") == 0)
            def _():
                result[part, :] = x_ref[...]

        copy = pltpu.make_async_copy(result.at[part], out_ref.at[part], sems.at[c])
        copy.start()
        copies.append(copy)
    for copy in copies:
        copy.wait()


def unit(held, steps, *operands):
    shapes = jax.eval_shape(steps, *operands)
    return lax.cond(held, steps, lambda *_: jax.tree.map(lambda s: jnp.zeros(s.shape, s.dtype), shapes), *operands)


def call(kernel, outs, operands, in_specs=None, out_specs=None, scratch=()):
    return pl.pallas_call(
        kernel,
        out_shape=outs,
        in_specs=in_specs or [VMEM] * len(operands),
        out_specs=out_specs or jax.tree.map(lambda _: VMEM, outs),
        scratch_shapes=list(scratch),
        compiler_params=PARAMS,
        cost_estimate=pl.CostEstimate(flops=1, bytes_accessed=1, transcendentals=0),
    )(*operands)


def local(n, m, slab, panel, pivots):
    rows, cols = slab.shape
    width = pivots.shape[0]
    piece = panel.shape[1]
    me = lax.axis_index("prow")
    panel_t = panel.T
    pivot_row = pivots.reshape(1, width)

    def exchange(block, d):
        return lax.ppermute(block, "pcol", [(c, c ^ d) for c in range(m)])

    top, rest = call(
        cut_kernel,
        (jax.ShapeDtypeStruct((piece, width), F32), jax.ShapeDtypeStruct((piece, rows - width), F32)),
        (panel_t,),
        in_specs=[pl.BlockSpec(memory_space=pl.ANY)],
        scratch=[pltpu.SemaphoreType.DMA((rows // width,))],
    )
    tops = [top] + [exchange(top, d) for d in top_order(m)[1:]]
    rests = [rest] + [exchange(rest, d) for d in range(1, m)]

    gathered, leading, local_rows = call(
        pack_kernel,
        (
            jax.ShapeDtypeStruct((CAP, cols), F32),
            jax.ShapeDtypeStruct((n * CAP, cols), F32),
            jax.ShapeDtypeStruct((1, 128), jnp.int32),
        ),
        (pivot_row, slab),
    )
    lower = call(
        functools.partial(assemble_kernel, m),
        jax.ShapeDtypeStruct((width * 3 // 4, width), F32),
        tops,
        scratch=[pltpu.VMEM((width, width), F32)],
    )

    def split(leading):
        blocks = leading.reshape(2, -1, cols)
        return blocks[0], blocks[1]

    def levels(lower, gathered, leading):
        span, other, held = n // 2, 2, lower
        while span > 1:
            moved = lax.ppermute(lower, "prow", [(r, tree_partner(r, span)) for r in range(n)])
            lower = call(
                functools.partial(pick_kernel, span),
                jax.ShapeDtypeStruct(lower.shape, F32),
                (moved, held),
            )
            kept, sent = split(leading)
            count = gathered.shape[0]
            message = jnp.concatenate([gathered, sent], axis=0)
            moved = lax.ppermute(message, "prow", [(r, r ^ other) for r in range(n)])
            moved, held = lax.optimization_barrier((moved, lower))
            gathered = jnp.concatenate([gathered, moved[:count]], axis=0)
            leading = jnp.where(me & other != 0, moved[count:], kept)
            span, other = span // 2, other * 2
        pivot_rows = call(
            functools.partial(order_kernel, n, rows),
            jax.ShapeDtypeStruct((width, cols), F32),
            (pivot_row, gathered),
            scratch=[pltpu.VMEM((n * CAP, cols), F32)],
        )
        inverse = call(
            invert_kernel,
            jax.ShapeDtypeStruct(lower.shape, F32),
            (lower,),
            scratch=[pltpu.VMEM((width, width), F32)],
        )
        moved = lax.ppermute(inverse, "prow", [(r, r ^ 1) for r in range(n)])
        inverse = jnp.where(me & 1 != 0, moved, inverse)
        return leading, call(solve_kernel, jax.ShapeDtypeStruct((width, cols), F32), (inverse, pivot_rows))

    gathered, lower = lax.optimization_barrier((gathered, lower))
    twins = [(r, r ^ 1) for r in range(n)]
    moved = lax.ppermute(gathered, "prow", twins)
    gathered = jnp.concatenate([gathered, moved], axis=0)
    kept, sent = split(leading)
    leading = jnp.where(me & 1 != 0, lax.ppermute(sent, "prow", twins), kept)
    leading, upper_rows = unit(me < n, levels, lower, gathered, leading)
    return call(
        functools.partial(update_kernel, m),
        jax.ShapeDtypeStruct((rows, cols), F32),
        (local_rows, leading, upper_rows, slab, *tops, *rests),
        in_specs=[VMEM] * (2 * m + 4),
        out_specs=pl.BlockSpec(memory_space=pl.ANY),
        scratch=[
            pltpu.VMEM((rows + 8, cols), F32),
            pltpu.SMEM((1, 128), jnp.int32),
            pltpu.SemaphoreType.DMA((rows // width + 1,)),
        ],
    )


def solution(mesh):
    return jax.shard_map(
        functools.partial(local, mesh.shape["prow"], mesh.shape["pcol"]),
        mesh=mesh,
        in_specs=(P("prow", "pcol"), P("prow", "pcol"), P()),
        out_specs=P("prow", "pcol"),
        check_vma=False,
    )
```

```python
import functools

import jax
import jax.numpy as jnp
from jax import lax
from jax.experimental import pallas as pl
from jax.experimental.pallas import tpu as pltpu
from jax.sharding import PartitionSpec as P

CAP = 32
BLOCK = 32
F32 = jnp.float32
BF16 = jnp.bfloat16
VMEM = pl.BlockSpec(memory_space=pltpu.VMEM)
PARAMS = pltpu.CompilerParams(vmem_limit_bytes=24 * 1024 * 1024)


def split3(x):
    high = x.astype(BF16)
    rest = x - high.astype(F32)
    mid = rest.astype(BF16)
    low = (rest - mid.astype(F32)).astype(BF16)
    return high, mid, low


def split2(x):
    high = x.astype(BF16)
    return high, (x - high.astype(F32)).astype(BF16)


def select_rows(one_hot, x):
    return sum(jnp.dot(one_hot, part, preferred_element_type=F32) for part in split3(x))


def dot_full(a, b):
    high, mid, low = split3(a)
    left = jnp.concatenate([low, mid, high, mid, high, high], axis=1)
    high, mid, low = split3(b)
    right = jnp.concatenate([high, mid, low, high, mid, high], axis=0)
    return jnp.dot(left, right, preferred_element_type=F32)


def tree_partner(r, span):
    if span == 1 or r % span > 1:
        return r ^ 1
    if r % 2 == 0:
        return r + 1 if r & span else r + span
    return r - span if r & span else r - 1


def lead_place(owner, n):
    bits = n.bit_length() - 1
    return sum((lax.shift_right_logical(owner, bit) & 1) * (1 << (bits - 1 - bit)) for bit in range(bits))


def slots(pivot_row, rows):
    width = pivot_row.shape[1]
    by_sublane = jnp.broadcast_to(pivot_row, (width, width)).T
    shift = rows.bit_length() - 1
    owner_row = jnp.broadcast_to(lax.shift_right_logical(pivot_row, shift), (width, width))
    owner_col = lax.shift_right_logical(by_sublane, shift)
    sub = lax.broadcasted_iota(jnp.int32, (width, width), 0)
    lane = lax.broadcasted_iota(jnp.int32, (width, width), 1)
    same = owner_row == owner_col
    rank_row = jnp.sum(jnp.where(same & (sub < lane), 1, 0), axis=0, keepdims=True)
    rank_col = jnp.sum(jnp.where(same & (lane < sub), 1, 0), axis=1, keepdims=True)
    return owner_row[:1], rank_row, owner_col[:, :1], rank_col


def pack_kernel(pivot_ref, slab_ref, packed_ref, lead_ref, local_ref):
    rows = slab_ref.shape[0]
    width = pivot_ref.shape[1]
    count = lead_ref.shape[0]
    lanes = local_ref.shape[1]
    me = lax.axis_index("prow")
    pivot_row = pivot_ref[...]
    owner_row, rank_row, owner_col, rank_col = slots(pivot_row, rows)
    pivot_col = jnp.broadcast_to(pivot_row, (lanes, width)).T
    slot = lax.broadcasted_iota(jnp.int32, (width, lanes), 1)
    mine = (owner_col == me) & (rank_col == slot)
    local = jnp.sum(jnp.where(mine, pivot_col - (me + 1) * rows, 0), axis=0, keepdims=True) + rows
    local_ref[...] = local
    slot = lax.broadcasted_iota(jnp.int32, (CAP, width), 0)
    mine = (owner_row == me) & (rank_row == slot)
    local = jnp.sum(jnp.where(mine, pivot_row - (me + 1) * rows, 0), axis=1, keepdims=True) + rows
    one_hot = (lax.broadcasted_iota(jnp.int32, (CAP, rows), 1) == local).astype(F32).astype(BF16)
    packed_ref[...] = select_rows(one_hot, slab_ref[...])
    slot = lax.broadcasted_iota(jnp.int32, (count, width), 0)
    one_hot = (slot == lead_place(owner_row, count // CAP) * CAP + rank_row).astype(F32).astype(BF16)
    lead_ref[...] = select_rows(one_hot, slab_ref[:width, :])


def block_inverses(lower):
    width = lower.shape[0]
    lane = lax.broadcasted_iota(jnp.int32, (BLOCK, width), 1)
    sub = lax.broadcasted_iota(jnp.int32, (BLOCK, width), 0)
    block = lane // BLOCK
    within = lane % BLOCK
    diag = jnp.zeros((BLOCK, width), F32)
    for b in range(width // BLOCK):
        diag = jnp.where(block == b, lower[b * BLOCK : (b + 1) * BLOCK], diag)
    diag = jnp.where(within < sub, diag, 0.0)
    inv = jnp.where(within == sub, 1.0, 0.0).astype(F32)
    half = 128
    first = (lax.broadcasted_iota(jnp.int32, (BLOCK, half), 1) // BLOCK) * BLOCK
    outs = []
    for h in range(0, width, half):
        d, x = diag[:, h : h + half], inv[:, h : h + half]
        for k in range(BLOCK - 1):
            column = jnp.take_along_axis(d, first + k, axis=1)
            x = x - column * x[k : k + 1, :]
        outs.append(x)
    return outs


def order_kernel(n, rows, pivot_ref, gathered_ref, out_ref, gathered):
    width = pivot_ref.shape[1]
    me = lax.axis_index("prow")
    for q in range(n):
        source = jnp.bitwise_xor(me, q)
        gathered[pl.ds(pl.multiple_of(source * CAP, CAP), CAP), :] = gathered_ref[q * CAP : (q + 1) * CAP, :]
    _, _, owner_col, rank_col = slots(pivot_ref[...], rows)
    slot = lax.broadcasted_iota(jnp.int32, (width, gathered.shape[0]), 1)
    one_hot = (slot == owner_col * CAP + rank_col).astype(F32).astype(BF16)
    out_ref[...] = select_rows(one_hot, gathered[...])


def top_order(m):
    return [0, 1, *range(m - 1, 1, -1)]


def cut_kernel(panel_ref, top_ref, rest_ref, sems):
    width = top_ref.shape[1]
    copies = []
    for c in range(sems.shape[0]):
        target = rest_ref.at[:, pl.ds((c - 1) * width, width)] if c else top_ref
        copies.append(pltpu.make_async_copy(panel_ref.at[:, pl.ds(c * width, width)], target, sems.at[c]))
        copies[-1].start()
    for copy in copies:
        copy.wait()


def assemble_kernel(m, *refs):
    *pieces, out_ref, lower_t = refs
    width = lower_t.shape[0]
    piece = width // m
    half = width // 2
    z = lax.axis_index("pcol")
    for d, ref in zip(top_order(m), pieces):
        lower_t[pl.ds(pl.multiple_of(jnp.bitwise_xor(z, d) * piece, piece), piece), :] = ref[...]
    out_ref[:half, :] = lower_t[:half, :]
    out_ref[half:, :half] = lower_t[half : half + half // 2, half:]
    out_ref[half:, half:] = lower_t[half + half // 2 :, half:]


def pick_kernel(span, moved_ref, held_ref, out_ref):
    child = lax.rem(lax.axis_index("prow"), 2 * span) == span

    @pl.when(child)
    def _():
        out_ref[...] = moved_ref[...]

    @pl.when(jnp.logical_not(child))
    def _():
        out_ref[...] = held_ref[...]


def invert_kernel(lower_ref, out_ref, lower_t):
    width = lower_t.shape[0]
    half = width // 2
    lower_t[:half, :] = lower_ref[:half, :]
    lower_t[half:, :half] = jnp.zeros((half, half), F32)
    lower_t[half : half + half // 2, half:] = lower_ref[half:, :half]
    lower_t[half + half // 2 :, half:] = lower_ref[half:, half:]
    lower = lower_t[...].T
    blocks = block_inverses(lower)
    row = lax.broadcasted_iota(jnp.int32, (half, half), 0)
    col = lax.broadcasted_iota(jnp.int32, (half, half), 1)
    for h, strip in enumerate(blocks):
        corner = lower[h * half : (h + 1) * half, h * half : (h + 1) * half]
        inv = jnp.where(row // BLOCK == col // BLOCK, jnp.concatenate([strip] * (half // BLOCK), axis=0), 0.0)
        size = BLOCK
        while size < half:
            off = (row // (2 * size) == col // (2 * size)) & (row // size > col // size)
            inv = inv - dot_full(dot_full(inv, jnp.where(off, corner, 0.0)), inv)
            size *= 2
        out_ref[:half, h * half : (h + 1) * half] = inv
    out_ref[half:, :half] = lower[half : half + half // 2, :half]
    out_ref[half:, half:] = lower[half + half // 2 :, :half]


def solve_kernel(inverse_ref, pivot_rows_ref, x_ref):
    half = pivot_rows_ref.shape[0] // 2
    quarter = jnp.concatenate([inverse_ref[half:, :half], inverse_ref[half:, half:]], axis=0)
    first = dot_full(inverse_ref[:half, :half], pivot_rows_ref[:half, :])
    x_ref[:half, :] = first
    x_ref[half:, :] = dot_full(inverse_ref[:half, half:], pivot_rows_ref[half:, :] - dot_full(quarter, first))


def product(pieces, upper):
    high, low = zip(*(split2(piece) for piece in pieces))
    high, low = jnp.concatenate(high, axis=0), jnp.concatenate(low, axis=0)
    upper_high, upper_low = upper
    width = upper_high.shape[1]

    def dot(a, b):
        return lax.dot_general(a, b, (((0,), (0,)), ((), ())), preferred_element_type=F32)

    both = dot(high, jnp.concatenate([upper_high, upper_low], axis=1))
    return both[:, :width] + (both[:, width:] + dot(low, upper_high))


def piece_rows(x_ref, m, d):
    piece = x_ref.shape[0] // m
    source = jnp.bitwise_xor(lax.axis_index("pcol"), d)
    return x_ref[pl.ds(pl.multiple_of(source * piece, piece), piece), :]


def update_kernel(m, local_ref, lead_ref, x_ref, slab_ref, *refs):
    *pieces, out_ref, result, swaps, sems = refs
    tops, rests = pieces[:m], pieces[m:]
    rows = slab_ref.shape[0]
    width = x_ref.shape[0]
    blocks = rows // width
    fetch = pltpu.make_async_copy(local_ref, swaps, sems.at[blocks])
    fetch.start()
    result[:rows, :] = slab_ref[...]
    top_upper = split2(jnp.concatenate([piece_rows(x_ref, m, d) for d in top_order(m)], axis=0))
    upper = split2(jnp.concatenate([piece_rows(x_ref, m, d) for d in range(m)], axis=0))
    copies = []
    for c in range(blocks):
        part = pl.ds(c * width, width)
        if c:
            total = product([rest[:, (c - 1) * width : c * width] for rest in rests], upper)
        else:
            total = product([top[...] for top in tops], top_upper)
            fetch.wait()
            for s in range(CAP):
                result[pl.ds(swaps[0, s], 1), :] = lead_ref[pl.ds(s, 1), :]
        result[part, :] = result[part, :] - total
        if c == 0:

            @pl.when(lax.axis_index("prow") == 0)
            def _():
                result[part, :] = x_ref[...]

        copy = pltpu.make_async_copy(result.at[part], out_ref.at[part], sems.at[c])
        copy.start()
        copies.append(copy)
    for copy in copies:
        copy.wait()


def unit(held, steps, *operands):
    shapes = jax.eval_shape(steps, *operands)
    return lax.cond(held, steps, lambda *_: jax.tree.map(lambda s: jnp.zeros(s.shape, s.dtype), shapes), *operands)


def call(kernel, outs, operands, in_specs=None, out_specs=None, scratch=()):
    return pl.pallas_call(
        kernel,
        out_shape=outs,
        in_specs=in_specs or [VMEM] * len(operands),
        out_specs=out_specs or jax.tree.map(lambda _: VMEM, outs),
        scratch_shapes=list(scratch),
        compiler_params=PARAMS,
        cost_estimate=pl.CostEstimate(flops=1, bytes_accessed=1, transcendentals=0),
    )(*operands)


def local(n, m, slab, panel, pivots):
    rows, cols = slab.shape
    width = pivots.shape[0]
    piece = panel.shape[1]
    me = lax.axis_index("prow")
    panel_t = panel.T
    pivot_row = pivots.reshape(1, width)

    def exchange(block, d):
        return lax.ppermute(block, "pcol", [(c, c ^ d) for c in range(m)])

    top, rest = call(
        cut_kernel,
        (jax.ShapeDtypeStruct((piece, width), F32), jax.ShapeDtypeStruct((piece, rows - width), F32)),
        (panel_t,),
        in_specs=[pl.BlockSpec(memory_space=pl.ANY)],
        scratch=[pltpu.SemaphoreType.DMA((rows // width,))],
    )
    tops = [top] + [exchange(top, d) for d in top_order(m)[1:]]
    rests = [rest] + [exchange(rest, d) for d in range(1, m)]

    gathered, leading, local_rows = call(
        pack_kernel,
        (
            jax.ShapeDtypeStruct((CAP, cols), F32),
            jax.ShapeDtypeStruct((n * CAP, cols), F32),
            jax.ShapeDtypeStruct((1, 128), jnp.int32),
        ),
        (pivot_row, slab),
    )
    lower = call(
        functools.partial(assemble_kernel, m),
        jax.ShapeDtypeStruct((width * 3 // 4, width), F32),
        tops,
        scratch=[pltpu.VMEM((width, width), F32)],
    )

    def split(leading):
        blocks = leading.reshape(2, -1, cols)
        return blocks[0], blocks[1]

    def levels(lower, gathered, leading):
        span, other, held = n // 2, 2, lower
        while span > 1:
            moved = lax.ppermute(lower, "prow", [(r, tree_partner(r, span)) for r in range(n)])
            lower = call(
                functools.partial(pick_kernel, span),
                jax.ShapeDtypeStruct(lower.shape, F32),
                (moved, held),
            )
            kept, sent = split(leading)
            count = gathered.shape[0]
            message = jnp.concatenate([gathered, sent], axis=0)
            moved = lax.ppermute(message, "prow", [(r, r ^ other) for r in range(n)])
            moved, held = lax.optimization_barrier((moved, lower))
            gathered = jnp.concatenate([gathered, moved[:count]], axis=0)
            leading = jnp.where(me & other != 0, moved[count:], kept)
            span, other = span // 2, other * 2
        pivot_rows = call(
            functools.partial(order_kernel, n, rows),
            jax.ShapeDtypeStruct((width, cols), F32),
            (pivot_row, gathered),
            scratch=[pltpu.VMEM((n * CAP, cols), F32)],
        )
        inverse = call(
            invert_kernel,
            jax.ShapeDtypeStruct(lower.shape, F32),
            (lower,),
            scratch=[pltpu.VMEM((width, width), F32)],
        )
        moved = lax.ppermute(inverse, "prow", [(r, r ^ 1) for r in range(n)])
        inverse = jnp.where(me & 1 != 0, moved, inverse)
        return leading, call(solve_kernel, jax.ShapeDtypeStruct((width, cols), F32), (inverse, pivot_rows))

    gathered, lower = lax.optimization_barrier((gathered, lower))
    twins = [(r, r ^ 1) for r in range(n)]
    moved = lax.ppermute(gathered, "prow", twins)
    gathered = jnp.concatenate([gathered, moved], axis=0)
    kept, sent = split(leading)
    leading = jnp.where(me & 1 != 0, lax.ppermute(sent, "prow", twins), kept)
    leading, upper_rows = unit(me < n, levels, lower, gathered, leading)
    return call(
        functools.partial(update_kernel, m),
        jax.ShapeDtypeStruct((rows, cols), F32),
        (local_rows, leading, upper_rows, slab, *tops, *rests),
        in_specs=[VMEM] * (2 * m + 4),
        out_specs=pl.BlockSpec(memory_space=pl.ANY),
        scratch=[
            pltpu.VMEM((rows + 8, cols), F32),
            pltpu.SMEM((1, 128), jnp.int32),
            pltpu.SemaphoreType.DMA((rows // width + 1,)),
        ],
    )


def solution(mesh):
    return jax.shard_map(
        functools.partial(local, mesh.shape["prow"], mesh.shape["pcol"]),
        mesh=mesh,
        in_specs=(P("prow", "pcol"), P("prow", "pcol"), P()),
        out_specs=P("prow", "pcol"),
        check_vma=False,
    )
```

```python
import functools

import jax
import jax.numpy as jnp
from jax import lax
from jax.experimental import pallas as pl
from jax.experimental.pallas import tpu as pltpu
from jax.sharding import PartitionSpec as P

CAP = 32
BLOCK = 64
F32 = jnp.float32
BF16 = jnp.bfloat16
VMEM = pl.BlockSpec(memory_space=pltpu.VMEM)
PARAMS = pltpu.CompilerParams(vmem_limit_bytes=24 * 1024 * 1024)


def split3(x):
    high = x.astype(BF16)
    rest = x - high.astype(F32)
    mid = rest.astype(BF16)
    low = (rest - mid.astype(F32)).astype(BF16)
    return high, mid, low


def split2(x):
    high = x.astype(BF16)
    return high, (x - high.astype(F32)).astype(BF16)


def select_rows(one_hot, x):
    return sum(jnp.dot(one_hot, part, preferred_element_type=F32) for part in split3(x))


def dot_full(a, b):
    high, mid, low = split3(a)
    left = jnp.concatenate([low, mid, high, mid, high, high], axis=1)
    high, mid, low = split3(b)
    right = jnp.concatenate([high, mid, low, high, mid, high], axis=0)
    return jnp.dot(left, right, preferred_element_type=F32)


def tree_partner(r, span):
    if span == 1 or r % span > 1:
        return r ^ 1
    if r % 2 == 0:
        return r + 1 if r & span else r + span
    return r - span if r & span else r - 1


def lead_place(owner, n):
    bits = n.bit_length() - 1
    return sum((lax.shift_right_logical(owner, bit) & 1) * (1 << (bits - 1 - bit)) for bit in range(bits))


def slots(pivot_row, rows):
    width = pivot_row.shape[1]
    by_sublane = jnp.broadcast_to(pivot_row, (width, width)).T
    shift = rows.bit_length() - 1
    owner_row = jnp.broadcast_to(lax.shift_right_logical(pivot_row, shift), (width, width))
    owner_col = lax.shift_right_logical(by_sublane, shift)
    sub = lax.broadcasted_iota(jnp.int32, (width, width), 0)
    lane = lax.broadcasted_iota(jnp.int32, (width, width), 1)
    same = owner_row == owner_col
    rank_row = jnp.sum(jnp.where(same & (sub < lane), 1, 0), axis=0, keepdims=True)
    rank_col = jnp.sum(jnp.where(same & (lane < sub), 1, 0), axis=1, keepdims=True)
    return owner_row[:1], rank_row, owner_col[:, :1], rank_col


def pack_kernel(pivot_ref, slab_ref, packed_ref, lead_ref, local_ref):
    rows = slab_ref.shape[0]
    width = pivot_ref.shape[1]
    count = lead_ref.shape[0]
    lanes = local_ref.shape[1]
    me = lax.axis_index("prow")
    pivot_row = pivot_ref[...]
    owner_row, rank_row, owner_col, rank_col = slots(pivot_row, rows)
    pivot_col = jnp.broadcast_to(pivot_row, (lanes, width)).T
    slot = lax.broadcasted_iota(jnp.int32, (width, lanes), 1)
    mine = (owner_col == me) & (rank_col == slot)
    local = jnp.sum(jnp.where(mine, pivot_col - (me + 1) * rows, 0), axis=0, keepdims=True) + rows
    local_ref[...] = local
    slot = lax.broadcasted_iota(jnp.int32, (CAP, width), 0)
    mine = (owner_row == me) & (rank_row == slot)
    local = jnp.sum(jnp.where(mine, pivot_row - (me + 1) * rows, 0), axis=1, keepdims=True) + rows
    one_hot = (lax.broadcasted_iota(jnp.int32, (CAP, rows), 1) == local).astype(F32).astype(BF16)
    packed_ref[...] = select_rows(one_hot, slab_ref[...])
    slot = lax.broadcasted_iota(jnp.int32, (count, width), 0)
    one_hot = (slot == lead_place(owner_row, count // CAP) * CAP + rank_row).astype(F32).astype(BF16)
    lead_ref[...] = select_rows(one_hot, slab_ref[:width, :])


def block_inverses(lower):
    width = lower.shape[0]
    lane = lax.broadcasted_iota(jnp.int32, (BLOCK, width), 1)
    sub = lax.broadcasted_iota(jnp.int32, (BLOCK, width), 0)
    block = lane // BLOCK
    within = lane % BLOCK
    diag = jnp.zeros((BLOCK, width), F32)
    for b in range(width // BLOCK):
        diag = jnp.where(block == b, lower[b * BLOCK : (b + 1) * BLOCK], diag)
    diag = jnp.where(within < sub, diag, 0.0)
    inv = jnp.where(within == sub, 1.0, 0.0).astype(F32)
    half, tile = 128, 8
    first = (lax.broadcasted_iota(jnp.int32, (tile, half), 1) // BLOCK) * BLOCK
    starts = range(0, width, half)
    tops = range(0, BLOCK, tile)
    d = [[diag[t : t + tile, h : h + half] for t in tops] for h in starts]
    x = [[inv[t : t + tile, h : h + half] for t in tops] for h in starts]
    for k in range(BLOCK - 1):
        for h in range(len(starts)):
            row = x[h][k // tile][k % tile : k % tile + 1, :]
            for t in range((k + 1) // tile, len(tops)):
                column = jnp.take_along_axis(d[h][t], first + k, axis=1)
                x[h][t] = x[h][t] - column * row
    return [jnp.concatenate(tiles, axis=0) for tiles in x]


def order_kernel(n, rows, pivot_ref, gathered_ref, out_ref, gathered):
    width = pivot_ref.shape[1]
    me = lax.axis_index("prow")
    for q in range(n):
        source = jnp.bitwise_xor(me, q)
        gathered[pl.ds(pl.multiple_of(source * CAP, CAP), CAP), :] = gathered_ref[q * CAP : (q + 1) * CAP, :]
    _, _, owner_col, rank_col = slots(pivot_ref[...], rows)
    slot = lax.broadcasted_iota(jnp.int32, (width, gathered.shape[0]), 1)
    one_hot = (slot == owner_col * CAP + rank_col).astype(F32).astype(BF16)
    out_ref[...] = select_rows(one_hot, gathered[...])


def top_order(m):
    return [0, 1, *range(m - 1, 1, -1)]


def cut_kernel(panel_ref, top_ref, rest_ref, sems):
    width = top_ref.shape[1]
    copies = []
    for c in range(sems.shape[0]):
        target = rest_ref.at[:, pl.ds((c - 1) * width, width)] if c else top_ref
        copies.append(pltpu.make_async_copy(panel_ref.at[:, pl.ds(c * width, width)], target, sems.at[c]))
        copies[-1].start()
    for copy in copies:
        copy.wait()


def assemble_kernel(m, *refs):
    *pieces, out_ref, lower_t = refs
    width = lower_t.shape[0]
    piece = width // m
    half = width // 2
    z = lax.axis_index("pcol")
    for d, ref in zip(top_order(m), pieces):
        lower_t[pl.ds(pl.multiple_of(jnp.bitwise_xor(z, d) * piece, piece), piece), :] = ref[...]
    out_ref[:half, :] = lower_t[:half, :]
    out_ref[half:, :half] = lower_t[half : half + half // 2, half:]
    out_ref[half:, half:] = lower_t[half + half // 2 :, half:]


def pick_kernel(span, moved_ref, held_ref, out_ref):
    child = lax.rem(lax.axis_index("prow"), 2 * span) == span

    @pl.when(child)
    def _():
        out_ref[...] = moved_ref[...]

    @pl.when(jnp.logical_not(child))
    def _():
        out_ref[...] = held_ref[...]


def invert_kernel(lower_ref, out_ref, lower_t):
    width = lower_t.shape[0]
    half = width // 2
    lower_t[:half, :] = lower_ref[:half, :]
    lower_t[half:, :half] = jnp.zeros((half, half), F32)
    lower_t[half : half + half // 2, half:] = lower_ref[half:, :half]
    lower_t[half + half // 2 :, half:] = lower_ref[half:, half:]
    lower = lower_t[...].T
    blocks = block_inverses(lower)
    row = lax.broadcasted_iota(jnp.int32, (half, half), 0)
    col = lax.broadcasted_iota(jnp.int32, (half, half), 1)
    for h, strip in enumerate(blocks):
        corner = lower[h * half : (h + 1) * half, h * half : (h + 1) * half]
        inv = jnp.where(row // BLOCK == col // BLOCK, jnp.concatenate([strip] * (half // BLOCK), axis=0), 0.0)
        size = BLOCK
        while size < half:
            off = (row // (2 * size) == col // (2 * size)) & (row // size > col // size)
            inv = inv - dot_full(dot_full(inv, jnp.where(off, corner, 0.0)), inv)
            size *= 2
        out_ref[:half, h * half : (h + 1) * half] = inv
    out_ref[half:, :half] = lower[half : half + half // 2, :half]
    out_ref[half:, half:] = lower[half + half // 2 :, :half]


def solve_kernel(inverse_ref, pivot_rows_ref, x_ref):
    half = pivot_rows_ref.shape[0] // 2
    quarter = jnp.concatenate([inverse_ref[half:, :half], inverse_ref[half:, half:]], axis=0)
    first = dot_full(inverse_ref[:half, :half], pivot_rows_ref[:half, :])
    x_ref[:half, :] = first
    x_ref[half:, :] = dot_full(inverse_ref[:half, half:], pivot_rows_ref[half:, :] - dot_full(quarter, first))


def product(pieces, upper):
    high, low = zip(*(split2(piece) for piece in pieces))
    high, low = jnp.concatenate(high, axis=0), jnp.concatenate(low, axis=0)
    upper_high, upper_low = upper
    width = upper_high.shape[1]

    def dot(a, b):
        return lax.dot_general(a, b, (((0,), (0,)), ((), ())), preferred_element_type=F32)

    both = dot(high, jnp.concatenate([upper_high, upper_low], axis=1))
    return both[:, :width] + (both[:, width:] + dot(low, upper_high))


def piece_rows(x_ref, m, d):
    piece = x_ref.shape[0] // m
    source = jnp.bitwise_xor(lax.axis_index("pcol"), d)
    return x_ref[pl.ds(pl.multiple_of(source * piece, piece), piece), :]


def update_kernel(m, local_ref, lead_ref, x_ref, slab_ref, *refs):
    *pieces, out_ref, result, swaps, sems = refs
    tops, rests = pieces[:m], pieces[m:]
    rows = slab_ref.shape[0]
    width = x_ref.shape[0]
    blocks = rows // width
    fetch = pltpu.make_async_copy(local_ref, swaps, sems.at[blocks])
    fetch.start()
    result[:rows, :] = slab_ref[...]
    top_upper = split2(jnp.concatenate([piece_rows(x_ref, m, d) for d in top_order(m)], axis=0))
    upper = split2(jnp.concatenate([piece_rows(x_ref, m, d) for d in range(m)], axis=0))
    copies = []
    for c in range(blocks):
        part = pl.ds(c * width, width)
        if c:
            total = product([rest[:, (c - 1) * width : c * width] for rest in rests], upper)
        else:
            total = product([top[...] for top in tops], top_upper)
            fetch.wait()
            for s in range(CAP):
                result[pl.ds(swaps[0, s], 1), :] = lead_ref[pl.ds(s, 1), :]
        result[part, :] = result[part, :] - total
        if c == 0:

            @pl.when(lax.axis_index("prow") == 0)
            def _():
                result[part, :] = x_ref[...]

        copy = pltpu.make_async_copy(result.at[part], out_ref.at[part], sems.at[c])
        copy.start()
        copies.append(copy)
    for copy in copies:
        copy.wait()


def unit(held, steps, *operands):
    shapes = jax.eval_shape(steps, *operands)
    return lax.cond(held, steps, lambda *_: jax.tree.map(lambda s: jnp.zeros(s.shape, s.dtype), shapes), *operands)


def call(kernel, outs, operands, in_specs=None, out_specs=None, scratch=()):
    return pl.pallas_call(
        kernel,
        out_shape=outs,
        in_specs=in_specs or [VMEM] * len(operands),
        out_specs=out_specs or jax.tree.map(lambda _: VMEM, outs),
        scratch_shapes=list(scratch),
        compiler_params=PARAMS,
        cost_estimate=pl.CostEstimate(flops=1, bytes_accessed=1, transcendentals=0),
    )(*operands)


def local(n, m, slab, panel, pivots):
    rows, cols = slab.shape
    width = pivots.shape[0]
    piece = panel.shape[1]
    me = lax.axis_index("prow")
    panel_t = panel.T
    pivot_row = pivots.reshape(1, width)

    def exchange(block, d):
        return lax.ppermute(block, "pcol", [(c, c ^ d) for c in range(m)])

    top, rest = call(
        cut_kernel,
        (jax.ShapeDtypeStruct((piece, width), F32), jax.ShapeDtypeStruct((piece, rows - width), F32)),
        (panel_t,),
        in_specs=[pl.BlockSpec(memory_space=pl.ANY)],
        scratch=[pltpu.SemaphoreType.DMA((rows // width,))],
    )
    tops = [top] + [exchange(top, d) for d in top_order(m)[1:]]
    rests = [rest] + [exchange(rest, d) for d in range(1, m)]

    gathered, leading, local_rows = call(
        pack_kernel,
        (
            jax.ShapeDtypeStruct((CAP, cols), F32),
            jax.ShapeDtypeStruct((n * CAP, cols), F32),
            jax.ShapeDtypeStruct((1, 128), jnp.int32),
        ),
        (pivot_row, slab),
    )
    lower = call(
        functools.partial(assemble_kernel, m),
        jax.ShapeDtypeStruct((width * 3 // 4, width), F32),
        tops,
        scratch=[pltpu.VMEM((width, width), F32)],
    )

    def split(leading):
        blocks = leading.reshape(2, -1, cols)
        return blocks[0], blocks[1]

    def levels(lower, gathered, leading):
        span, other, held = n // 2, 2, lower
        while span > 1:
            moved = lax.ppermute(lower, "prow", [(r, tree_partner(r, span)) for r in range(n)])
            lower = call(
                functools.partial(pick_kernel, span),
                jax.ShapeDtypeStruct(lower.shape, F32),
                (moved, held),
            )
            kept, sent = split(leading)
            count = gathered.shape[0]
            message = jnp.concatenate([gathered, sent], axis=0)
            moved = lax.ppermute(message, "prow", [(r, r ^ other) for r in range(n)])
            moved, held = lax.optimization_barrier((moved, lower))
            gathered = jnp.concatenate([gathered, moved[:count]], axis=0)
            leading = jnp.where(me & other != 0, moved[count:], kept)
            span, other = span // 2, other * 2
        pivot_rows = call(
            functools.partial(order_kernel, n, rows),
            jax.ShapeDtypeStruct((width, cols), F32),
            (pivot_row, gathered),
            scratch=[pltpu.VMEM((n * CAP, cols), F32)],
        )
        inverse = call(
            invert_kernel,
            jax.ShapeDtypeStruct(lower.shape, F32),
            (lower,),
            scratch=[pltpu.VMEM((width, width), F32)],
        )
        moved = lax.ppermute(inverse, "prow", [(r, r ^ 1) for r in range(n)])
        inverse = jnp.where(me & 1 != 0, moved, inverse)
        return leading, call(solve_kernel, jax.ShapeDtypeStruct((width, cols), F32), (inverse, pivot_rows))

    gathered, lower = lax.optimization_barrier((gathered, lower))
    twins = [(r, r ^ 1) for r in range(n)]
    moved = lax.ppermute(gathered, "prow", twins)
    gathered = jnp.concatenate([gathered, moved], axis=0)
    kept, sent = split(leading)
    leading = jnp.where(me & 1 != 0, lax.ppermute(sent, "prow", twins), kept)
    leading, upper_rows = unit(me < n, levels, lower, gathered, leading)
    return call(
        functools.partial(update_kernel, m),
        jax.ShapeDtypeStruct((rows, cols), F32),
        (local_rows, leading, upper_rows, slab, *tops, *rests),
        in_specs=[VMEM] * (2 * m + 4),
        out_specs=pl.BlockSpec(memory_space=pl.ANY),
        scratch=[
            pltpu.VMEM((rows + 8, cols), F32),
            pltpu.SMEM((1, 128), jnp.int32),
            pltpu.SemaphoreType.DMA((rows // width + 1,)),
        ],
    )


def solution(mesh):
    return jax.shard_map(
        functools.partial(local, mesh.shape["prow"], mesh.shape["pcol"]),
        mesh=mesh,
        in_specs=(P("prow", "pcol"), P("prow", "pcol"), P()),
        out_specs=P("prow", "pcol"),
        check_vma=False,
    )
```

```python
import functools

import jax
import jax.numpy as jnp
from jax import lax
from jax.experimental import pallas as pl
from jax.experimental.pallas import tpu as pltpu
from jax.sharding import PartitionSpec as P

CAP = 32
BLOCK = 32
F32 = jnp.float32
BF16 = jnp.bfloat16
VMEM = pl.BlockSpec(memory_space=pltpu.VMEM)
PARAMS = pltpu.CompilerParams(vmem_limit_bytes=24 * 1024 * 1024)


def split3(x):
    high = x.astype(BF16)
    rest = x - high.astype(F32)
    mid = rest.astype(BF16)
    low = (rest - mid.astype(F32)).astype(BF16)
    return high, mid, low


def split2(x):
    high = x.astype(BF16)
    return high, (x - high.astype(F32)).astype(BF16)


def select_rows(one_hot, x):
    return sum(jnp.dot(one_hot, part, preferred_element_type=F32) for part in split3(x))


def dot_full(a, b):
    high, mid, low = split3(a)
    left = jnp.concatenate([low, mid, high, mid, high, high], axis=1)
    high, mid, low = split3(b)
    right = jnp.concatenate([high, mid, low, high, mid, high], axis=0)
    return jnp.dot(left, right, preferred_element_type=F32)


def tree_partner(r, span):
    if span == 1 or r % span > 1:
        return r ^ 1
    if r % 2 == 0:
        return r + 1 if r & span else r + span
    return r - span if r & span else r - 1


def lead_place(owner, n):
    bits = n.bit_length() - 1
    return sum((lax.shift_right_logical(owner, bit) & 1) * (1 << (bits - 1 - bit)) for bit in range(bits))


def slots(pivot_row, rows):
    width = pivot_row.shape[1]
    by_sublane = jnp.broadcast_to(pivot_row, (width, width)).T
    shift = rows.bit_length() - 1
    owner_row = jnp.broadcast_to(lax.shift_right_logical(pivot_row, shift), (width, width))
    owner_col = lax.shift_right_logical(by_sublane, shift)
    sub = lax.broadcasted_iota(jnp.int32, (width, width), 0)
    lane = lax.broadcasted_iota(jnp.int32, (width, width), 1)
    same = owner_row == owner_col
    rank_row = jnp.sum(jnp.where(same & (sub < lane), 1, 0), axis=0, keepdims=True)
    rank_col = jnp.sum(jnp.where(same & (lane < sub), 1, 0), axis=1, keepdims=True)
    return owner_row[:1], rank_row, owner_col[:, :1], rank_col


def pack_kernel(pivot_ref, slab_ref, packed_ref, lead_ref, local_ref):
    rows = slab_ref.shape[0]
    width = pivot_ref.shape[1]
    count = lead_ref.shape[0]
    lanes = local_ref.shape[1]
    me = lax.axis_index("prow")
    pivot_row = pivot_ref[...]
    owner_row, rank_row, owner_col, rank_col = slots(pivot_row, rows)
    pivot_col = jnp.broadcast_to(pivot_row, (lanes, width)).T
    slot = lax.broadcasted_iota(jnp.int32, (width, lanes), 1)
    mine = (owner_col == me) & (rank_col == slot)
    local = jnp.sum(jnp.where(mine, pivot_col - (me + 1) * rows, 0), axis=0, keepdims=True) + rows
    local_ref[...] = local
    slot = lax.broadcasted_iota(jnp.int32, (CAP, width), 0)
    mine = (owner_row == me) & (rank_row == slot)
    local = jnp.sum(jnp.where(mine, pivot_row - (me + 1) * rows, 0), axis=1, keepdims=True) + rows
    one_hot = (lax.broadcasted_iota(jnp.int32, (CAP, rows), 1) == local).astype(F32).astype(BF16)
    packed_ref[...] = select_rows(one_hot, slab_ref[...])
    slot = lax.broadcasted_iota(jnp.int32, (count, width), 0)
    one_hot = (slot == lead_place(owner_row, count // CAP) * CAP + rank_row).astype(F32).astype(BF16)
    lead_ref[...] = select_rows(one_hot, slab_ref[:width, :])


def block_inverses(lower):
    width = lower.shape[0]
    lane = lax.broadcasted_iota(jnp.int32, (BLOCK, width), 1)
    sub = lax.broadcasted_iota(jnp.int32, (BLOCK, width), 0)
    block = lane // BLOCK
    within = lane % BLOCK
    diag = jnp.zeros((BLOCK, width), F32)
    for b in range(width // BLOCK):
        diag = jnp.where(block == b, lower[b * BLOCK : (b + 1) * BLOCK], diag)
    diag = jnp.where(within < sub, diag, 0.0)
    inv = jnp.where(within == sub, 1.0, 0.0).astype(F32)
    half = 128
    first = (lax.broadcasted_iota(jnp.int32, (BLOCK, half), 1) // BLOCK) * BLOCK
    outs = []
    for h in range(0, width, half):
        d, x = diag[:, h : h + half], inv[:, h : h + half]
        for k in range(BLOCK - 1):
            column = jnp.take_along_axis(d, first + k, axis=1)
            x = x - column * x[k : k + 1, :]
        outs.append(x)
    return outs


def order_kernel(n, rows, pivot_ref, gathered_ref, out_ref, gathered):
    width = pivot_ref.shape[1]
    me = lax.axis_index("prow")
    for q in range(n):
        source = jnp.bitwise_xor(me, q)
        gathered[pl.ds(pl.multiple_of(source * CAP, CAP), CAP), :] = gathered_ref[q * CAP : (q + 1) * CAP, :]
    _, _, owner_col, rank_col = slots(pivot_ref[...], rows)
    slot = lax.broadcasted_iota(jnp.int32, (width, gathered.shape[0]), 1)
    one_hot = (slot == owner_col * CAP + rank_col).astype(F32).astype(BF16)
    out_ref[...] = select_rows(one_hot, gathered[...])


def top_order(m):
    return [0, 1, *range(m - 1, 1, -1)]


def cut_kernel(panel_ref, top_ref, rest_ref, sems):
    width = top_ref.shape[1]
    copies = []
    for c in range(sems.shape[0]):
        target = rest_ref.at[:, pl.ds((c - 1) * width, width)] if c else top_ref
        copies.append(pltpu.make_async_copy(panel_ref.at[:, pl.ds(c * width, width)], target, sems.at[c]))
        copies[-1].start()
    for copy in copies:
        copy.wait()


def assemble_kernel(m, *refs):
    *pieces, out_ref, lower_t = refs
    width = lower_t.shape[0]
    piece = width // m
    half = width // 2
    z = lax.axis_index("pcol")
    for d, ref in zip(top_order(m), pieces):
        lower_t[pl.ds(pl.multiple_of(jnp.bitwise_xor(z, d) * piece, piece), piece), :] = ref[...]
    out_ref[:half, :] = lower_t[:half, :]
    out_ref[half:, :half] = lower_t[half : half + half // 2, half:]
    out_ref[half:, half:] = lower_t[half + half // 2 :, half:]


def pick_kernel(span, moved_ref, held_ref, out_ref):
    child = lax.rem(lax.axis_index("prow"), 2 * span) == span

    @pl.when(child)
    def _():
        out_ref[...] = moved_ref[...]

    @pl.when(jnp.logical_not(child))
    def _():
        out_ref[...] = held_ref[...]


def invert_kernel(lower_ref, out_ref, lower_t):
    holds = lax.axis_index("prow") & 1 == 0

    @pl.when(jnp.logical_not(holds))
    def _():
        out_ref[...] = jnp.zeros_like(out_ref)

    @pl.when(holds)
    def _():
        width = lower_t.shape[0]
        half = width // 2
        lower_t[:half, :] = lower_ref[:half, :]
        lower_t[half:, :half] = jnp.zeros((half, half), F32)
        lower_t[half : half + half // 2, half:] = lower_ref[half:, :half]
        lower_t[half + half // 2 :, half:] = lower_ref[half:, half:]
        lower = lower_t[...].T
        blocks = block_inverses(lower)
        row = lax.broadcasted_iota(jnp.int32, (half, half), 0)
        col = lax.broadcasted_iota(jnp.int32, (half, half), 1)
        for h, strip in enumerate(blocks):
            corner = lower[h * half : (h + 1) * half, h * half : (h + 1) * half]
            inv = jnp.where(row // BLOCK == col // BLOCK, jnp.concatenate([strip] * (half // BLOCK), axis=0), 0.0)
            size = BLOCK
            while size < half:
                off = (row // (2 * size) == col // (2 * size)) & (row // size > col // size)
                inv = inv - dot_full(dot_full(inv, jnp.where(off, corner, 0.0)), inv)
                size *= 2
            out_ref[:half, h * half : (h + 1) * half] = inv
        out_ref[half:, :half] = lower[half : half + half // 2, :half]
        out_ref[half:, half:] = lower[half + half // 2 :, :half]


def solve_kernel(inverse_ref, pivot_rows_ref, x_ref):
    half = pivot_rows_ref.shape[0] // 2
    quarter = jnp.concatenate([inverse_ref[half:, :half], inverse_ref[half:, half:]], axis=0)
    first = dot_full(inverse_ref[:half, :half], pivot_rows_ref[:half, :])
    x_ref[:half, :] = first
    x_ref[half:, :] = dot_full(inverse_ref[:half, half:], pivot_rows_ref[half:, :] - dot_full(quarter, first))


def product(pieces, upper):
    high, low = zip(*(split2(piece) for piece in pieces))
    high, low = jnp.concatenate(high, axis=0), jnp.concatenate(low, axis=0)
    upper_high, upper_low = upper
    width = upper_high.shape[1]

    def dot(a, b):
        return lax.dot_general(a, b, (((0,), (0,)), ((), ())), preferred_element_type=F32)

    both = dot(high, jnp.concatenate([upper_high, upper_low], axis=1))
    return both[:, :width] + (both[:, width:] + dot(low, upper_high))


def piece_rows(x_ref, m, d):
    piece = x_ref.shape[0] // m
    source = jnp.bitwise_xor(lax.axis_index("pcol"), d)
    return x_ref[pl.ds(pl.multiple_of(source * piece, piece), piece), :]


def update_kernel(m, local_ref, lead_ref, x_ref, slab_ref, *refs):
    *pieces, out_ref, result, swaps, sems = refs
    tops, rests = pieces[:m], pieces[m:]
    rows = slab_ref.shape[0]
    width = x_ref.shape[0]
    blocks = rows // width
    fetch = pltpu.make_async_copy(local_ref, swaps, sems.at[blocks])
    fetch.start()
    result[:rows, :] = slab_ref[...]
    top_upper = split2(jnp.concatenate([piece_rows(x_ref, m, d) for d in top_order(m)], axis=0))
    upper = split2(jnp.concatenate([piece_rows(x_ref, m, d) for d in range(m)], axis=0))
    copies = []
    for c in range(blocks):
        part = pl.ds(c * width, width)
        if c:
            total = product([rest[:, (c - 1) * width : c * width] for rest in rests], upper)
        else:
            total = product([top[...] for top in tops], top_upper)
            fetch.wait()
            for s in range(CAP):
                result[pl.ds(swaps[0, s], 1), :] = lead_ref[pl.ds(s, 1), :]
        result[part, :] = result[part, :] - total
        if c == 0:

            @pl.when(lax.axis_index("prow") == 0)
            def _():
                result[part, :] = x_ref[...]

        copy = pltpu.make_async_copy(result.at[part], out_ref.at[part], sems.at[c])
        copy.start()
        copies.append(copy)
    for copy in copies:
        copy.wait()


def unit(held, steps, *operands):
    shapes = jax.eval_shape(steps, *operands)
    return lax.cond(held, steps, lambda *_: jax.tree.map(lambda s: jnp.zeros(s.shape, s.dtype), shapes), *operands)


def call(kernel, outs, operands, in_specs=None, out_specs=None, scratch=()):
    return pl.pallas_call(
        kernel,
        out_shape=outs,
        in_specs=in_specs or [VMEM] * len(operands),
        out_specs=out_specs or jax.tree.map(lambda _: VMEM, outs),
        scratch_shapes=list(scratch),
        compiler_params=PARAMS,
        cost_estimate=pl.CostEstimate(flops=1, bytes_accessed=1, transcendentals=0),
    )(*operands)


def local(n, m, slab, panel, pivots):
    rows, cols = slab.shape
    width = pivots.shape[0]
    piece = panel.shape[1]
    me = lax.axis_index("prow")
    panel_t = panel.T
    pivot_row = pivots.reshape(1, width)

    def exchange(block, d):
        return lax.ppermute(block, "pcol", [(c, c ^ d) for c in range(m)])

    top, rest = call(
        cut_kernel,
        (jax.ShapeDtypeStruct((piece, width), F32), jax.ShapeDtypeStruct((piece, rows - width), F32)),
        (panel_t,),
        in_specs=[pl.BlockSpec(memory_space=pl.ANY)],
        scratch=[pltpu.SemaphoreType.DMA((rows // width,))],
    )
    tops = [top] + [exchange(top, d) for d in top_order(m)[1:]]
    rests = [rest] + [exchange(rest, d) for d in range(1, m)]

    gathered, leading, local_rows = call(
        pack_kernel,
        (
            jax.ShapeDtypeStruct((CAP, cols), F32),
            jax.ShapeDtypeStruct((n * CAP, cols), F32),
            jax.ShapeDtypeStruct((1, 128), jnp.int32),
        ),
        (pivot_row, slab),
    )
    lower = call(
        functools.partial(assemble_kernel, m),
        jax.ShapeDtypeStruct((width * 3 // 4, width), F32),
        tops,
        scratch=[pltpu.VMEM((width, width), F32)],
    )

    def split(leading):
        blocks = leading.reshape(2, -1, cols)
        return blocks[0], blocks[1]

    def levels(lower, gathered, leading):
        span, other, held = n // 2, 2, lower
        while span > 1:
            moved = lax.ppermute(lower, "prow", [(r, tree_partner(r, span)) for r in range(n)])
            lower = call(
                functools.partial(pick_kernel, span),
                jax.ShapeDtypeStruct(lower.shape, F32),
                (moved, held),
            )
            kept, sent = split(leading)
            count = gathered.shape[0]
            message = jnp.concatenate([gathered, sent], axis=0)
            moved = lax.ppermute(message, "prow", [(r, r ^ other) for r in range(n)])
            moved, held = lax.optimization_barrier((moved, lower))
            gathered = jnp.concatenate([gathered, moved[:count]], axis=0)
            leading = jnp.where(me & other != 0, moved[count:], kept)
            span, other = span // 2, other * 2
        pivot_rows = call(
            functools.partial(order_kernel, n, rows),
            jax.ShapeDtypeStruct((width, cols), F32),
            (pivot_row, gathered),
            scratch=[pltpu.VMEM((n * CAP, cols), F32)],
        )
        inverse = call(
            invert_kernel,
            jax.ShapeDtypeStruct(lower.shape, F32),
            (lower,),
            scratch=[pltpu.VMEM((width, width), F32)],
        )
        moved = lax.ppermute(inverse, "prow", [(r, r ^ 1) for r in range(n)])
        inverse = jnp.where(me & 1 != 0, moved, inverse)
        return leading, call(solve_kernel, jax.ShapeDtypeStruct((width, cols), F32), (inverse, pivot_rows))

    gathered, lower = lax.optimization_barrier((gathered, lower))
    twins = [(r, r ^ 1) for r in range(n)]
    moved = lax.ppermute(gathered, "prow", twins)
    gathered = jnp.concatenate([gathered, moved], axis=0)
    kept, sent = split(leading)
    leading = jnp.where(me & 1 != 0, lax.ppermute(sent, "prow", twins), kept)
    leading, upper_rows = unit(me < n, levels, lower, gathered, leading)
    return call(
        functools.partial(update_kernel, m),
        jax.ShapeDtypeStruct((rows, cols), F32),
        (local_rows, leading, upper_rows, slab, *tops, *rests),
        in_specs=[VMEM] * (2 * m + 4),
        out_specs=pl.BlockSpec(memory_space=pl.ANY),
        scratch=[
            pltpu.VMEM((rows + 8, cols), F32),
            pltpu.SMEM((1, 128), jnp.int32),
            pltpu.SemaphoreType.DMA((rows // width + 1,)),
        ],
    )


def solution(mesh):
    return jax.shard_map(
        functools.partial(local, mesh.shape["prow"], mesh.shape["pcol"]),
        mesh=mesh,
        in_specs=(P("prow", "pcol"), P("prow", "pcol"), P()),
        out_specs=P("prow", "pcol"),
        check_vma=False,
    )
```

```python
import functools

import jax
import jax.numpy as jnp
from jax import lax
from jax.experimental import pallas as pl
from jax.experimental.pallas import tpu as pltpu
from jax.sharding import PartitionSpec as P

CAP = 32
BLOCK = 32
F32 = jnp.float32
BF16 = jnp.bfloat16
VMEM = pl.BlockSpec(memory_space=pltpu.VMEM)
PARAMS = pltpu.CompilerParams(vmem_limit_bytes=24 * 1024 * 1024)


def split3(x):
    high = x.astype(BF16)
    rest = x - high.astype(F32)
    mid = rest.astype(BF16)
    low = (rest - mid.astype(F32)).astype(BF16)
    return high, mid, low


def split2(x):
    high = x.astype(BF16)
    return high, (x - high.astype(F32)).astype(BF16)


def select_rows(one_hot, x):
    return sum(jnp.dot(one_hot, part, preferred_element_type=F32) for part in split3(x))


def dot_full(a, b):
    high, mid, low = split3(a)
    left = jnp.concatenate([low, mid, high, mid, high, high], axis=1)
    high, mid, low = split3(b)
    right = jnp.concatenate([high, mid, low, high, mid, high], axis=0)
    return jnp.dot(left, right, preferred_element_type=F32)


def tree_partner(r, span):
    if span == 1 or r % span > 1:
        return r ^ 1
    if r % 2 == 0:
        return r + 1 if r & span else r + span
    return r - span if r & span else r - 1


def lead_place(owner, n):
    bits = n.bit_length() - 1
    return sum((lax.shift_right_logical(owner, bit) & 1) * (1 << (bits - 1 - bit)) for bit in range(bits))


def slots(pivot_row, rows):
    width = pivot_row.shape[1]
    by_sublane = jnp.broadcast_to(pivot_row, (width, width)).T
    shift = rows.bit_length() - 1
    owner_row = jnp.broadcast_to(lax.shift_right_logical(pivot_row, shift), (width, width))
    owner_col = lax.shift_right_logical(by_sublane, shift)
    sub = lax.broadcasted_iota(jnp.int32, (width, width), 0)
    lane = lax.broadcasted_iota(jnp.int32, (width, width), 1)
    same = owner_row == owner_col
    rank_row = jnp.sum(jnp.where(same & (sub < lane), 1, 0), axis=0, keepdims=True)
    rank_col = jnp.sum(jnp.where(same & (lane < sub), 1, 0), axis=1, keepdims=True)
    return owner_row[:1], rank_row, owner_col[:, :1], rank_col


def pack_kernel(pivot_ref, slab_ref, packed_ref, lead_ref, local_ref):
    rows = slab_ref.shape[0]
    width = pivot_ref.shape[1]
    count = lead_ref.shape[0]
    lanes = local_ref.shape[1]
    me = lax.axis_index("prow")
    pivot_row = pivot_ref[...]
    owner_row, rank_row, owner_col, rank_col = slots(pivot_row, rows)
    pivot_col = jnp.broadcast_to(pivot_row, (lanes, width)).T
    slot = lax.broadcasted_iota(jnp.int32, (width, lanes), 1)
    mine = (owner_col == me) & (rank_col == slot)
    local = jnp.sum(jnp.where(mine, pivot_col - (me + 1) * rows, 0), axis=0, keepdims=True) + rows
    local_ref[...] = local
    slot = lax.broadcasted_iota(jnp.int32, (CAP, width), 0)
    mine = (owner_row == me) & (rank_row == slot)
    local = jnp.sum(jnp.where(mine, pivot_row - (me + 1) * rows, 0), axis=1, keepdims=True) + rows
    one_hot = (lax.broadcasted_iota(jnp.int32, (CAP, rows), 1) == local).astype(F32).astype(BF16)
    packed_ref[...] = select_rows(one_hot, slab_ref[...])
    slot = lax.broadcasted_iota(jnp.int32, (count, width), 0)
    one_hot = (slot == lead_place(owner_row, count // CAP) * CAP + rank_row).astype(F32).astype(BF16)
    lead_ref[...] = select_rows(one_hot, slab_ref[:width, :])


def block_inverses(lower):
    width = lower.shape[0]
    lane = lax.broadcasted_iota(jnp.int32, (BLOCK, width), 1)
    sub = lax.broadcasted_iota(jnp.int32, (BLOCK, width), 0)
    block = lane // BLOCK
    within = lane % BLOCK
    diag = jnp.zeros((BLOCK, width), F32)
    for b in range(width // BLOCK):
        diag = jnp.where(block == b, lower[b * BLOCK : (b + 1) * BLOCK], diag)
    diag = jnp.where(within < sub, diag, 0.0)
    inv = jnp.where(within == sub, 1.0, 0.0).astype(F32)
    half = 128
    first = (lax.broadcasted_iota(jnp.int32, (BLOCK, half), 1) // BLOCK) * BLOCK
    outs = []
    for h in range(0, width, half):
        d, x = diag[:, h : h + half], inv[:, h : h + half]
        for k in range(BLOCK - 1):
            column = jnp.take_along_axis(d, first + k, axis=1)
            x = x - column * x[k : k + 1, :]
        outs.append(x)
    return outs


def choice_kernel(n, rows, pivot_ref, out_ref):
    _, _, owner_col, rank_col = slots(pivot_ref[...], rows)
    place = jnp.bitwise_xor(owner_col, lax.axis_index("prow")) * CAP + rank_col
    out_ref[...] = (lax.broadcasted_iota(jnp.int32, out_ref.shape, 1) == place).astype(F32).astype(BF16)


def order_kernel(choice_ref, gathered_ref, out_ref):
    out_ref[...] = select_rows(choice_ref[...], gathered_ref[...])


def top_order(m):
    return [0, 1, *range(m - 1, 1, -1)]


def cut_kernel(panel_ref, top_ref, rest_ref, sems):
    width = top_ref.shape[1]
    copies = []
    for c in range(sems.shape[0]):
        target = rest_ref.at[:, pl.ds((c - 1) * width, width)] if c else top_ref
        copies.append(pltpu.make_async_copy(panel_ref.at[:, pl.ds(c * width, width)], target, sems.at[c]))
        copies[-1].start()
    for copy in copies:
        copy.wait()


def assemble_kernel(m, *refs):
    *pieces, out_ref, lower_t = refs
    width = lower_t.shape[0]
    piece = width // m
    half = width // 2
    z = lax.axis_index("pcol")
    for d, ref in zip(top_order(m), pieces):
        lower_t[pl.ds(pl.multiple_of(jnp.bitwise_xor(z, d) * piece, piece), piece), :] = ref[...]
    out_ref[:half, :] = lower_t[:half, :]
    out_ref[half:, :half] = lower_t[half : half + half // 2, half:]
    out_ref[half:, half:] = lower_t[half + half // 2 :, half:]


def pick_kernel(span, moved_ref, held_ref, out_ref):
    child = lax.rem(lax.axis_index("prow"), 2 * span) == span

    @pl.when(child)
    def _():
        out_ref[...] = moved_ref[...]

    @pl.when(jnp.logical_not(child))
    def _():
        out_ref[...] = held_ref[...]


def invert_kernel(lower_ref, out_ref, lower_t):
    holds = lax.axis_index("prow") & 1 == 0

    @pl.when(jnp.logical_not(holds))
    def _():
        out_ref[...] = jnp.zeros_like(out_ref)

    @pl.when(holds)
    def _():
        width = lower_t.shape[0]
        half = width // 2
        lower_t[:half, :] = lower_ref[:half, :]
        lower_t[half:, :half] = jnp.zeros((half, half), F32)
        lower_t[half : half + half // 2, half:] = lower_ref[half:, :half]
        lower_t[half + half // 2 :, half:] = lower_ref[half:, half:]
        lower = lower_t[...].T
        blocks = block_inverses(lower)
        row = lax.broadcasted_iota(jnp.int32, (half, half), 0)
        col = lax.broadcasted_iota(jnp.int32, (half, half), 1)
        for h, strip in enumerate(blocks):
            corner = lower[h * half : (h + 1) * half, h * half : (h + 1) * half]
            inv = jnp.where(row // BLOCK == col // BLOCK, jnp.concatenate([strip] * (half // BLOCK), axis=0), 0.0)
            size = BLOCK
            while size < half:
                off = (row // (2 * size) == col // (2 * size)) & (row // size > col // size)
                inv = inv - dot_full(dot_full(inv, jnp.where(off, corner, 0.0)), inv)
                size *= 2
            out_ref[:half, h * half : (h + 1) * half] = inv
        out_ref[half:, :half] = lower[half : half + half // 2, :half]
        out_ref[half:, half:] = lower[half + half // 2 :, :half]


def solve_kernel(inverse_ref, pivot_rows_ref, x_ref):
    half = pivot_rows_ref.shape[0] // 2
    quarter = jnp.concatenate([inverse_ref[half:, :half], inverse_ref[half:, half:]], axis=0)
    first = dot_full(inverse_ref[:half, :half], pivot_rows_ref[:half, :])
    x_ref[:half, :] = first
    x_ref[half:, :] = dot_full(inverse_ref[:half, half:], pivot_rows_ref[half:, :] - dot_full(quarter, first))


def product(pieces, upper):
    high, low = zip(*(split2(piece) for piece in pieces))
    high, low = jnp.concatenate(high, axis=0), jnp.concatenate(low, axis=0)
    upper_high, upper_low = upper
    width = upper_high.shape[1]

    def dot(a, b):
        return lax.dot_general(a, b, (((0,), (0,)), ((), ())), preferred_element_type=F32)

    both = dot(high, jnp.concatenate([upper_high, upper_low], axis=1))
    return both[:, :width] + (both[:, width:] + dot(low, upper_high))


def piece_rows(x_ref, m, d):
    piece = x_ref.shape[0] // m
    source = jnp.bitwise_xor(lax.axis_index("pcol"), d)
    return x_ref[pl.ds(pl.multiple_of(source * piece, piece), piece), :]


def update_kernel(m, local_ref, lead_ref, x_ref, slab_ref, *refs):
    *pieces, out_ref, result, swaps, sems = refs
    tops, rests = pieces[:m], pieces[m:]
    rows = slab_ref.shape[0]
    width = x_ref.shape[0]
    blocks = rows // width
    fetch = pltpu.make_async_copy(local_ref, swaps, sems.at[blocks])
    fetch.start()
    result[:rows, :] = slab_ref[...]
    top_upper = split2(jnp.concatenate([piece_rows(x_ref, m, d) for d in top_order(m)], axis=0))
    upper = split2(jnp.concatenate([piece_rows(x_ref, m, d) for d in range(m)], axis=0))
    copies = []
    for c in range(blocks):
        part = pl.ds(c * width, width)
        if c:
            total = product([rest[:, (c - 1) * width : c * width] for rest in rests], upper)
        else:
            total = product([top[...] for top in tops], top_upper)
            fetch.wait()
            for s in range(CAP):
                result[pl.ds(swaps[0, s], 1), :] = lead_ref[pl.ds(s, 1), :]
        result[part, :] = result[part, :] - total
        if c == 0:

            @pl.when(lax.axis_index("prow") == 0)
            def _():
                result[part, :] = x_ref[...]

        copy = pltpu.make_async_copy(result.at[part], out_ref.at[part], sems.at[c])
        copy.start()
        copies.append(copy)
    for copy in copies:
        copy.wait()


def unit(held, steps, *operands):
    shapes = jax.eval_shape(steps, *operands)
    return lax.cond(held, steps, lambda *_: jax.tree.map(lambda s: jnp.zeros(s.shape, s.dtype), shapes), *operands)


def call(kernel, outs, operands, in_specs=None, out_specs=None, scratch=()):
    return pl.pallas_call(
        kernel,
        out_shape=outs,
        in_specs=in_specs or [VMEM] * len(operands),
        out_specs=out_specs or jax.tree.map(lambda _: VMEM, outs),
        scratch_shapes=list(scratch),
        compiler_params=PARAMS,
        cost_estimate=pl.CostEstimate(flops=1, bytes_accessed=1, transcendentals=0),
    )(*operands)


def local(n, m, slab, panel, pivots):
    rows, cols = slab.shape
    width = pivots.shape[0]
    piece = panel.shape[1]
    me = lax.axis_index("prow")
    panel_t = panel.T
    pivot_row = pivots.reshape(1, width)

    def exchange(block, d):
        return lax.ppermute(block, "pcol", [(c, c ^ d) for c in range(m)])

    top, rest = call(
        cut_kernel,
        (jax.ShapeDtypeStruct((piece, width), F32), jax.ShapeDtypeStruct((piece, rows - width), F32)),
        (panel_t,),
        in_specs=[pl.BlockSpec(memory_space=pl.ANY)],
        scratch=[pltpu.SemaphoreType.DMA((rows // width,))],
    )
    tops = [top] + [exchange(top, d) for d in top_order(m)[1:]]
    rests = [rest] + [exchange(rest, d) for d in range(1, m)]

    gathered, leading, local_rows = call(
        pack_kernel,
        (
            jax.ShapeDtypeStruct((CAP, cols), F32),
            jax.ShapeDtypeStruct((n * CAP, cols), F32),
            jax.ShapeDtypeStruct((1, 128), jnp.int32),
        ),
        (pivot_row, slab),
    )
    lower = call(
        functools.partial(assemble_kernel, m),
        jax.ShapeDtypeStruct((width * 3 // 4, width), F32),
        tops,
        scratch=[pltpu.VMEM((width, width), F32)],
    )

    def split(leading):
        blocks = leading.reshape(2, -1, cols)
        return blocks[0], blocks[1]

    def levels(lower, gathered, leading):
        span, other, held = n // 2, 2, lower
        while span > 1:
            moved = lax.ppermute(lower, "prow", [(r, tree_partner(r, span)) for r in range(n)])
            lower = call(
                functools.partial(pick_kernel, span),
                jax.ShapeDtypeStruct(lower.shape, F32),
                (moved, held),
            )
            kept, sent = split(leading)
            count = gathered.shape[0]
            message = jnp.concatenate([gathered, sent], axis=0)
            moved = lax.ppermute(message, "prow", [(r, r ^ other) for r in range(n)])
            moved, held = lax.optimization_barrier((moved, lower))
            gathered = jnp.concatenate([gathered, moved[:count]], axis=0)
            leading = jnp.where(me & other != 0, moved[count:], kept)
            span, other = span // 2, other * 2
        choice = call(
            functools.partial(choice_kernel, n, rows), jax.ShapeDtypeStruct((width, n * CAP), BF16), (pivot_row,)
        )
        pivot_rows = call(order_kernel, jax.ShapeDtypeStruct((width, cols), F32), (choice, gathered))
        inverse = call(
            invert_kernel,
            jax.ShapeDtypeStruct(lower.shape, F32),
            (lower,),
            scratch=[pltpu.VMEM((width, width), F32)],
        )
        moved = lax.ppermute(inverse, "prow", [(r, r ^ 1) for r in range(n)])
        inverse = jnp.where(me & 1 != 0, moved, inverse)
        return leading, call(solve_kernel, jax.ShapeDtypeStruct((width, cols), F32), (inverse, pivot_rows))

    gathered, lower = lax.optimization_barrier((gathered, lower))
    twins = [(r, r ^ 1) for r in range(n)]
    moved = lax.ppermute(gathered, "prow", twins)
    gathered = jnp.concatenate([gathered, moved], axis=0)
    kept, sent = split(leading)
    leading = jnp.where(me & 1 != 0, lax.ppermute(sent, "prow", twins), kept)
    leading, upper_rows = unit(me < n, levels, lower, gathered, leading)
    return call(
        functools.partial(update_kernel, m),
        jax.ShapeDtypeStruct((rows, cols), F32),
        (local_rows, leading, upper_rows, slab, *tops, *rests),
        in_specs=[VMEM] * (2 * m + 4),
        out_specs=pl.BlockSpec(memory_space=pl.ANY),
        scratch=[
            pltpu.VMEM((rows + 8, cols), F32),
            pltpu.SMEM((1, 128), jnp.int32),
            pltpu.SemaphoreType.DMA((rows // width + 1,)),
        ],
    )


def solution(mesh):
    return jax.shard_map(
        functools.partial(local, mesh.shape["prow"], mesh.shape["pcol"]),
        mesh=mesh,
        in_specs=(P("prow", "pcol"), P("prow", "pcol"), P()),
        out_specs=P("prow", "pcol"),
        check_vma=False,
    )
```

```python
import functools

import jax
import jax.numpy as jnp
from jax import lax
from jax.experimental import pallas as pl
from jax.experimental.pallas import tpu as pltpu
from jax.sharding import PartitionSpec as P

CAP = 32
BLOCK = 32
F32 = jnp.float32
BF16 = jnp.bfloat16
VMEM = pl.BlockSpec(memory_space=pltpu.VMEM)
PARAMS = pltpu.CompilerParams(vmem_limit_bytes=24 * 1024 * 1024)


def split3(x):
    high = x.astype(BF16)
    rest = x - high.astype(F32)
    mid = rest.astype(BF16)
    low = (rest - mid.astype(F32)).astype(BF16)
    return high, mid, low


def split2(x):
    high = x.astype(BF16)
    return high, (x - high.astype(F32)).astype(BF16)


def select_rows(one_hot, x):
    return sum(jnp.dot(one_hot, part, preferred_element_type=F32) for part in split3(x))


def dot_full(a, b):
    high, mid, low = split3(a)
    left = jnp.concatenate([low, mid, high, mid, high, high], axis=1)
    high, mid, low = split3(b)
    right = jnp.concatenate([high, mid, low, high, mid, high], axis=0)
    return jnp.dot(left, right, preferred_element_type=F32)


def tree_partner(r, span):
    if span == 1 or r % span > 1:
        return r ^ 1
    if r % 2 == 0:
        return r + 1 if r & span else r + span
    return r - span if r & span else r - 1


def lead_place(owner, n):
    bits = n.bit_length() - 1
    return sum((lax.shift_right_logical(owner, bit) & 1) * (1 << (bits - 1 - bit)) for bit in range(bits))


def slots(pivot_row, rows):
    width = pivot_row.shape[1]
    by_sublane = jnp.broadcast_to(pivot_row, (width, width)).T
    shift = rows.bit_length() - 1
    owner_row = jnp.broadcast_to(lax.shift_right_logical(pivot_row, shift), (width, width))
    owner_col = lax.shift_right_logical(by_sublane, shift)
    sub = lax.broadcasted_iota(jnp.int32, (width, width), 0)
    lane = lax.broadcasted_iota(jnp.int32, (width, width), 1)
    same = owner_row == owner_col
    rank_row = jnp.sum(jnp.where(same & (sub < lane), 1, 0), axis=0, keepdims=True)
    rank_col = jnp.sum(jnp.where(same & (lane < sub), 1, 0), axis=1, keepdims=True)
    return owner_row[:1], rank_row, owner_col[:, :1], rank_col


def pack_kernel(pivot_ref, slab_ref, packed_ref, lead_ref, local_ref):
    rows = slab_ref.shape[0]
    width = pivot_ref.shape[1]
    count = lead_ref.shape[0]
    lanes = local_ref.shape[1]
    me = lax.axis_index("prow")
    pivot_row = pivot_ref[...]
    owner_row, rank_row, owner_col, rank_col = slots(pivot_row, rows)
    pivot_col = jnp.broadcast_to(pivot_row, (lanes, width)).T
    slot = lax.broadcasted_iota(jnp.int32, (width, lanes), 1)
    mine = (owner_col == me) & (rank_col == slot)
    local = jnp.sum(jnp.where(mine, pivot_col - (me + 1) * rows, 0), axis=0, keepdims=True) + rows
    local_ref[...] = local
    slot = lax.broadcasted_iota(jnp.int32, (CAP, width), 0)
    mine = (owner_row == me) & (rank_row == slot)
    local = jnp.sum(jnp.where(mine, pivot_row - (me + 1) * rows, 0), axis=1, keepdims=True) + rows
    one_hot = (lax.broadcasted_iota(jnp.int32, (CAP, rows), 1) == local).astype(F32).astype(BF16)
    packed_ref[...] = select_rows(one_hot, slab_ref[...])
    slot = lax.broadcasted_iota(jnp.int32, (count, width), 0)
    one_hot = (slot == lead_place(owner_row, count // CAP) * CAP + rank_row).astype(F32).astype(BF16)
    lead_ref[...] = select_rows(one_hot, slab_ref[:width, :])


def block_inverses(lower):
    width = lower.shape[0]
    lane = lax.broadcasted_iota(jnp.int32, (BLOCK, width), 1)
    sub = lax.broadcasted_iota(jnp.int32, (BLOCK, width), 0)
    block = lane // BLOCK
    within = lane % BLOCK
    diag = jnp.zeros((BLOCK, width), F32)
    for b in range(width // BLOCK):
        diag = jnp.where(block == b, lower[b * BLOCK : (b + 1) * BLOCK], diag)
    diag = jnp.where(within < sub, diag, 0.0)
    inv = jnp.where(within == sub, 1.0, 0.0).astype(F32)
    half = 128
    first = (lax.broadcasted_iota(jnp.int32, (BLOCK, half), 1) // BLOCK) * BLOCK
    outs = []
    for h in range(0, width, half):
        d, x = diag[:, h : h + half], inv[:, h : h + half]
        for k in range(BLOCK - 1):
            column = jnp.take_along_axis(d, first + k, axis=1)
            x = x - column * x[k : k + 1, :]
        outs.append(x)
    return outs


def choice_kernel(n, rows, pivot_ref, out_ref):
    _, _, owner_col, rank_col = slots(pivot_ref[...], rows)
    place = jnp.bitwise_xor(owner_col, lax.axis_index("prow")) * CAP + rank_col
    out_ref[...] = (lax.broadcasted_iota(jnp.int32, out_ref.shape, 1) == place).astype(F32).astype(BF16)


def order_kernel(choice_ref, gathered_ref, out_ref):
    out_ref[...] = select_rows(choice_ref[...], gathered_ref[...])


def top_order(m):
    return [0, 1, *range(m - 1, 1, -1)]


def cut_kernel(panel_ref, top_ref, rest_ref, sems):
    width = top_ref.shape[1]
    copies = []
    for c in range(sems.shape[0]):
        target = rest_ref.at[:, pl.ds((c - 1) * width, width)] if c else top_ref
        copies.append(pltpu.make_async_copy(panel_ref.at[:, pl.ds(c * width, width)], target, sems.at[c]))
        copies[-1].start()
    for copy in copies:
        copy.wait()


def assemble_kernel(m, *refs):
    *pieces, out_ref, lower_t = refs
    width = lower_t.shape[0]
    piece = width // m
    half = width // 2
    z = lax.axis_index("pcol")
    for d, ref in zip(top_order(m), pieces):
        lower_t[pl.ds(pl.multiple_of(jnp.bitwise_xor(z, d) * piece, piece), piece), :] = ref[...]
    out_ref[:half, :] = lower_t[:half, :]
    out_ref[half:, :half] = lower_t[half : half + half // 2, half:]
    out_ref[half:, half:] = lower_t[half + half // 2 :, half:]


def pick_kernel(span, moved_ref, held_ref, out_ref):
    child = lax.rem(lax.axis_index("prow"), 2 * span) == span

    @pl.when(child)
    def _():
        out_ref[...] = moved_ref[...]

    @pl.when(jnp.logical_not(child))
    def _():
        out_ref[...] = held_ref[...]


def invert_kernel(lower_ref, out_ref, lower_t):
    holds = lax.axis_index("prow") & 1 == 0

    @pl.when(jnp.logical_not(holds))
    def _():
        out_ref[...] = jnp.zeros_like(out_ref)

    @pl.when(holds)
    def _():
        width = lower_t.shape[0]
        half = width // 2
        lower_t[:half, :] = lower_ref[:half, :]
        lower_t[half:, :half] = jnp.zeros((half, half), F32)
        lower_t[half : half + half // 2, half:] = lower_ref[half:, :half]
        lower_t[half + half // 2 :, half:] = lower_ref[half:, half:]
        lower = lower_t[...].T
        blocks = block_inverses(lower)
        row = lax.broadcasted_iota(jnp.int32, (half, half), 0)
        col = lax.broadcasted_iota(jnp.int32, (half, half), 1)
        for h, strip in enumerate(blocks):
            corner = lower[h * half : (h + 1) * half, h * half : (h + 1) * half]
            inv = jnp.where(row // BLOCK == col // BLOCK, jnp.concatenate([strip] * (half // BLOCK), axis=0), 0.0)
            size = BLOCK
            while size < half:
                off = (row // (2 * size) == col // (2 * size)) & (row // size > col // size)
                inv = inv - dot_full(dot_full(inv, jnp.where(off, corner, 0.0)), inv)
                size *= 2
            out_ref[:half, h * half : (h + 1) * half] = inv
        out_ref[half:, :half] = lower[half : half + half // 2, :half]
        out_ref[half:, half:] = lower[half + half // 2 :, :half]


def solve_kernel(inverse_ref, pivot_rows_ref, x_ref):
    half = pivot_rows_ref.shape[0] // 2
    quarter = jnp.concatenate([inverse_ref[half:, :half], inverse_ref[half:, half:]], axis=0)
    first = dot_full(inverse_ref[:half, :half], pivot_rows_ref[:half, :])
    x_ref[:half, :] = first
    x_ref[half:, :] = dot_full(inverse_ref[:half, half:], pivot_rows_ref[half:, :] - dot_full(quarter, first))


def product(pieces, upper):
    high, low = zip(*(split2(piece) for piece in pieces))
    high, low = jnp.concatenate(high, axis=0), jnp.concatenate(low, axis=0)
    upper_high, upper_low = upper
    width = upper_high.shape[1]

    def dot(a, b):
        return lax.dot_general(a, b, (((0,), (0,)), ((), ())), preferred_element_type=F32)

    both = dot(high, jnp.concatenate([upper_high, upper_low], axis=1))
    return both[:, :width] + (both[:, width:] + dot(low, upper_high))


def piece_rows(x_ref, m, d):
    piece = (x_ref.shape[0] - CAP) // m
    source = jnp.bitwise_xor(lax.axis_index("pcol"), d)
    return x_ref[pl.ds(pl.multiple_of(source * piece, piece), piece), :]


def update_kernel(m, local_ref, x_ref, slab_ref, *refs):
    *pieces, out_ref, result, swaps, sems = refs
    tops, rests = pieces[:m], pieces[m:]
    rows = slab_ref.shape[0]
    width = x_ref.shape[0] - CAP
    blocks = rows // width
    fetch = pltpu.make_async_copy(local_ref, swaps, sems.at[blocks])
    fetch.start()
    result[:rows, :] = slab_ref[...]
    top_upper = split2(jnp.concatenate([piece_rows(x_ref, m, d) for d in top_order(m)], axis=0))
    upper = split2(jnp.concatenate([piece_rows(x_ref, m, d) for d in range(m)], axis=0))
    copies = []
    for c in range(blocks):
        part = pl.ds(c * width, width)
        if c:
            total = product([rest[:, (c - 1) * width : c * width] for rest in rests], upper)
        else:
            total = product([top[...] for top in tops], top_upper)
            fetch.wait()
            for s in range(CAP):
                result[pl.ds(swaps[0, s], 1), :] = x_ref[pl.ds(width + s, 1), :]
        result[part, :] = result[part, :] - total
        if c == 0:

            @pl.when(lax.axis_index("prow") == 0)
            def _():
                result[part, :] = x_ref[:width, :]

        copy = pltpu.make_async_copy(result.at[part], out_ref.at[part], sems.at[c])
        copy.start()
        copies.append(copy)
    for copy in copies:
        copy.wait()


def unit(held, steps, *operands):
    shapes = jax.eval_shape(steps, *operands)
    return lax.cond(held, steps, lambda *_: jax.tree.map(lambda s: jnp.zeros(s.shape, s.dtype), shapes), *operands)


def call(kernel, outs, operands, in_specs=None, out_specs=None, scratch=()):
    return pl.pallas_call(
        kernel,
        out_shape=outs,
        in_specs=in_specs or [VMEM] * len(operands),
        out_specs=out_specs or jax.tree.map(lambda _: VMEM, outs),
        scratch_shapes=list(scratch),
        compiler_params=PARAMS,
        cost_estimate=pl.CostEstimate(flops=1, bytes_accessed=1, transcendentals=0),
    )(*operands)


def local(n, m, slab, panel, pivots):
    rows, cols = slab.shape
    width = pivots.shape[0]
    piece = panel.shape[1]
    me = lax.axis_index("prow")
    panel_t = panel.T
    pivot_row = pivots.reshape(1, width)

    def exchange(block, d):
        return lax.ppermute(block, "pcol", [(c, c ^ d) for c in range(m)])

    top, rest = call(
        cut_kernel,
        (jax.ShapeDtypeStruct((piece, width), F32), jax.ShapeDtypeStruct((piece, rows - width), F32)),
        (panel_t,),
        in_specs=[pl.BlockSpec(memory_space=pl.ANY)],
        scratch=[pltpu.SemaphoreType.DMA((rows // width,))],
    )
    tops = [top] + [exchange(top, d) for d in top_order(m)[1:]]
    rests = [rest] + [exchange(rest, d) for d in range(1, m)]

    gathered, leading, local_rows = call(
        pack_kernel,
        (
            jax.ShapeDtypeStruct((CAP, cols), F32),
            jax.ShapeDtypeStruct((n * CAP, cols), F32),
            jax.ShapeDtypeStruct((1, 128), jnp.int32),
        ),
        (pivot_row, slab),
    )
    lower = call(
        functools.partial(assemble_kernel, m),
        jax.ShapeDtypeStruct((width * 3 // 4, width), F32),
        tops,
        scratch=[pltpu.VMEM((width, width), F32)],
    )

    def split(leading):
        blocks = leading.reshape(2, -1, cols)
        return blocks[0], blocks[1]

    def levels(lower, gathered, leading):
        span, other, held = n // 2, 2, lower
        while span > 1:
            moved = lax.ppermute(lower, "prow", [(r, tree_partner(r, span)) for r in range(n)])
            lower = call(
                functools.partial(pick_kernel, span),
                jax.ShapeDtypeStruct(lower.shape, F32),
                (moved, held),
            )
            kept, sent = split(leading)
            count = gathered.shape[0]
            message = jnp.concatenate([gathered, sent], axis=0)
            moved = lax.ppermute(message, "prow", [(r, r ^ other) for r in range(n)])
            moved, held = lax.optimization_barrier((moved, lower))
            gathered = jnp.concatenate([gathered, moved[:count]], axis=0)
            leading = jnp.where(me & other != 0, moved[count:], kept)
            span, other = span // 2, other * 2
        choice = call(
            functools.partial(choice_kernel, n, rows), jax.ShapeDtypeStruct((width, n * CAP), BF16), (pivot_row,)
        )
        pivot_rows = call(order_kernel, jax.ShapeDtypeStruct((width, cols), F32), (choice, gathered))
        inverse = call(
            invert_kernel,
            jax.ShapeDtypeStruct(lower.shape, F32),
            (lower,),
            scratch=[pltpu.VMEM((width, width), F32)],
        )
        moved = lax.ppermute(inverse, "prow", [(r, r ^ 1) for r in range(n)])
        inverse = jnp.where(me & 1 != 0, moved, inverse)
        upper_rows = call(solve_kernel, jax.ShapeDtypeStruct((width, cols), F32), (inverse, pivot_rows))
        return jnp.concatenate([upper_rows, leading], axis=0)

    gathered, lower = lax.optimization_barrier((gathered, lower))
    twins = [(r, r ^ 1) for r in range(n)]
    moved = lax.ppermute(gathered, "prow", twins)
    gathered = jnp.concatenate([gathered, moved], axis=0)
    kept, sent = split(leading)
    leading = jnp.where(me & 1 != 0, lax.ppermute(sent, "prow", twins), kept)
    upper_rows = unit(me < n, levels, lower, gathered, leading)
    return call(
        functools.partial(update_kernel, m),
        jax.ShapeDtypeStruct((rows, cols), F32),
        (local_rows, upper_rows, slab, *tops, *rests),
        in_specs=[VMEM] * (2 * m + 3),
        out_specs=pl.BlockSpec(memory_space=pl.ANY),
        scratch=[
            pltpu.VMEM((rows + 8, cols), F32),
            pltpu.SMEM((1, 128), jnp.int32),
            pltpu.SemaphoreType.DMA((rows // width + 1,)),
        ],
    )


def solution(mesh):
    return jax.shard_map(
        functools.partial(local, mesh.shape["prow"], mesh.shape["pcol"]),
        mesh=mesh,
        in_specs=(P("prow", "pcol"), P("prow", "pcol"), P()),
        out_specs=P("prow", "pcol"),
        check_vma=False,
    )
```

```python
import functools

import jax
import jax.numpy as jnp
from jax import lax
from jax.experimental import pallas as pl
from jax.experimental.pallas import tpu as pltpu
from jax.sharding import PartitionSpec as P

CAP = 32
BLOCK = 32
F32 = jnp.float32
BF16 = jnp.bfloat16
VMEM = pl.BlockSpec(memory_space=pltpu.VMEM)
PARAMS = pltpu.CompilerParams(vmem_limit_bytes=16 * 1024 * 1024)


def split3(x):
    high = x.astype(BF16)
    rest = x - high.astype(F32)
    mid = rest.astype(BF16)
    low = (rest - mid.astype(F32)).astype(BF16)
    return high, mid, low


def split2(x):
    high = x.astype(BF16)
    return high, (x - high.astype(F32)).astype(BF16)


def select_rows(one_hot, x):
    return sum(jnp.dot(one_hot, part, preferred_element_type=F32) for part in split3(x))


def dot_full(a, b):
    high, mid, low = split3(a)
    left = jnp.concatenate([low, mid, high, mid, high, high], axis=1)
    high, mid, low = split3(b)
    right = jnp.concatenate([high, mid, low, high, mid, high], axis=0)
    return jnp.dot(left, right, preferred_element_type=F32)


def tree_partner(r, span):
    if span == 1 or r % span > 1:
        return r ^ 1
    if r % 2 == 0:
        return r + 1 if r & span else r + span
    return r - span if r & span else r - 1


def lead_place(owner, n):
    bits = n.bit_length() - 1
    return sum((lax.shift_right_logical(owner, bit) & 1) * (1 << (bits - 1 - bit)) for bit in range(bits))


def slots(pivot_row, rows):
    width = pivot_row.shape[1]
    by_sublane = jnp.broadcast_to(pivot_row, (width, width)).T
    shift = rows.bit_length() - 1
    owner_row = jnp.broadcast_to(lax.shift_right_logical(pivot_row, shift), (width, width))
    owner_col = lax.shift_right_logical(by_sublane, shift)
    sub = lax.broadcasted_iota(jnp.int32, (width, width), 0)
    lane = lax.broadcasted_iota(jnp.int32, (width, width), 1)
    same = owner_row == owner_col
    rank_row = jnp.sum(jnp.where(same & (sub < lane), 1, 0), axis=0, keepdims=True)
    rank_col = jnp.sum(jnp.where(same & (lane < sub), 1, 0), axis=1, keepdims=True)
    return owner_row[:1], rank_row, owner_col[:, :1], rank_col


def pack_kernel(pivot_ref, slab_ref, packed_ref, lead_ref, local_ref):
    rows = slab_ref.shape[0]
    width = pivot_ref.shape[1]
    count = lead_ref.shape[0]
    lanes = local_ref.shape[1]
    me = lax.axis_index("prow")
    pivot_row = pivot_ref[...]
    owner_row, rank_row, owner_col, rank_col = slots(pivot_row, rows)
    pivot_col = jnp.broadcast_to(pivot_row, (lanes, width)).T
    slot = lax.broadcasted_iota(jnp.int32, (width, lanes), 1)
    mine = (owner_col == me) & (rank_col == slot)
    local = jnp.sum(jnp.where(mine, pivot_col - (me + 1) * rows, 0), axis=0, keepdims=True) + rows
    local_ref[...] = local
    slot = lax.broadcasted_iota(jnp.int32, (CAP, width), 0)
    mine = (owner_row == me) & (rank_row == slot)
    local = jnp.sum(jnp.where(mine, pivot_row - (me + 1) * rows, 0), axis=1, keepdims=True) + rows
    one_hot = (lax.broadcasted_iota(jnp.int32, (CAP, rows), 1) == local).astype(F32).astype(BF16)
    packed_ref[...] = select_rows(one_hot, slab_ref[...])
    slot = lax.broadcasted_iota(jnp.int32, (count, width), 0)
    one_hot = (slot == lead_place(owner_row, count // CAP) * CAP + rank_row).astype(F32).astype(BF16)
    lead_ref[...] = select_rows(one_hot, slab_ref[:width, :])


def block_inverses(lower):
    width = lower.shape[0]
    lane = lax.broadcasted_iota(jnp.int32, (BLOCK, width), 1)
    sub = lax.broadcasted_iota(jnp.int32, (BLOCK, width), 0)
    block = lane // BLOCK
    within = lane % BLOCK
    diag = jnp.zeros((BLOCK, width), F32)
    for b in range(width // BLOCK):
        diag = jnp.where(block == b, lower[b * BLOCK : (b + 1) * BLOCK], diag)
    diag = jnp.where(within < sub, diag, 0.0)
    inv = jnp.where(within == sub, 1.0, 0.0).astype(F32)
    half = 128
    first = (lax.broadcasted_iota(jnp.int32, (BLOCK, half), 1) // BLOCK) * BLOCK
    outs = []
    for h in range(0, width, half):
        d, x = diag[:, h : h + half], inv[:, h : h + half]
        for k in range(BLOCK - 1):
            column = jnp.take_along_axis(d, first + k, axis=1)
            x = x - column * x[k : k + 1, :]
        outs.append(x)
    return outs


def choice_kernel(n, rows, pivot_ref, out_ref):
    _, _, owner_col, rank_col = slots(pivot_ref[...], rows)
    place = jnp.bitwise_xor(owner_col, lax.axis_index("prow")) * CAP + rank_col
    out_ref[...] = (lax.broadcasted_iota(jnp.int32, out_ref.shape, 1) == place).astype(F32).astype(BF16)


def order_kernel(choice_ref, gathered_ref, out_ref):
    out_ref[...] = select_rows(choice_ref[...], gathered_ref[...])


def top_order(m):
    return [0, 1, *range(m - 1, 1, -1)]


def cut_kernel(panel_ref, top_ref, rest_ref, sems):
    width = top_ref.shape[1]
    copies = []
    for c in range(sems.shape[0]):
        target = rest_ref.at[:, pl.ds((c - 1) * width, width)] if c else top_ref
        copies.append(pltpu.make_async_copy(panel_ref.at[:, pl.ds(c * width, width)], target, sems.at[c]))
        copies[-1].start()
    for copy in copies:
        copy.wait()


def assemble_kernel(m, *refs):
    *pieces, out_ref, lower_t = refs
    width = lower_t.shape[0]
    piece = width // m
    half = width // 2
    z = lax.axis_index("pcol")
    for d, ref in zip(top_order(m), pieces):
        lower_t[pl.ds(pl.multiple_of(jnp.bitwise_xor(z, d) * piece, piece), piece), :] = ref[...]
    out_ref[:half, :] = lower_t[:half, :]
    out_ref[half:, :half] = lower_t[half : half + half // 2, half:]
    out_ref[half:, half:] = lower_t[half + half // 2 :, half:]


def pick_kernel(span, moved_ref, held_ref, out_ref):
    child = lax.rem(lax.axis_index("prow"), 2 * span) == span

    @pl.when(child)
    def _():
        out_ref[...] = moved_ref[...]

    @pl.when(jnp.logical_not(child))
    def _():
        out_ref[...] = held_ref[...]


def invert_kernel(lower_ref, out_ref, lower_t):
    holds = lax.axis_index("prow") & 1 == 0

    @pl.when(jnp.logical_not(holds))
    def _():
        out_ref[...] = jnp.zeros_like(out_ref)

    @pl.when(holds)
    def _():
        width = lower_t.shape[0]
        half = width // 2
        lower_t[:half, :] = lower_ref[:half, :]
        lower_t[half:, :half] = jnp.zeros((half, half), F32)
        lower_t[half : half + half // 2, half:] = lower_ref[half:, :half]
        lower_t[half + half // 2 :, half:] = lower_ref[half:, half:]
        lower = lower_t[...].T
        blocks = block_inverses(lower)
        row = lax.broadcasted_iota(jnp.int32, (half, half), 0)
        col = lax.broadcasted_iota(jnp.int32, (half, half), 1)
        for h, strip in enumerate(blocks):
            corner = lower[h * half : (h + 1) * half, h * half : (h + 1) * half]
            inv = jnp.where(row // BLOCK == col // BLOCK, jnp.concatenate([strip] * (half // BLOCK), axis=0), 0.0)
            size = BLOCK
            while size < half:
                off = (row // (2 * size) == col // (2 * size)) & (row // size > col // size)
                inv = inv - dot_full(dot_full(inv, jnp.where(off, corner, 0.0)), inv)
                size *= 2
            out_ref[:half, h * half : (h + 1) * half] = inv
        out_ref[half:, :half] = lower[half : half + half // 2, :half]
        out_ref[half:, half:] = lower[half + half // 2 :, :half]


def solve_kernel(inverse_ref, pivot_rows_ref, x_ref):
    half = pivot_rows_ref.shape[0] // 2
    quarter = jnp.concatenate([inverse_ref[half:, :half], inverse_ref[half:, half:]], axis=0)
    first = dot_full(inverse_ref[:half, :half], pivot_rows_ref[:half, :])
    x_ref[:half, :] = first
    x_ref[half:, :] = dot_full(inverse_ref[:half, half:], pivot_rows_ref[half:, :] - dot_full(quarter, first))


def product(pieces, upper):
    high, low = zip(*(split2(piece) for piece in pieces))
    high, low = jnp.concatenate(high, axis=0), jnp.concatenate(low, axis=0)
    upper_high, upper_low = upper
    width = upper_high.shape[1]

    def dot(a, b):
        return lax.dot_general(a, b, (((0,), (0,)), ((), ())), preferred_element_type=F32)

    both = dot(high, jnp.concatenate([upper_high, upper_low], axis=1))
    return both[:, :width] + (both[:, width:] + dot(low, upper_high))


def piece_rows(x_ref, m, d):
    piece = (x_ref.shape[0] - CAP) // m
    source = jnp.bitwise_xor(lax.axis_index("pcol"), d)
    return x_ref[pl.ds(pl.multiple_of(source * piece, piece), piece), :]


def update_kernel(m, local_ref, x_ref, slab_ref, *refs):
    *pieces, out_ref, result, swaps, sems = refs
    tops, rests = pieces[:m], pieces[m:]
    rows = slab_ref.shape[0]
    width = x_ref.shape[0] - CAP
    blocks = rows // width
    fetch = pltpu.make_async_copy(local_ref, swaps, sems.at[blocks])
    fetch.start()
    result[:rows, :] = slab_ref[...]
    top_upper = split2(jnp.concatenate([piece_rows(x_ref, m, d) for d in top_order(m)], axis=0))
    upper = split2(jnp.concatenate([piece_rows(x_ref, m, d) for d in range(m)], axis=0))
    copies = []
    for c in range(blocks):
        part = pl.ds(c * width, width)
        if c:
            total = product([rest[:, (c - 1) * width : c * width] for rest in rests], upper)
        else:
            total = product([top[...] for top in tops], top_upper)
            fetch.wait()
            for s in range(CAP):
                result[pl.ds(swaps[0, s], 1), :] = x_ref[pl.ds(width + s, 1), :]
        result[part, :] = result[part, :] - total
        if c == 0:

            @pl.when(lax.axis_index("prow") == 0)
            def _():
                result[part, :] = x_ref[:width, :]

        copy = pltpu.make_async_copy(result.at[part], out_ref.at[part], sems.at[c])
        copy.start()
        copies.append(copy)
    for copy in copies:
        copy.wait()


def unit(held, steps, *operands):
    shapes = jax.eval_shape(steps, *operands)
    return lax.cond(held, steps, lambda *_: jax.tree.map(lambda s: jnp.zeros(s.shape, s.dtype), shapes), *operands)


def call(kernel, outs, operands, in_specs=None, out_specs=None, scratch=()):
    return pl.pallas_call(
        kernel,
        out_shape=outs,
        in_specs=in_specs or [VMEM] * len(operands),
        out_specs=out_specs or jax.tree.map(lambda _: VMEM, outs),
        scratch_shapes=list(scratch),
        compiler_params=PARAMS,
        cost_estimate=pl.CostEstimate(flops=1, bytes_accessed=1, transcendentals=0),
    )(*operands)


def local(n, m, slab, panel, pivots):
    rows, cols = slab.shape
    width = pivots.shape[0]
    piece = panel.shape[1]
    me = lax.axis_index("prow")
    panel_t = panel.T
    pivot_row = pivots.reshape(1, width)

    def exchange(block, d):
        return lax.ppermute(block, "pcol", [(c, c ^ d) for c in range(m)])

    top, rest = call(
        cut_kernel,
        (jax.ShapeDtypeStruct((piece, width), F32), jax.ShapeDtypeStruct((piece, rows - width), F32)),
        (panel_t,),
        in_specs=[pl.BlockSpec(memory_space=pl.ANY)],
        scratch=[pltpu.SemaphoreType.DMA((rows // width,))],
    )
    tops = [top] + [exchange(top, d) for d in top_order(m)[1:]]
    rests = [rest] + [exchange(rest, d) for d in range(1, m)]

    gathered, leading, local_rows = call(
        pack_kernel,
        (
            jax.ShapeDtypeStruct((CAP, cols), F32),
            jax.ShapeDtypeStruct((n * CAP, cols), F32),
            jax.ShapeDtypeStruct((1, 128), jnp.int32),
        ),
        (pivot_row, slab),
    )
    lower = call(
        functools.partial(assemble_kernel, m),
        jax.ShapeDtypeStruct((width * 3 // 4, width), F32),
        tops,
        scratch=[pltpu.VMEM((width, width), F32)],
    )

    def split(leading):
        blocks = leading.reshape(2, -1, cols)
        return blocks[0], blocks[1]

    def levels(lower, gathered, leading):
        span, other, held = n // 2, 2, lower
        while span > 1:
            moved = lax.ppermute(lower, "prow", [(r, tree_partner(r, span)) for r in range(n)])
            lower = call(
                functools.partial(pick_kernel, span),
                jax.ShapeDtypeStruct(lower.shape, F32),
                (moved, held),
            )
            kept, sent = split(leading)
            count = gathered.shape[0]
            message = jnp.concatenate([gathered, sent], axis=0)
            moved = lax.ppermute(message, "prow", [(r, r ^ other) for r in range(n)])
            moved, held = lax.optimization_barrier((moved, lower))
            gathered = jnp.concatenate([gathered, moved[:count]], axis=0)
            leading = jnp.where(me & other != 0, moved[count:], kept)
            span, other = span // 2, other * 2
        choice = call(
            functools.partial(choice_kernel, n, rows), jax.ShapeDtypeStruct((width, n * CAP), BF16), (pivot_row,)
        )
        pivot_rows = call(order_kernel, jax.ShapeDtypeStruct((width, cols), F32), (choice, gathered))
        inverse = call(
            invert_kernel,
            jax.ShapeDtypeStruct(lower.shape, F32),
            (lower,),
            scratch=[pltpu.VMEM((width, width), F32)],
        )
        moved = lax.ppermute(inverse, "prow", [(r, r ^ 1) for r in range(n)])
        inverse = jnp.where(me & 1 != 0, moved, inverse)
        upper_rows = call(solve_kernel, jax.ShapeDtypeStruct((width, cols), F32), (inverse, pivot_rows))
        return jnp.concatenate([upper_rows, leading], axis=0)

    gathered, lower = lax.optimization_barrier((gathered, lower))
    twins = [(r, r ^ 1) for r in range(n)]
    moved = lax.ppermute(gathered, "prow", twins)
    gathered = jnp.concatenate([gathered, moved], axis=0)
    kept, sent = split(leading)
    leading = jnp.where(me & 1 != 0, lax.ppermute(sent, "prow", twins), kept)
    upper_rows = unit(me < n, levels, lower, gathered, leading)
    return call(
        functools.partial(update_kernel, m),
        jax.ShapeDtypeStruct((rows, cols), F32),
        (local_rows, upper_rows, slab, *tops, *rests),
        in_specs=[VMEM] * (2 * m + 3),
        out_specs=pl.BlockSpec(memory_space=pl.ANY),
        scratch=[
            pltpu.VMEM((rows + 8, cols), F32),
            pltpu.SMEM((1, 128), jnp.int32),
            pltpu.SemaphoreType.DMA((rows // width + 1,)),
        ],
    )


def solution(mesh):
    return jax.shard_map(
        functools.partial(local, mesh.shape["prow"], mesh.shape["pcol"]),
        mesh=mesh,
        in_specs=(P("prow", "pcol"), P("prow", "pcol"), P()),
        out_specs=P("prow", "pcol"),
        check_vma=False,
    )
```

```python
import functools

import jax
import jax.numpy as jnp
from jax import lax
from jax.experimental import pallas as pl
from jax.experimental.pallas import tpu as pltpu
from jax.sharding import PartitionSpec as P

CAP = 32
BLOCK = 32
F32 = jnp.float32
BF16 = jnp.bfloat16
VMEM = pl.BlockSpec(memory_space=pltpu.VMEM)
PARAMS = pltpu.CompilerParams(vmem_limit_bytes=24 * 1024 * 1024)


def split3(x):
    high = x.astype(BF16)
    rest = x - high.astype(F32)
    mid = rest.astype(BF16)
    low = (rest - mid.astype(F32)).astype(BF16)
    return high, mid, low


def split2(x):
    high = x.astype(BF16)
    return high, (x - high.astype(F32)).astype(BF16)


def select_rows(one_hot, x):
    return sum(jnp.dot(one_hot, part, preferred_element_type=F32) for part in split3(x))


def dot_full(a, b):
    high, mid, low = split3(a)
    left = jnp.concatenate([low, mid, high, mid, high, high], axis=1)
    high, mid, low = split3(b)
    right = jnp.concatenate([high, mid, low, high, mid, high], axis=0)
    return jnp.dot(left, right, preferred_element_type=F32)


def tree_partner(r, span):
    if span == 1 or r % span > 1:
        return r ^ 1
    if r % 2 == 0:
        return r + 1 if r & span else r + span
    return r - span if r & span else r - 1


def lead_place(owner, n):
    bits = n.bit_length() - 1
    return sum((lax.shift_right_logical(owner, bit) & 1) * (1 << (bits - 1 - bit)) for bit in range(bits))


def slots(pivot_row, rows):
    width = pivot_row.shape[1]
    by_sublane = jnp.broadcast_to(pivot_row, (width, width)).T
    shift = rows.bit_length() - 1
    owner_row = jnp.broadcast_to(lax.shift_right_logical(pivot_row, shift), (width, width))
    owner_col = lax.shift_right_logical(by_sublane, shift)
    sub = lax.broadcasted_iota(jnp.int32, (width, width), 0)
    lane = lax.broadcasted_iota(jnp.int32, (width, width), 1)
    same = owner_row == owner_col
    rank_row = jnp.sum(jnp.where(same & (sub < lane), 1, 0), axis=0, keepdims=True)
    rank_col = jnp.sum(jnp.where(same & (lane < sub), 1, 0), axis=1, keepdims=True)
    return owner_row[:1], rank_row, owner_col[:, :1], rank_col


def pack_kernel(pivot_ref, slab_ref, packed_ref, lead_ref, local_ref):
    rows = slab_ref.shape[0]
    width = pivot_ref.shape[1]
    count = lead_ref.shape[0]
    lanes = local_ref.shape[1]
    me = lax.axis_index("prow")
    pivot_row = pivot_ref[...]
    owner_row, rank_row, owner_col, rank_col = slots(pivot_row, rows)
    pivot_col = jnp.broadcast_to(pivot_row, (lanes, width)).T
    slot = lax.broadcasted_iota(jnp.int32, (width, lanes), 1)
    mine = (owner_col == me) & (rank_col == slot)
    local = jnp.sum(jnp.where(mine, pivot_col - (me + 1) * rows, 0), axis=0, keepdims=True) + rows
    local_ref[...] = local
    slot = lax.broadcasted_iota(jnp.int32, (CAP, width), 0)
    mine = (owner_row == me) & (rank_row == slot)
    local = jnp.sum(jnp.where(mine, pivot_row - (me + 1) * rows, 0), axis=1, keepdims=True) + rows
    one_hot = (lax.broadcasted_iota(jnp.int32, (CAP, rows), 1) == local).astype(F32).astype(BF16)
    packed_ref[...] = select_rows(one_hot, slab_ref[...])
    slot = lax.broadcasted_iota(jnp.int32, (count, width), 0)
    one_hot = (slot == lead_place(owner_row, count // CAP) * CAP + rank_row).astype(F32).astype(BF16)
    lead_ref[...] = select_rows(one_hot, slab_ref[:width, :])


def block_inverses(lower):
    width = lower.shape[0]
    lane = lax.broadcasted_iota(jnp.int32, (BLOCK, width), 1)
    sub = lax.broadcasted_iota(jnp.int32, (BLOCK, width), 0)
    block = lane // BLOCK
    within = lane % BLOCK
    diag = jnp.zeros((BLOCK, width), F32)
    for b in range(width // BLOCK):
        diag = jnp.where(block == b, lower[b * BLOCK : (b + 1) * BLOCK], diag)
    diag = jnp.where(within < sub, diag, 0.0)
    inv = jnp.where(within == sub, 1.0, 0.0).astype(F32)
    half = 128
    first = (lax.broadcasted_iota(jnp.int32, (BLOCK, half), 1) // BLOCK) * BLOCK
    outs = []
    for h in range(0, width, half):
        d, x = diag[:, h : h + half], inv[:, h : h + half]
        for k in range(BLOCK - 1):
            column = jnp.take_along_axis(d, first + k, axis=1)
            x = x - column * x[k : k + 1, :]
        outs.append(x)
    return outs


def choice_kernel(n, rows, pivot_ref, out_ref):
    _, _, owner_col, rank_col = slots(pivot_ref[...], rows)
    place = jnp.bitwise_xor(owner_col, lax.axis_index("prow")) * CAP + rank_col
    out_ref[...] = (lax.broadcasted_iota(jnp.int32, out_ref.shape, 1) == place).astype(F32).astype(BF16)


def order_kernel(choice_ref, gathered_ref, out_ref):
    out_ref[...] = select_rows(choice_ref[...], gathered_ref[...])


def top_order(m):
    return [0, 1, *range(m - 1, 1, -1)]


def cut_kernel(panel_ref, top_ref, rest_ref, sems):
    width = top_ref.shape[1]
    copies = []
    for c in range(sems.shape[0]):
        target = rest_ref.at[:, pl.ds((c - 1) * width, width)] if c else top_ref
        copies.append(pltpu.make_async_copy(panel_ref.at[:, pl.ds(c * width, width)], target, sems.at[c]))
        copies[-1].start()
    for copy in copies:
        copy.wait()


def assemble_kernel(m, *refs):
    *pieces, out_ref, lower_t = refs
    width = lower_t.shape[0]
    piece = width // m
    half = width // 2
    z = lax.axis_index("pcol")
    for d, ref in zip(top_order(m), pieces):
        lower_t[pl.ds(pl.multiple_of(jnp.bitwise_xor(z, d) * piece, piece), piece), :] = ref[...]
    out_ref[:half, :] = lower_t[:half, :]
    out_ref[half:, :half] = lower_t[half : half + half // 2, half:]
    out_ref[half:, half:] = lower_t[half + half // 2 :, half:]


def pick_kernel(span, moved_ref, held_ref, out_ref):
    child = lax.rem(lax.axis_index("prow"), 2 * span) == span

    @pl.when(child)
    def _():
        out_ref[...] = moved_ref[...]

    @pl.when(jnp.logical_not(child))
    def _():
        out_ref[...] = held_ref[...]


def invert_kernel(lower_ref, out_ref, lower_t):
    holds = lax.axis_index("prow") & 1 == 0

    @pl.when(jnp.logical_not(holds))
    def _():
        out_ref[...] = jnp.zeros_like(out_ref)

    @pl.when(holds)
    def _():
        width = lower_t.shape[0]
        half = width // 2
        lower_t[:half, :] = lower_ref[:half, :]
        lower_t[half:, :half] = jnp.zeros((half, half), F32)
        lower_t[half : half + half // 2, half:] = lower_ref[half:, :half]
        lower_t[half + half // 2 :, half:] = lower_ref[half:, half:]
        lower = lower_t[...].T
        blocks = block_inverses(lower)
        row = lax.broadcasted_iota(jnp.int32, (half, half), 0)
        col = lax.broadcasted_iota(jnp.int32, (half, half), 1)
        for h, strip in enumerate(blocks):
            corner = lower[h * half : (h + 1) * half, h * half : (h + 1) * half]
            inv = jnp.where(row // BLOCK == col // BLOCK, jnp.concatenate([strip] * (half // BLOCK), axis=0), 0.0)
            size = BLOCK
            while size < half:
                off = (row // (2 * size) == col // (2 * size)) & (row // size > col // size)
                inv = inv - dot_full(dot_full(inv, jnp.where(off, corner, 0.0)), inv)
                size *= 2
            out_ref[:half, h * half : (h + 1) * half] = inv
        out_ref[half:, :half] = lower[half : half + half // 2, :half]
        out_ref[half:, half:] = lower[half + half // 2 :, :half]


def solve_kernel(inverse_ref, pivot_rows_ref, x_ref):
    half = pivot_rows_ref.shape[0] // 2
    quarter = jnp.concatenate([inverse_ref[half:, :half], inverse_ref[half:, half:]], axis=0)
    first = dot_full(inverse_ref[:half, :half], pivot_rows_ref[:half, :])
    x_ref[:half, :] = first
    x_ref[half:, :] = dot_full(inverse_ref[:half, half:], pivot_rows_ref[half:, :] - dot_full(quarter, first))


def product(pieces, upper):
    high, low = zip(*(split2(piece) for piece in pieces))
    high, low = jnp.concatenate(high, axis=0), jnp.concatenate(low, axis=0)
    upper_high, upper_low = upper
    width = upper_high.shape[1]

    def dot(a, b):
        return lax.dot_general(a, b, (((0,), (0,)), ((), ())), preferred_element_type=F32)

    both = dot(high, jnp.concatenate([upper_high, upper_low], axis=1))
    return both[:, :width] + (both[:, width:] + dot(low, upper_high))


def piece_rows(x_ref, m, d):
    piece = x_ref.shape[0] // m
    source = jnp.bitwise_xor(lax.axis_index("pcol"), d)
    return x_ref[pl.ds(pl.multiple_of(source * piece, piece), piece), :]


def update_kernel(m, local_ref, lead_ref, x_ref, slab_ref, *refs):
    *pieces, out_ref, result, swaps, sems = refs
    tops, rests = pieces[:m], pieces[m:]
    rows = slab_ref.shape[0]
    width = x_ref.shape[0]
    blocks = rows // width
    fetch = pltpu.make_async_copy(local_ref, swaps, sems.at[blocks])
    fetch.start()
    result[:rows, :] = slab_ref[...]
    top_upper = split2(jnp.concatenate([piece_rows(x_ref, m, d) for d in top_order(m)], axis=0))
    upper = split2(jnp.concatenate([piece_rows(x_ref, m, d) for d in range(m)], axis=0))
    copies = []
    for c in range(blocks):
        part = pl.ds(c * width, width)
        if c:
            total = product([rest[:, (c - 1) * width : c * width] for rest in rests], upper)
        else:
            total = product([top[...] for top in tops], top_upper)
            fetch.wait()
            for s in range(CAP):
                result[pl.ds(swaps[0, s], 1), :] = lead_ref[pl.ds(s, 1), :]
        result[part, :] = result[part, :] - total
        if c == 0:

            @pl.when(lax.axis_index("prow") == 0)
            def _():
                result[part, :] = x_ref[...]

        copy = pltpu.make_async_copy(result.at[part], out_ref.at[part], sems.at[c])
        copy.start()
        copies.append(copy)
    for copy in copies:
        copy.wait()


def unit(held, steps, *operands):
    shapes = jax.eval_shape(steps, *operands)
    return lax.cond(held, steps, lambda *_: jax.tree.map(lambda s: jnp.zeros(s.shape, s.dtype), shapes), *operands)


def call(kernel, outs, operands, in_specs=None, out_specs=None, scratch=()):
    return pl.pallas_call(
        kernel,
        out_shape=outs,
        in_specs=in_specs or [VMEM] * len(operands),
        out_specs=out_specs or jax.tree.map(lambda _: VMEM, outs),
        scratch_shapes=list(scratch),
        compiler_params=PARAMS,
        cost_estimate=pl.CostEstimate(flops=1, bytes_accessed=1, transcendentals=0),
    )(*operands)


def local(n, m, slab, panel, pivots):
    rows, cols = slab.shape
    width = pivots.shape[0]
    piece = panel.shape[1]
    me = lax.axis_index("prow")
    panel_t = panel.T
    pivot_row = pivots.reshape(1, width)

    def exchange(block, d):
        return lax.ppermute(block, "pcol", [(c, c ^ d) for c in range(m)])

    top, rest = call(
        cut_kernel,
        (jax.ShapeDtypeStruct((piece, width), F32), jax.ShapeDtypeStruct((piece, rows - width), F32)),
        (panel_t,),
        in_specs=[pl.BlockSpec(memory_space=pl.ANY)],
        scratch=[pltpu.SemaphoreType.DMA((rows // width,))],
    )
    tops = [top] + [exchange(top, d) for d in top_order(m)[1:]]
    rests = [rest] + [exchange(rest, d) for d in range(1, m)]

    gathered, leading, local_rows = call(
        pack_kernel,
        (
            jax.ShapeDtypeStruct((CAP, cols), F32),
            jax.ShapeDtypeStruct((n * CAP, cols), F32),
            jax.ShapeDtypeStruct((1, 128), jnp.int32),
        ),
        (pivot_row, slab),
    )
    lower = call(
        functools.partial(assemble_kernel, m),
        jax.ShapeDtypeStruct((width * 3 // 4, width), F32),
        tops,
        scratch=[pltpu.VMEM((width, width), F32)],
    )

    def split(leading):
        blocks = leading.reshape(2, -1, cols)
        return blocks[0], blocks[1]

    def levels(lower, gathered, leading, choice):
        span, other, held = n // 2, 2, lower
        while span > 1:
            moved = lax.ppermute(lower, "prow", [(r, tree_partner(r, span)) for r in range(n)])
            lower = call(
                functools.partial(pick_kernel, span),
                jax.ShapeDtypeStruct(lower.shape, F32),
                (moved, held),
            )
            kept, sent = split(leading)
            count = gathered.shape[0]
            message = jnp.concatenate([gathered, sent], axis=0)
            moved = lax.ppermute(message, "prow", [(r, r ^ other) for r in range(n)])
            moved, held = lax.optimization_barrier((moved, lower))
            gathered = jnp.concatenate([gathered, moved[:count]], axis=0)
            leading = jnp.where(me & other != 0, moved[count:], kept)
            span, other = span // 2, other * 2
        pivot_rows = call(order_kernel, jax.ShapeDtypeStruct((width, cols), F32), (choice, gathered))
        inverse = call(
            invert_kernel,
            jax.ShapeDtypeStruct(lower.shape, F32),
            (lower,),
            scratch=[pltpu.VMEM((width, width), F32)],
        )
        moved = lax.ppermute(inverse, "prow", [(r, r ^ 1) for r in range(n)])
        inverse = jnp.where(me & 1 != 0, moved, inverse)
        return leading, call(solve_kernel, jax.ShapeDtypeStruct((width, cols), F32), (inverse, pivot_rows))

    gathered, lower, pivot_row = lax.optimization_barrier((gathered, lower, pivot_row))
    choice = call(
        functools.partial(choice_kernel, n, rows), jax.ShapeDtypeStruct((width, n * CAP), BF16), (pivot_row,)
    )
    twins = [(r, r ^ 1) for r in range(n)]
    moved = lax.ppermute(gathered, "prow", twins)
    gathered = jnp.concatenate([gathered, moved], axis=0)
    kept, sent = split(leading)
    leading = jnp.where(me & 1 != 0, lax.ppermute(sent, "prow", twins), kept)
    leading, upper_rows = unit(me < n, levels, lower, gathered, leading, choice)
    return call(
        functools.partial(update_kernel, m),
        jax.ShapeDtypeStruct((rows, cols), F32),
        (local_rows, leading, upper_rows, slab, *tops, *rests),
        in_specs=[VMEM] * (2 * m + 4),
        out_specs=pl.BlockSpec(memory_space=pl.ANY),
        scratch=[
            pltpu.VMEM((rows + 8, cols), F32),
            pltpu.SMEM((1, 128), jnp.int32),
            pltpu.SemaphoreType.DMA((rows // width + 1,)),
        ],
    )


def solution(mesh):
    return jax.shard_map(
        functools.partial(local, mesh.shape["prow"], mesh.shape["pcol"]),
        mesh=mesh,
        in_specs=(P("prow", "pcol"), P("prow", "pcol"), P()),
        out_specs=P("prow", "pcol"),
        check_vma=False,
    )
```

```python
import functools

import jax
import jax.numpy as jnp
from jax import lax
from jax.experimental import pallas as pl
from jax.experimental.pallas import tpu as pltpu
from jax.sharding import PartitionSpec as P

CAP = 32
BLOCK = 32
F32 = jnp.float32
BF16 = jnp.bfloat16
VMEM = pl.BlockSpec(memory_space=pltpu.VMEM)
PARAMS = pltpu.CompilerParams(vmem_limit_bytes=24 * 1024 * 1024)


def split3(x):
    high = x.astype(BF16)
    rest = x - high.astype(F32)
    mid = rest.astype(BF16)
    low = (rest - mid.astype(F32)).astype(BF16)
    return high, mid, low


def split2(x):
    high = x.astype(BF16)
    return high, (x - high.astype(F32)).astype(BF16)


def select_rows(one_hot, x):
    return sum(jnp.dot(one_hot, part, preferred_element_type=F32) for part in split3(x))


def dot_full(a, b):
    high, mid, low = split3(a)
    left = jnp.concatenate([low, mid, high, mid, high, high], axis=1)
    high, mid, low = split3(b)
    right = jnp.concatenate([high, mid, low, high, mid, high], axis=0)
    return jnp.dot(left, right, preferred_element_type=F32)


def tree_partner(r, span):
    if span == 1 or r % span > 1:
        return r ^ 1
    if r % 2 == 0:
        return r + 1 if r & span else r + span
    return r - span if r & span else r - 1


def lead_place(owner, n):
    bits = n.bit_length() - 1
    return sum((lax.shift_right_logical(owner, bit) & 1) * (1 << (bits - 1 - bit)) for bit in range(bits))


def slots(pivot_row, rows):
    width = pivot_row.shape[1]
    by_sublane = jnp.broadcast_to(pivot_row, (width, width)).T
    shift = rows.bit_length() - 1
    owner_row = jnp.broadcast_to(lax.shift_right_logical(pivot_row, shift), (width, width))
    owner_col = lax.shift_right_logical(by_sublane, shift)
    sub = lax.broadcasted_iota(jnp.int32, (width, width), 0)
    lane = lax.broadcasted_iota(jnp.int32, (width, width), 1)
    same = owner_row == owner_col
    rank_row = jnp.sum(jnp.where(same & (sub < lane), 1, 0), axis=0, keepdims=True)
    rank_col = jnp.sum(jnp.where(same & (lane < sub), 1, 0), axis=1, keepdims=True)
    return owner_row[:1], rank_row, owner_col[:, :1], rank_col


def pack_kernel(pivot_ref, slab_ref, packed_ref, lead_ref, local_ref):
    rows = slab_ref.shape[0]
    width = pivot_ref.shape[1]
    count = lead_ref.shape[0]
    lanes = local_ref.shape[1]
    me = lax.axis_index("prow")
    pivot_row = pivot_ref[...]
    owner_row, rank_row, owner_col, rank_col = slots(pivot_row, rows)
    pivot_col = jnp.broadcast_to(pivot_row, (lanes, width)).T
    slot = lax.broadcasted_iota(jnp.int32, (width, lanes), 1)
    mine = (owner_col == me) & (rank_col == slot)
    local = jnp.sum(jnp.where(mine, pivot_col - (me + 1) * rows, 0), axis=0, keepdims=True) + rows
    local_ref[...] = local
    slot = lax.broadcasted_iota(jnp.int32, (CAP, width), 0)
    mine = (owner_row == me) & (rank_row == slot)
    local = jnp.sum(jnp.where(mine, pivot_row - (me + 1) * rows, 0), axis=1, keepdims=True) + rows
    one_hot = (lax.broadcasted_iota(jnp.int32, (CAP, rows), 1) == local).astype(F32).astype(BF16)
    packed_ref[...] = select_rows(one_hot, slab_ref[...])
    slot = lax.broadcasted_iota(jnp.int32, (count, width), 0)
    one_hot = (slot == lead_place(owner_row, count // CAP) * CAP + rank_row).astype(F32).astype(BF16)
    lead_ref[...] = select_rows(one_hot, slab_ref[:width, :])


def block_inverses(lower):
    width = lower.shape[0]
    lane = lax.broadcasted_iota(jnp.int32, (BLOCK, width), 1)
    sub = lax.broadcasted_iota(jnp.int32, (BLOCK, width), 0)
    block = lane // BLOCK
    within = lane % BLOCK
    diag = jnp.zeros((BLOCK, width), F32)
    for b in range(width // BLOCK):
        diag = jnp.where(block == b, lower[b * BLOCK : (b + 1) * BLOCK], diag)
    diag = jnp.where(within < sub, diag, 0.0)
    inv = jnp.where(within == sub, 1.0, 0.0).astype(F32)
    half = 128
    first = (lax.broadcasted_iota(jnp.int32, (BLOCK, half), 1) // BLOCK) * BLOCK
    outs = []
    for h in range(0, width, half):
        d, x = diag[:, h : h + half], inv[:, h : h + half]
        for k in range(BLOCK - 1):
            column = jnp.take_along_axis(d, first + k, axis=1)
            x = x - column * x[k : k + 1, :]
        outs.append(x)
    return outs


def choice_kernel(n, rows, pivot_ref, out_ref):
    _, _, owner_col, rank_col = slots(pivot_ref[...], rows)
    place = jnp.bitwise_xor(owner_col, lax.axis_index("prow")) * CAP + rank_col
    out_ref[...] = (lax.broadcasted_iota(jnp.int32, out_ref.shape, 1) == place).astype(F32).astype(BF16)


def order_kernel(choice_ref, gathered_ref, out_ref):
    out_ref[...] = select_rows(choice_ref[...], gathered_ref[...])


def top_order(m):
    return [0, 1, *range(m - 1, 1, -1)]


def cut_kernel(panel_ref, top_ref, rest_ref, sems):
    width = top_ref.shape[1]
    copies = []
    for c in range(sems.shape[0]):
        target = rest_ref.at[:, pl.ds((c - 1) * width, width)] if c else top_ref
        copies.append(pltpu.make_async_copy(panel_ref.at[:, pl.ds(c * width, width)], target, sems.at[c]))
        copies[-1].start()
    for copy in copies:
        copy.wait()


def assemble_kernel(m, *refs):
    *pieces, out_ref, lower_t = refs
    width = lower_t.shape[0]
    piece = width // m
    half = width // 2
    z = lax.axis_index("pcol")
    for d, ref in zip(top_order(m), pieces):
        lower_t[pl.ds(pl.multiple_of(jnp.bitwise_xor(z, d) * piece, piece), piece), :] = ref[...]
    out_ref[:half, :] = lower_t[:half, :]
    out_ref[half:, :half] = lower_t[half : half + half // 2, half:]
    out_ref[half:, half:] = lower_t[half + half // 2 :, half:]


def pick_kernel(span, moved_ref, held_ref, out_ref):
    child = lax.rem(lax.axis_index("prow"), 2 * span) == span

    @pl.when(child)
    def _():
        out_ref[...] = moved_ref[...]

    @pl.when(jnp.logical_not(child))
    def _():
        out_ref[...] = held_ref[...]


def invert_kernel(lower_ref, out_ref, lower_t):
    holds = lax.axis_index("prow") & 1 == 0

    @pl.when(jnp.logical_not(holds))
    def _():
        out_ref[...] = jnp.zeros_like(out_ref)

    @pl.when(holds)
    def _():
        width = lower_t.shape[0]
        half = width // 2
        lower_t[:half, :] = lower_ref[:half, :]
        lower_t[half:, :half] = jnp.zeros((half, half), F32)
        lower_t[half : half + half // 2, half:] = lower_ref[half:, :half]
        lower_t[half + half // 2 :, half:] = lower_ref[half:, half:]
        lower = lower_t[...].T
        blocks = block_inverses(lower)
        row = lax.broadcasted_iota(jnp.int32, (half, half), 0)
        col = lax.broadcasted_iota(jnp.int32, (half, half), 1)
        for h, strip in enumerate(blocks):
            corner = lower[h * half : (h + 1) * half, h * half : (h + 1) * half]
            inv = jnp.where(row // BLOCK == col // BLOCK, jnp.concatenate([strip] * (half // BLOCK), axis=0), 0.0)
            size = BLOCK
            while size < half:
                off = (row // (2 * size) == col // (2 * size)) & (row // size > col // size)
                inv = inv - dot_full(dot_full(inv, jnp.where(off, corner, 0.0)), inv)
                size *= 2
            out_ref[:half, h * half : (h + 1) * half] = inv
        first, second = out_ref[:half, :half], out_ref[:half, half:]
        quarter = -dot_full(dot_full(second, lower[half:, :half]), first)
        out_ref[half:, :half] = quarter[: half // 2]
        out_ref[half:, half:] = quarter[half // 2 :]


def solve_kernel(inverse_ref, pivot_rows_ref, x_ref):
    half = pivot_rows_ref.shape[0] // 2
    quarter = jnp.concatenate([inverse_ref[half:, :half], inverse_ref[half:, half:]], axis=0)
    lower_half = jnp.concatenate([quarter, inverse_ref[:half, half:]], axis=1)
    x_ref[:half, :] = dot_full(inverse_ref[:half, :half], pivot_rows_ref[:half, :])
    x_ref[half:, :] = dot_full(lower_half, pivot_rows_ref[...])


def product(pieces, upper):
    high, low = zip(*(split2(piece) for piece in pieces))
    high, low = jnp.concatenate(high, axis=0), jnp.concatenate(low, axis=0)
    upper_high, upper_low = upper
    width = upper_high.shape[1]

    def dot(a, b):
        return lax.dot_general(a, b, (((0,), (0,)), ((), ())), preferred_element_type=F32)

    both = dot(high, jnp.concatenate([upper_high, upper_low], axis=1))
    return both[:, :width] + (both[:, width:] + dot(low, upper_high))


def piece_rows(x_ref, m, d):
    piece = x_ref.shape[0] // m
    source = jnp.bitwise_xor(lax.axis_index("pcol"), d)
    return x_ref[pl.ds(pl.multiple_of(source * piece, piece), piece), :]


def update_kernel(m, local_ref, lead_ref, x_ref, slab_ref, *refs):
    *pieces, out_ref, result, swaps, sems = refs
    tops, rests = pieces[:m], pieces[m:]
    rows = slab_ref.shape[0]
    width = x_ref.shape[0]
    blocks = rows // width
    fetch = pltpu.make_async_copy(local_ref, swaps, sems.at[blocks])
    fetch.start()
    result[:rows, :] = slab_ref[...]
    top_upper = split2(jnp.concatenate([piece_rows(x_ref, m, d) for d in top_order(m)], axis=0))
    upper = split2(jnp.concatenate([piece_rows(x_ref, m, d) for d in range(m)], axis=0))
    copies = []
    for c in range(blocks):
        part = pl.ds(c * width, width)
        if c:
            total = product([rest[:, (c - 1) * width : c * width] for rest in rests], upper)
        else:
            total = product([top[...] for top in tops], top_upper)
            fetch.wait()
            for s in range(CAP):
                result[pl.ds(swaps[0, s], 1), :] = lead_ref[pl.ds(s, 1), :]
        result[part, :] = result[part, :] - total
        if c == 0:

            @pl.when(lax.axis_index("prow") == 0)
            def _():
                result[part, :] = x_ref[...]

        copy = pltpu.make_async_copy(result.at[part], out_ref.at[part], sems.at[c])
        copy.start()
        copies.append(copy)
    for copy in copies:
        copy.wait()


def unit(held, steps, *operands):
    shapes = jax.eval_shape(steps, *operands)
    return lax.cond(held, steps, lambda *_: jax.tree.map(lambda s: jnp.zeros(s.shape, s.dtype), shapes), *operands)


def call(kernel, outs, operands, in_specs=None, out_specs=None, scratch=()):
    return pl.pallas_call(
        kernel,
        out_shape=outs,
        in_specs=in_specs or [VMEM] * len(operands),
        out_specs=out_specs or jax.tree.map(lambda _: VMEM, outs),
        scratch_shapes=list(scratch),
        compiler_params=PARAMS,
        cost_estimate=pl.CostEstimate(flops=1, bytes_accessed=1, transcendentals=0),
    )(*operands)


def local(n, m, slab, panel, pivots):
    rows, cols = slab.shape
    width = pivots.shape[0]
    piece = panel.shape[1]
    me = lax.axis_index("prow")
    panel_t = panel.T
    pivot_row = pivots.reshape(1, width)

    def exchange(block, d):
        return lax.ppermute(block, "pcol", [(c, c ^ d) for c in range(m)])

    top, rest = call(
        cut_kernel,
        (jax.ShapeDtypeStruct((piece, width), F32), jax.ShapeDtypeStruct((piece, rows - width), F32)),
        (panel_t,),
        in_specs=[pl.BlockSpec(memory_space=pl.ANY)],
        scratch=[pltpu.SemaphoreType.DMA((rows // width,))],
    )
    tops = [top] + [exchange(top, d) for d in top_order(m)[1:]]
    rests = [rest] + [exchange(rest, d) for d in range(1, m)]

    gathered, leading, local_rows = call(
        pack_kernel,
        (
            jax.ShapeDtypeStruct((CAP, cols), F32),
            jax.ShapeDtypeStruct((n * CAP, cols), F32),
            jax.ShapeDtypeStruct((1, 128), jnp.int32),
        ),
        (pivot_row, slab),
    )
    lower = call(
        functools.partial(assemble_kernel, m),
        jax.ShapeDtypeStruct((width * 3 // 4, width), F32),
        tops,
        scratch=[pltpu.VMEM((width, width), F32)],
    )

    def split(leading):
        blocks = leading.reshape(2, -1, cols)
        return blocks[0], blocks[1]

    def levels(lower, gathered, leading, choice):
        span, other, held = n // 2, 2, lower
        while span > 1:
            moved = lax.ppermute(lower, "prow", [(r, tree_partner(r, span)) for r in range(n)])
            lower = call(
                functools.partial(pick_kernel, span),
                jax.ShapeDtypeStruct(lower.shape, F32),
                (moved, held),
            )
            kept, sent = split(leading)
            count = gathered.shape[0]
            message = jnp.concatenate([gathered, sent], axis=0)
            moved = lax.ppermute(message, "prow", [(r, r ^ other) for r in range(n)])
            moved, held = lax.optimization_barrier((moved, lower))
            gathered = jnp.concatenate([gathered, moved[:count]], axis=0)
            leading = jnp.where(me & other != 0, moved[count:], kept)
            span, other = span // 2, other * 2
        pivot_rows = call(order_kernel, jax.ShapeDtypeStruct((width, cols), F32), (choice, gathered))
        inverse = call(
            invert_kernel,
            jax.ShapeDtypeStruct(lower.shape, F32),
            (lower,),
            scratch=[pltpu.VMEM((width, width), F32)],
        )
        moved = lax.ppermute(inverse, "prow", [(r, r ^ 1) for r in range(n)])
        inverse = jnp.where(me & 1 != 0, moved, inverse)
        return leading, call(solve_kernel, jax.ShapeDtypeStruct((width, cols), F32), (inverse, pivot_rows))

    gathered, lower, pivot_row = lax.optimization_barrier((gathered, lower, pivot_row))
    choice = call(
        functools.partial(choice_kernel, n, rows), jax.ShapeDtypeStruct((width, n * CAP), BF16), (pivot_row,)
    )
    twins = [(r, r ^ 1) for r in range(n)]
    moved = lax.ppermute(gathered, "prow", twins)
    gathered = jnp.concatenate([gathered, moved], axis=0)
    kept, sent = split(leading)
    leading = jnp.where(me & 1 != 0, lax.ppermute(sent, "prow", twins), kept)
    leading, upper_rows = unit(me < n, levels, lower, gathered, leading, choice)
    return call(
        functools.partial(update_kernel, m),
        jax.ShapeDtypeStruct((rows, cols), F32),
        (local_rows, leading, upper_rows, slab, *tops, *rests),
        in_specs=[VMEM] * (2 * m + 4),
        out_specs=pl.BlockSpec(memory_space=pl.ANY),
        scratch=[
            pltpu.VMEM((rows + 8, cols), F32),
            pltpu.SMEM((1, 128), jnp.int32),
            pltpu.SemaphoreType.DMA((rows // width + 1,)),
        ],
    )


def solution(mesh):
    return jax.shard_map(
        functools.partial(local, mesh.shape["prow"], mesh.shape["pcol"]),
        mesh=mesh,
        in_specs=(P("prow", "pcol"), P("prow", "pcol"), P()),
        out_specs=P("prow", "pcol"),
        check_vma=False,
    )
```

```python
import functools

import jax
import jax.numpy as jnp
from jax import lax
from jax.experimental import pallas as pl
from jax.experimental.pallas import tpu as pltpu
from jax.sharding import PartitionSpec as P

CAP = 32
BLOCK = 32
F32 = jnp.float32
BF16 = jnp.bfloat16
VMEM = pl.BlockSpec(memory_space=pltpu.VMEM)
PARAMS = pltpu.CompilerParams(vmem_limit_bytes=24 * 1024 * 1024)


def split3(x):
    high = x.astype(BF16)
    rest = x - high.astype(F32)
    mid = rest.astype(BF16)
    low = (rest - mid.astype(F32)).astype(BF16)
    return high, mid, low


def split2(x):
    high = x.astype(BF16)
    return high, (x - high.astype(F32)).astype(BF16)


def select_rows(one_hot, x):
    return sum(jnp.dot(one_hot, part, preferred_element_type=F32) for part in split3(x))


def dot_full(a, b):
    high, mid, low = split3(a)
    left = jnp.concatenate([low, mid, high, mid, high, high], axis=1)
    high, mid, low = split3(b)
    right = jnp.concatenate([high, mid, low, high, mid, high], axis=0)
    return jnp.dot(left, right, preferred_element_type=F32)


def tree_partner(r, span):
    if span == 1 or r % span > 1:
        return r ^ 1
    if r % 2 == 0:
        return r + 1 if r & span else r + span
    return r - span if r & span else r - 1


def lead_place(owner, n):
    bits = n.bit_length() - 1
    return sum((lax.shift_right_logical(owner, bit) & 1) * (1 << (bits - 1 - bit)) for bit in range(bits))


def slots(pivot_row, rows):
    width = pivot_row.shape[1]
    by_sublane = jnp.broadcast_to(pivot_row, (width, width)).T
    shift = rows.bit_length() - 1
    owner_row = jnp.broadcast_to(lax.shift_right_logical(pivot_row, shift), (width, width))
    owner_col = lax.shift_right_logical(by_sublane, shift)
    sub = lax.broadcasted_iota(jnp.int32, (width, width), 0)
    lane = lax.broadcasted_iota(jnp.int32, (width, width), 1)
    same = owner_row == owner_col
    rank_row = jnp.sum(jnp.where(same & (sub < lane), 1, 0), axis=0, keepdims=True)
    rank_col = jnp.sum(jnp.where(same & (lane < sub), 1, 0), axis=1, keepdims=True)
    return owner_row[:1], rank_row, owner_col[:, :1], rank_col


def pack_kernel(pivot_ref, slab_ref, packed_ref, lead_ref, local_ref):
    rows = slab_ref.shape[0]
    width = pivot_ref.shape[1]
    count = lead_ref.shape[0]
    lanes = local_ref.shape[1]
    me = lax.axis_index("prow")
    pivot_row = pivot_ref[...]
    owner_row, rank_row, owner_col, rank_col = slots(pivot_row, rows)
    pivot_col = jnp.broadcast_to(pivot_row, (lanes, width)).T
    slot = lax.broadcasted_iota(jnp.int32, (width, lanes), 1)
    mine = (owner_col == me) & (rank_col == slot)
    local = jnp.sum(jnp.where(mine, pivot_col - (me + 1) * rows, 0), axis=0, keepdims=True) + rows
    local_ref[...] = local
    slot = lax.broadcasted_iota(jnp.int32, (CAP, width), 0)
    mine = (owner_row == me) & (rank_row == slot)
    local = jnp.sum(jnp.where(mine, pivot_row - (me + 1) * rows, 0), axis=1, keepdims=True) + rows
    one_hot = (lax.broadcasted_iota(jnp.int32, (CAP, rows), 1) == local).astype(F32).astype(BF16)
    packed_ref[...] = select_rows(one_hot, slab_ref[...])
    slot = lax.broadcasted_iota(jnp.int32, (count, width), 0)
    one_hot = (slot == lead_place(owner_row, count // CAP) * CAP + rank_row).astype(F32).astype(BF16)
    lead_ref[...] = select_rows(one_hot, slab_ref[:width, :])


def block_inverses(lower):
    width = lower.shape[0]
    lane = lax.broadcasted_iota(jnp.int32, (BLOCK, width), 1)
    sub = lax.broadcasted_iota(jnp.int32, (BLOCK, width), 0)
    block = lane // BLOCK
    within = lane % BLOCK
    diag = jnp.zeros((BLOCK, width), F32)
    for b in range(width // BLOCK):
        diag = jnp.where(block == b, lower[b * BLOCK : (b + 1) * BLOCK], diag)
    diag = jnp.where(within < sub, diag, 0.0)
    inv = jnp.where(within == sub, 1.0, 0.0).astype(F32)
    half = 128
    first = (lax.broadcasted_iota(jnp.int32, (BLOCK, half), 1) // BLOCK) * BLOCK
    outs = []
    for h in range(0, width, half):
        d, x = diag[:, h : h + half], inv[:, h : h + half]
        for k in range(BLOCK - 1):
            column = jnp.take_along_axis(d, first + k, axis=1)
            x = x - column * x[k : k + 1, :]
        outs.append(x)
    return outs


def choice_kernel(n, rows, pivot_ref, out_ref):
    _, _, owner_col, rank_col = slots(pivot_ref[...], rows)
    place = jnp.bitwise_xor(owner_col, lax.axis_index("prow")) * CAP + rank_col
    out_ref[...] = (lax.broadcasted_iota(jnp.int32, out_ref.shape, 1) == place).astype(F32).astype(BF16)


def order_kernel(choice_ref, gathered_ref, out_ref):
    out_ref[...] = select_rows(choice_ref[...], gathered_ref[...])


def top_order(m):
    return [0, 1, *range(m - 1, 1, -1)]


def cut_kernel(panel_ref, top_ref, rest_ref, sems):
    width = top_ref.shape[1]
    copies = []
    for c in range(sems.shape[0]):
        target = rest_ref.at[:, pl.ds((c - 1) * width, width)] if c else top_ref
        copies.append(pltpu.make_async_copy(panel_ref.at[:, pl.ds(c * width, width)], target, sems.at[c]))
        copies[-1].start()
    for copy in copies:
        copy.wait()


def assemble_kernel(m, *refs):
    *pieces, out_ref, lower_t = refs
    width = lower_t.shape[0]
    piece = width // m
    half = width // 2
    z = lax.axis_index("pcol")
    for d, ref in zip(top_order(m), pieces):
        lower_t[pl.ds(pl.multiple_of(jnp.bitwise_xor(z, d) * piece, piece), piece), :] = ref[...]
    out_ref[:half, :] = lower_t[:half, :]
    out_ref[half:, :half] = lower_t[half : half + half // 2, half:]
    out_ref[half:, half:] = lower_t[half + half // 2 :, half:]


def pick_kernel(span, moved_ref, held_ref, out_ref):
    child = lax.rem(lax.axis_index("prow"), 2 * span) == span

    @pl.when(child)
    def _():
        out_ref[...] = moved_ref[...]

    @pl.when(jnp.logical_not(child))
    def _():
        out_ref[...] = held_ref[...]


def invert_kernel(lower_ref, out_ref, lower_t):
    holds = lax.axis_index("prow") & 1 == 0

    @pl.when(jnp.logical_not(holds))
    def _():
        out_ref[...] = jnp.zeros_like(out_ref)

    @pl.when(holds)
    def _():
        width = lower_t.shape[0]
        half = width // 2
        lower_t[:half, :] = lower_ref[:half, :]
        lower_t[half:, :half] = jnp.zeros((half, half), F32)
        lower_t[half : half + half // 2, half:] = lower_ref[half:, :half]
        lower_t[half + half // 2 :, half:] = lower_ref[half:, half:]
        lower = lower_t[...].T
        blocks = block_inverses(lower)
        row = lax.broadcasted_iota(jnp.int32, (half, half), 0)
        col = lax.broadcasted_iota(jnp.int32, (half, half), 1)
        for h, strip in enumerate(blocks):
            corner = lower[h * half : (h + 1) * half, h * half : (h + 1) * half]
            inv = jnp.where(row // BLOCK == col // BLOCK, jnp.concatenate([strip] * (half // BLOCK), axis=0), 0.0)
            size = BLOCK
            while size < half:
                off = (row // (2 * size) == col // (2 * size)) & (row // size > col // size)
                inv = inv - dot_full(dot_full(inv, jnp.where(off, corner, 0.0)), inv)
                size *= 2
            out_ref[:half, h * half : (h + 1) * half] = inv
        first, second = out_ref[:half, :half], out_ref[:half, half:]
        quarter = -dot_full(dot_full(second, lower[half:, :half]), first)
        out_ref[half:, :half] = quarter[: half // 2]
        out_ref[half:, half:] = quarter[half // 2 :]


def solve_kernel(inverse_ref, pivot_rows_ref, x_ref):
    half = pivot_rows_ref.shape[0] // 2
    quarter = jnp.concatenate([inverse_ref[half:, :half], inverse_ref[half:, half:]], axis=0)
    lower_half = jnp.concatenate([quarter, inverse_ref[:half, half:]], axis=1)
    x_ref[:half, :] = dot_full(inverse_ref[:half, :half], pivot_rows_ref[:half, :])
    x_ref[half:, :] = dot_full(lower_half, pivot_rows_ref[...])


def product(pieces, upper):
    high, low = zip(*(split2(piece) for piece in pieces))
    high, low = jnp.concatenate(high, axis=0), jnp.concatenate(low, axis=0)
    upper_high, upper_low = upper
    width = upper_high.shape[1]

    def dot(a, b):
        return lax.dot_general(a, b, (((0,), (0,)), ((), ())), preferred_element_type=F32)

    both = dot(high, jnp.concatenate([upper_high, upper_low], axis=1))
    return both[:, :width] + (both[:, width:] + dot(low, upper_high))


def piece_rows(x_ref, m, d):
    piece = x_ref.shape[0] // m
    source = jnp.bitwise_xor(lax.axis_index("pcol"), d)
    return x_ref[pl.ds(pl.multiple_of(source * piece, piece), piece), :]


def update_kernel(m, local_ref, lead_ref, x_ref, slab_ref, *refs):
    *pieces, out_ref, result, swaps, sems = refs
    tops, rests = pieces[:m], pieces[m:]
    rows = slab_ref.shape[0]
    width = x_ref.shape[0]
    blocks = rows // width
    fetch = pltpu.make_async_copy(local_ref, swaps, sems.at[blocks + 1])
    fetch.start()
    result[:rows, :] = slab_ref[...]
    top_upper = split2(jnp.concatenate([piece_rows(x_ref, m, d) for d in top_order(m)], axis=0))
    upper = split2(jnp.concatenate([piece_rows(x_ref, m, d) for d in range(m)], axis=0))
    copies = []
    starts = [*range(0, rows, width), rows - width // 2, rows]
    for c, (start, stop) in enumerate(zip(starts, starts[1:])):
        part = pl.ds(start, stop - start)
        if c:
            total = product([rest[:, start - width : stop - width] for rest in rests], upper)
        else:
            total = product([top[...] for top in tops], top_upper)
            fetch.wait()
            for s in range(CAP):
                result[pl.ds(swaps[0, s], 1), :] = lead_ref[pl.ds(s, 1), :]
        result[part, :] = result[part, :] - total
        if c == 0:

            @pl.when(lax.axis_index("prow") == 0)
            def _():
                result[part, :] = x_ref[...]

        copy = pltpu.make_async_copy(result.at[part], out_ref.at[part], sems.at[c])
        copy.start()
        copies.append(copy)
    for copy in copies:
        copy.wait()


def unit(held, steps, *operands):
    shapes = jax.eval_shape(steps, *operands)
    return lax.cond(held, steps, lambda *_: jax.tree.map(lambda s: jnp.zeros(s.shape, s.dtype), shapes), *operands)


def call(kernel, outs, operands, in_specs=None, out_specs=None, scratch=()):
    return pl.pallas_call(
        kernel,
        out_shape=outs,
        in_specs=in_specs or [VMEM] * len(operands),
        out_specs=out_specs or jax.tree.map(lambda _: VMEM, outs),
        scratch_shapes=list(scratch),
        compiler_params=PARAMS,
        cost_estimate=pl.CostEstimate(flops=1, bytes_accessed=1, transcendentals=0),
    )(*operands)


def local(n, m, slab, panel, pivots):
    rows, cols = slab.shape
    width = pivots.shape[0]
    piece = panel.shape[1]
    me = lax.axis_index("prow")
    panel_t = panel.T
    pivot_row = pivots.reshape(1, width)

    def exchange(block, d):
        return lax.ppermute(block, "pcol", [(c, c ^ d) for c in range(m)])

    top, rest = call(
        cut_kernel,
        (jax.ShapeDtypeStruct((piece, width), F32), jax.ShapeDtypeStruct((piece, rows - width), F32)),
        (panel_t,),
        in_specs=[pl.BlockSpec(memory_space=pl.ANY)],
        scratch=[pltpu.SemaphoreType.DMA((rows // width,))],
    )
    tops = [top] + [exchange(top, d) for d in top_order(m)[1:]]
    rests = [rest] + [exchange(rest, d) for d in range(1, m)]

    gathered, leading, local_rows = call(
        pack_kernel,
        (
            jax.ShapeDtypeStruct((CAP, cols), F32),
            jax.ShapeDtypeStruct((n * CAP, cols), F32),
            jax.ShapeDtypeStruct((1, 128), jnp.int32),
        ),
        (pivot_row, slab),
    )
    lower = call(
        functools.partial(assemble_kernel, m),
        jax.ShapeDtypeStruct((width * 3 // 4, width), F32),
        tops,
        scratch=[pltpu.VMEM((width, width), F32)],
    )

    def split(leading):
        blocks = leading.reshape(2, -1, cols)
        return blocks[0], blocks[1]

    def levels(lower, gathered, leading, choice):
        span, other, held = n // 2, 2, lower
        while span > 1:
            moved = lax.ppermute(lower, "prow", [(r, tree_partner(r, span)) for r in range(n)])
            lower = call(
                functools.partial(pick_kernel, span),
                jax.ShapeDtypeStruct(lower.shape, F32),
                (moved, held),
            )
            kept, sent = split(leading)
            count = gathered.shape[0]
            message = jnp.concatenate([gathered, sent], axis=0)
            moved = lax.ppermute(message, "prow", [(r, r ^ other) for r in range(n)])
            moved, held = lax.optimization_barrier((moved, lower))
            gathered = jnp.concatenate([gathered, moved[:count]], axis=0)
            leading = jnp.where(me & other != 0, moved[count:], kept)
            span, other = span // 2, other * 2
        pivot_rows = call(order_kernel, jax.ShapeDtypeStruct((width, cols), F32), (choice, gathered))
        inverse = call(
            invert_kernel,
            jax.ShapeDtypeStruct(lower.shape, F32),
            (lower,),
            scratch=[pltpu.VMEM((width, width), F32)],
        )
        moved = lax.ppermute(inverse, "prow", [(r, r ^ 1) for r in range(n)])
        inverse = jnp.where(me & 1 != 0, moved, inverse)
        return leading, call(solve_kernel, jax.ShapeDtypeStruct((width, cols), F32), (inverse, pivot_rows))

    gathered, lower, pivot_row = lax.optimization_barrier((gathered, lower, pivot_row))
    choice = call(
        functools.partial(choice_kernel, n, rows), jax.ShapeDtypeStruct((width, n * CAP), BF16), (pivot_row,)
    )
    twins = [(r, r ^ 1) for r in range(n)]
    moved = lax.ppermute(gathered, "prow", twins)
    gathered = jnp.concatenate([gathered, moved], axis=0)
    kept, sent = split(leading)
    leading = jnp.where(me & 1 != 0, lax.ppermute(sent, "prow", twins), kept)
    leading, upper_rows = unit(me < n, levels, lower, gathered, leading, choice)
    return call(
        functools.partial(update_kernel, m),
        jax.ShapeDtypeStruct((rows, cols), F32),
        (local_rows, leading, upper_rows, slab, *tops, *rests),
        in_specs=[VMEM] * (2 * m + 4),
        out_specs=pl.BlockSpec(memory_space=pl.ANY),
        scratch=[
            pltpu.VMEM((rows + 8, cols), F32),
            pltpu.SMEM((1, 128), jnp.int32),
            pltpu.SemaphoreType.DMA((rows // width + 2,)),
        ],
    )


def solution(mesh):
    return jax.shard_map(
        functools.partial(local, mesh.shape["prow"], mesh.shape["pcol"]),
        mesh=mesh,
        in_specs=(P("prow", "pcol"), P("prow", "pcol"), P()),
        out_specs=P("prow", "pcol"),
        check_vma=False,
    )
```

```python
import functools

import jax
import jax.numpy as jnp
from jax import lax
from jax.experimental import pallas as pl
from jax.experimental.pallas import tpu as pltpu
from jax.sharding import PartitionSpec as P

CAP = 32
BLOCK = 32
F32 = jnp.float32
BF16 = jnp.bfloat16
VMEM = pl.BlockSpec(memory_space=pltpu.VMEM)
PARAMS = pltpu.CompilerParams(vmem_limit_bytes=24 * 1024 * 1024)


def split3(x):
    high = x.astype(BF16)
    rest = x - high.astype(F32)
    mid = rest.astype(BF16)
    low = (rest - mid.astype(F32)).astype(BF16)
    return high, mid, low


def split2(x):
    high = x.astype(BF16)
    return high, (x - high.astype(F32)).astype(BF16)


def select_rows(one_hot, x):
    return sum(jnp.dot(one_hot, part, preferred_element_type=F32) for part in split3(x))


def dot_full(a, b):
    high, mid, low = split3(a)
    left = jnp.concatenate([low, mid, high, mid, high, high], axis=1)
    high, mid, low = split3(b)
    right = jnp.concatenate([high, mid, low, high, mid, high], axis=0)
    return jnp.dot(left, right, preferred_element_type=F32)


def tree_partner(r, span):
    if span == 1 or r % span > 1:
        return r ^ 1
    if r % 2 == 0:
        return r + 1 if r & span else r + span
    return r - span if r & span else r - 1


def lead_place(owner, n):
    bits = n.bit_length() - 1
    return sum((lax.shift_right_logical(owner, bit) & 1) * (1 << (bits - 1 - bit)) for bit in range(bits))


def slots(pivot_row, rows):
    width = pivot_row.shape[1]
    by_sublane = jnp.broadcast_to(pivot_row, (width, width)).T
    shift = rows.bit_length() - 1
    owner_row = jnp.broadcast_to(lax.shift_right_logical(pivot_row, shift), (width, width))
    owner_col = lax.shift_right_logical(by_sublane, shift)
    sub = lax.broadcasted_iota(jnp.int32, (width, width), 0)
    lane = lax.broadcasted_iota(jnp.int32, (width, width), 1)
    same = owner_row == owner_col
    rank_row = jnp.sum(jnp.where(same & (sub < lane), 1, 0), axis=0, keepdims=True)
    rank_col = jnp.sum(jnp.where(same & (lane < sub), 1, 0), axis=1, keepdims=True)
    return owner_row[:1], rank_row, owner_col[:, :1], rank_col


def pack_kernel(pivot_ref, slab_ref, packed_ref, lead_ref, local_ref):
    rows = slab_ref.shape[0]
    width = pivot_ref.shape[1]
    count = lead_ref.shape[0]
    lanes = local_ref.shape[1]
    me = lax.axis_index("prow")
    pivot_row = pivot_ref[...]
    owner_row, rank_row, owner_col, rank_col = slots(pivot_row, rows)
    pivot_col = jnp.broadcast_to(pivot_row, (lanes, width)).T
    slot = lax.broadcasted_iota(jnp.int32, (width, lanes), 1)
    mine = (owner_col == me) & (rank_col == slot)
    local = jnp.sum(jnp.where(mine, pivot_col - (me + 1) * rows, 0), axis=0, keepdims=True) + rows
    local_ref[...] = local
    slot = lax.broadcasted_iota(jnp.int32, (CAP, width), 0)
    mine = (owner_row == me) & (rank_row == slot)
    local = jnp.sum(jnp.where(mine, pivot_row - (me + 1) * rows, 0), axis=1, keepdims=True) + rows
    one_hot = (lax.broadcasted_iota(jnp.int32, (CAP, rows), 1) == local).astype(F32).astype(BF16)
    packed_ref[...] = select_rows(one_hot, slab_ref[...])
    slot = lax.broadcasted_iota(jnp.int32, (count, width), 0)
    one_hot = (slot == lead_place(owner_row, count // CAP) * CAP + rank_row).astype(F32).astype(BF16)
    lead_ref[...] = select_rows(one_hot, slab_ref[:width, :])


def block_inverses(lower):
    width = lower.shape[0]
    lane = lax.broadcasted_iota(jnp.int32, (BLOCK, width), 1)
    sub = lax.broadcasted_iota(jnp.int32, (BLOCK, width), 0)
    block = lane // BLOCK
    within = lane % BLOCK
    diag = jnp.zeros((BLOCK, width), F32)
    for b in range(width // BLOCK):
        diag = jnp.where(block == b, lower[b * BLOCK : (b + 1) * BLOCK], diag)
    diag = jnp.where(within < sub, diag, 0.0)
    inv = jnp.where(within == sub, 1.0, 0.0).astype(F32)
    half = 128
    first = (lax.broadcasted_iota(jnp.int32, (BLOCK, half), 1) // BLOCK) * BLOCK
    outs = []
    for h in range(0, width, half):
        d, x = diag[:, h : h + half], inv[:, h : h + half]
        for k in range(BLOCK - 1):
            column = jnp.take_along_axis(d, first + k, axis=1)
            x = x - column * x[k : k + 1, :]
        outs.append(x)
    return outs


def choice_kernel(n, rows, pivot_ref, out_ref):
    _, _, owner_col, rank_col = slots(pivot_ref[...], rows)
    place = jnp.bitwise_xor(owner_col, lax.axis_index("prow")) * CAP + rank_col
    out_ref[...] = (lax.broadcasted_iota(jnp.int32, out_ref.shape, 1) == place).astype(F32).astype(BF16)


def order_kernel(choice_ref, gathered_ref, out_ref):
    out_ref[...] = select_rows(choice_ref[...], gathered_ref[...])


def top_order(m):
    even = [0, 1, *range(m - 1, 1, -1)]
    return list(zip(even, [0, even[-1], *even[1:-1]]))


def cut_kernel(panel_ref, top_ref, rest_ref, sems):
    width = top_ref.shape[1]
    copies = []
    for c in range(sems.shape[0]):
        target = rest_ref.at[:, pl.ds((c - 1) * width, width)] if c else top_ref
        copies.append(pltpu.make_async_copy(panel_ref.at[:, pl.ds(c * width, width)], target, sems.at[c]))
        copies[-1].start()
    for copy in copies:
        copy.wait()


def assemble_kernel(m, *refs):
    *pieces, out_ref, lower_t = refs
    width = lower_t.shape[0]
    piece = width // m
    half = width // 2
    z = lax.axis_index("pcol")
    for (d, _), ref in zip(top_order(m), pieces):
        lower_t[pl.ds(pl.multiple_of(jnp.bitwise_xor(z, d) * piece, piece), piece), :] = ref[...]
    out_ref[:half, :] = lower_t[:half, :]
    out_ref[half:, :half] = lower_t[half : half + half // 2, half:]
    out_ref[half:, half:] = lower_t[half + half // 2 :, half:]


def pick_kernel(span, moved_ref, held_ref, out_ref):
    child = lax.rem(lax.axis_index("prow"), 2 * span) == span

    @pl.when(child)
    def _():
        out_ref[...] = moved_ref[...]

    @pl.when(jnp.logical_not(child))
    def _():
        out_ref[...] = held_ref[...]


def invert_kernel(lower_ref, out_ref, lower_t):
    holds = lax.axis_index("prow") & 1 == 0

    @pl.when(jnp.logical_not(holds))
    def _():
        out_ref[...] = jnp.zeros_like(out_ref)

    @pl.when(holds)
    def _():
        width = lower_t.shape[0]
        half = width // 2
        lower_t[:half, :] = lower_ref[:half, :]
        lower_t[half:, :half] = jnp.zeros((half, half), F32)
        lower_t[half : half + half // 2, half:] = lower_ref[half:, :half]
        lower_t[half + half // 2 :, half:] = lower_ref[half:, half:]
        lower = lower_t[...].T
        blocks = block_inverses(lower)
        row = lax.broadcasted_iota(jnp.int32, (half, half), 0)
        col = lax.broadcasted_iota(jnp.int32, (half, half), 1)
        for h, strip in enumerate(blocks):
            corner = lower[h * half : (h + 1) * half, h * half : (h + 1) * half]
            inv = jnp.where(row // BLOCK == col // BLOCK, jnp.concatenate([strip] * (half // BLOCK), axis=0), 0.0)
            size = BLOCK
            while size < half:
                off = (row // (2 * size) == col // (2 * size)) & (row // size > col // size)
                inv = inv - dot_full(dot_full(inv, jnp.where(off, corner, 0.0)), inv)
                size *= 2
            out_ref[:half, h * half : (h + 1) * half] = inv
        first, second = out_ref[:half, :half], out_ref[:half, half:]
        quarter = -dot_full(dot_full(second, lower[half:, :half]), first)
        out_ref[half:, :half] = quarter[: half // 2]
        out_ref[half:, half:] = quarter[half // 2 :]


def solve_kernel(inverse_ref, pivot_rows_ref, x_ref):
    half = pivot_rows_ref.shape[0] // 2
    quarter = jnp.concatenate([inverse_ref[half:, :half], inverse_ref[half:, half:]], axis=0)
    lower_half = jnp.concatenate([quarter, inverse_ref[:half, half:]], axis=1)
    x_ref[:half, :] = dot_full(inverse_ref[:half, :half], pivot_rows_ref[:half, :])
    x_ref[half:, :] = dot_full(lower_half, pivot_rows_ref[...])


def product(pieces, upper):
    high, low = zip(*(split2(piece) for piece in pieces))
    high, low = jnp.concatenate(high, axis=0), jnp.concatenate(low, axis=0)
    upper_high, upper_low = upper
    width = upper_high.shape[1]

    def dot(a, b):
        return lax.dot_general(a, b, (((0,), (0,)), ((), ())), preferred_element_type=F32)

    both = dot(high, jnp.concatenate([upper_high, upper_low], axis=1))
    return both[:, :width] + (both[:, width:] + dot(low, upper_high))


def piece_rows(x_ref, m, d):
    piece = x_ref.shape[0] // m
    source = jnp.bitwise_xor(lax.axis_index("pcol"), d)
    return x_ref[pl.ds(pl.multiple_of(source * piece, piece), piece), :]


def update_kernel(m, local_ref, lead_ref, x_ref, slab_ref, *refs):
    *pieces, out_ref, result, swaps, sems = refs
    tops, rests = pieces[:m], pieces[m:]
    rows = slab_ref.shape[0]
    width = x_ref.shape[0]
    blocks = rows // width
    fetch = pltpu.make_async_copy(local_ref, swaps, sems.at[blocks])
    fetch.start()
    result[:rows, :] = slab_ref[...]
    odd = lax.axis_index("prow") & 1 != 0
    top_upper = split2(
        jnp.concatenate([piece_rows(x_ref, m, jnp.where(odd, d, e)) for e, d in top_order(m)], axis=0)
    )
    upper = split2(jnp.concatenate([piece_rows(x_ref, m, d) for d in range(m)], axis=0))
    copies = []
    for c in range(blocks):
        part = pl.ds(c * width, width)
        if c:
            total = product([rest[:, (c - 1) * width : c * width] for rest in rests], upper)
        else:
            total = product([top[...] for top in tops], top_upper)
            fetch.wait()
            for s in range(CAP):
                result[pl.ds(swaps[0, s], 1), :] = lead_ref[pl.ds(s, 1), :]
        result[part, :] = result[part, :] - total
        if c == 0:

            @pl.when(lax.axis_index("prow") == 0)
            def _():
                result[part, :] = x_ref[...]

        copy = pltpu.make_async_copy(result.at[part], out_ref.at[part], sems.at[c])
        copy.start()
        copies.append(copy)
    for copy in copies:
        copy.wait()


def unit(held, steps, *operands):
    shapes = jax.eval_shape(steps, *operands)
    return lax.cond(held, steps, lambda *_: jax.tree.map(lambda s: jnp.zeros(s.shape, s.dtype), shapes), *operands)


def call(kernel, outs, operands, in_specs=None, out_specs=None, scratch=()):
    return pl.pallas_call(
        kernel,
        out_shape=outs,
        in_specs=in_specs or [VMEM] * len(operands),
        out_specs=out_specs or jax.tree.map(lambda _: VMEM, outs),
        scratch_shapes=list(scratch),
        compiler_params=PARAMS,
        cost_estimate=pl.CostEstimate(flops=1, bytes_accessed=1, transcendentals=0),
    )(*operands)


def local(n, m, slab, panel, pivots):
    rows, cols = slab.shape
    width = pivots.shape[0]
    piece = panel.shape[1]
    me = lax.axis_index("prow")
    panel_t = panel.T
    pivot_row = pivots.reshape(1, width)

    def exchange(block, d):
        return lax.ppermute(block, "pcol", [(c, c ^ d) for c in range(m)])

    top, rest = call(
        cut_kernel,
        (jax.ShapeDtypeStruct((piece, width), F32), jax.ShapeDtypeStruct((piece, rows - width), F32)),
        (panel_t,),
        in_specs=[pl.BlockSpec(memory_space=pl.ANY)],
        scratch=[pltpu.SemaphoreType.DMA((rows // width,))],
    )
    tops = [top]
    for by_parity in top_order(m)[1:]:
        pairs = [(r * m + c, r * m + (c ^ by_parity[r & 1])) for r in range(n) for c in range(m)]
        tops.append(lax.ppermute(top, ("prow", "pcol"), pairs))
    rests = [rest] + [exchange(rest, d) for d in range(1, m)]

    gathered, leading, local_rows = call(
        pack_kernel,
        (
            jax.ShapeDtypeStruct((CAP, cols), F32),
            jax.ShapeDtypeStruct((n * CAP, cols), F32),
            jax.ShapeDtypeStruct((1, 128), jnp.int32),
        ),
        (pivot_row, slab),
    )
    lower = call(
        functools.partial(assemble_kernel, m),
        jax.ShapeDtypeStruct((width * 3 // 4, width), F32),
        tops,
        scratch=[pltpu.VMEM((width, width), F32)],
    )

    def split(leading):
        blocks = leading.reshape(2, -1, cols)
        return blocks[0], blocks[1]

    def levels(lower, gathered, leading, choice):
        span, other, held = n // 2, 2, lower
        while span > 1:
            moved = lax.ppermute(lower, "prow", [(r, tree_partner(r, span)) for r in range(n)])
            lower = call(
                functools.partial(pick_kernel, span),
                jax.ShapeDtypeStruct(lower.shape, F32),
                (moved, held),
            )
            kept, sent = split(leading)
            count = gathered.shape[0]
            message = jnp.concatenate([gathered, sent], axis=0)
            moved = lax.ppermute(message, "prow", [(r, r ^ other) for r in range(n)])
            moved, held = lax.optimization_barrier((moved, lower))
            gathered = jnp.concatenate([gathered, moved[:count]], axis=0)
            leading = jnp.where(me & other != 0, moved[count:], kept)
            span, other = span // 2, other * 2
        pivot_rows = call(order_kernel, jax.ShapeDtypeStruct((width, cols), F32), (choice, gathered))
        inverse = call(
            invert_kernel,
            jax.ShapeDtypeStruct(lower.shape, F32),
            (lower,),
            scratch=[pltpu.VMEM((width, width), F32)],
        )
        moved = lax.ppermute(inverse, "prow", [(r, r ^ 1) for r in range(n)])
        inverse = jnp.where(me & 1 != 0, moved, inverse)
        return leading, call(solve_kernel, jax.ShapeDtypeStruct((width, cols), F32), (inverse, pivot_rows))

    gathered, lower, pivot_row = lax.optimization_barrier((gathered, lower, pivot_row))
    choice = call(
        functools.partial(choice_kernel, n, rows), jax.ShapeDtypeStruct((width, n * CAP), BF16), (pivot_row,)
    )
    twins = [(r, r ^ 1) for r in range(n)]
    moved = lax.ppermute(gathered, "prow", twins)
    gathered = jnp.concatenate([gathered, moved], axis=0)
    kept, sent = split(leading)
    leading = jnp.where(me & 1 != 0, lax.ppermute(sent, "prow", twins), kept)
    leading, upper_rows = unit(me < n, levels, lower, gathered, leading, choice)
    return call(
        functools.partial(update_kernel, m),
        jax.ShapeDtypeStruct((rows, cols), F32),
        (local_rows, leading, upper_rows, slab, *tops, *rests),
        in_specs=[VMEM] * (2 * m + 4),
        out_specs=pl.BlockSpec(memory_space=pl.ANY),
        scratch=[
            pltpu.VMEM((rows + 8, cols), F32),
            pltpu.SMEM((1, 128), jnp.int32),
            pltpu.SemaphoreType.DMA((rows // width + 1,)),
        ],
    )


def solution(mesh):
    return jax.shard_map(
        functools.partial(local, mesh.shape["prow"], mesh.shape["pcol"]),
        mesh=mesh,
        in_specs=(P("prow", "pcol"), P("prow", "pcol"), P()),
        out_specs=P("prow", "pcol"),
        check_vma=False,
    )
```

```python
import functools

import jax
import jax.numpy as jnp
from jax import lax
from jax.experimental import pallas as pl
from jax.experimental.pallas import tpu as pltpu
from jax.sharding import PartitionSpec as P

CAP = 32
BLOCK = 32
F32 = jnp.float32
BF16 = jnp.bfloat16
VMEM = pl.BlockSpec(memory_space=pltpu.VMEM)
PARAMS = pltpu.CompilerParams(vmem_limit_bytes=24 * 1024 * 1024)


def split3(x):
    high = x.astype(BF16)
    rest = x - high.astype(F32)
    mid = rest.astype(BF16)
    low = (rest - mid.astype(F32)).astype(BF16)
    return high, mid, low


def split2(x):
    high = x.astype(BF16)
    return high, (x - high.astype(F32)).astype(BF16)


def select_rows(one_hot, x):
    return sum(jnp.dot(one_hot, part, preferred_element_type=F32) for part in split3(x))


def dot_full(a, b):
    high, mid, low = split3(a)
    left = jnp.concatenate([low, mid, high, mid, high, high], axis=1)
    high, mid, low = split3(b)
    right = jnp.concatenate([high, mid, low, high, mid, high], axis=0)
    return jnp.dot(left, right, preferred_element_type=F32)


def tree_partner(r, span):
    if span == 1 or r % span > 1:
        return r ^ 1
    if r % 2 == 0:
        return r + 1 if r & span else r + span
    return r - span if r & span else r - 1


def lead_place(owner, n):
    bits = n.bit_length() - 1
    return sum((lax.shift_right_logical(owner, bit) & 1) * (1 << (bits - 1 - bit)) for bit in range(bits))


def slots(pivot_row, rows):
    width = pivot_row.shape[1]
    by_sublane = jnp.broadcast_to(pivot_row, (width, width)).T
    shift = rows.bit_length() - 1
    owner_row = jnp.broadcast_to(lax.shift_right_logical(pivot_row, shift), (width, width))
    owner_col = lax.shift_right_logical(by_sublane, shift)
    sub = lax.broadcasted_iota(jnp.int32, (width, width), 0)
    lane = lax.broadcasted_iota(jnp.int32, (width, width), 1)
    same = owner_row == owner_col
    rank_row = jnp.sum(jnp.where(same & (sub < lane), 1, 0), axis=0, keepdims=True)
    rank_col = jnp.sum(jnp.where(same & (lane < sub), 1, 0), axis=1, keepdims=True)
    return owner_row[:1], rank_row, owner_col[:, :1], rank_col


def pack_kernel(pivot_ref, slab_ref, packed_ref, lead_ref, local_ref):
    rows = slab_ref.shape[0]
    width = pivot_ref.shape[1]
    count = lead_ref.shape[0]
    lanes = local_ref.shape[1]
    me = lax.axis_index("prow")
    pivot_row = pivot_ref[...]
    owner_row, rank_row, owner_col, rank_col = slots(pivot_row, rows)
    pivot_col = jnp.broadcast_to(pivot_row, (lanes, width)).T
    slot = lax.broadcasted_iota(jnp.int32, (width, lanes), 1)
    mine = (owner_col == me) & (rank_col == slot)
    local = jnp.sum(jnp.where(mine, pivot_col - (me + 1) * rows, 0), axis=0, keepdims=True) + rows
    local_ref[...] = local
    slot = lax.broadcasted_iota(jnp.int32, (CAP, width), 0)
    mine = (owner_row == me) & (rank_row == slot)
    local = jnp.sum(jnp.where(mine, pivot_row - (me + 1) * rows, 0), axis=1, keepdims=True) + rows
    one_hot = (lax.broadcasted_iota(jnp.int32, (CAP, rows), 1) == local).astype(F32).astype(BF16)
    packed_ref[...] = select_rows(one_hot, slab_ref[...])
    slot = lax.broadcasted_iota(jnp.int32, (count, width), 0)
    one_hot = (slot == lead_place(owner_row, count // CAP) * CAP + rank_row).astype(F32).astype(BF16)
    lead_ref[...] = select_rows(one_hot, slab_ref[:width, :])


def block_inverses(lower):
    width = lower.shape[0]
    lane = lax.broadcasted_iota(jnp.int32, (BLOCK, width), 1)
    sub = lax.broadcasted_iota(jnp.int32, (BLOCK, width), 0)
    block = lane // BLOCK
    within = lane % BLOCK
    diag = jnp.zeros((BLOCK, width), F32)
    for b in range(width // BLOCK):
        diag = jnp.where(block == b, lower[b * BLOCK : (b + 1) * BLOCK], diag)
    diag = jnp.where(within < sub, diag, 0.0)
    inv = jnp.where(within == sub, 1.0, 0.0).astype(F32)
    half, tile = 128, 8
    first = (lax.broadcasted_iota(jnp.int32, (tile, half), 1) // BLOCK) * BLOCK
    starts = range(0, width, half)
    tops = range(0, BLOCK, tile)
    d = [[diag[t : t + tile, h : h + half] for t in tops] for h in starts]
    x = [[inv[t : t + tile, h : h + half] for t in tops] for h in starts]
    for k in range(BLOCK - 1):
        for h in range(len(starts)):
            row = x[h][k // tile][k % tile : k % tile + 1, :]
            for t in range((k + 1) // tile, len(tops)):
                column = jnp.take_along_axis(d[h][t], first + k, axis=1)
                x[h][t] = x[h][t] - column * row
    return [jnp.concatenate(tiles, axis=0) for tiles in x]


def choice_kernel(n, rows, pivot_ref, out_ref):
    _, _, owner_col, rank_col = slots(pivot_ref[...], rows)
    place = jnp.bitwise_xor(owner_col, lax.axis_index("prow")) * CAP + rank_col
    out_ref[...] = (lax.broadcasted_iota(jnp.int32, out_ref.shape, 1) == place).astype(F32).astype(BF16)


def order_kernel(choice_ref, gathered_ref, out_ref):
    out_ref[...] = select_rows(choice_ref[...], gathered_ref[...])


def top_order(m):
    return [0, 1, *range(m - 1, 1, -1)]


def cut_kernel(panel_ref, top_ref, rest_ref, sems):
    width = top_ref.shape[1]
    copies = []
    for c in range(sems.shape[0]):
        target = rest_ref.at[:, pl.ds((c - 1) * width, width)] if c else top_ref
        copies.append(pltpu.make_async_copy(panel_ref.at[:, pl.ds(c * width, width)], target, sems.at[c]))
        copies[-1].start()
    for copy in copies:
        copy.wait()


def assemble_kernel(m, *refs):
    *pieces, out_ref, lower_t = refs
    width = lower_t.shape[0]
    piece = width // m
    half = width // 2
    z = lax.axis_index("pcol")
    for d, ref in zip(top_order(m), pieces):
        lower_t[pl.ds(pl.multiple_of(jnp.bitwise_xor(z, d) * piece, piece), piece), :] = ref[...]
    out_ref[:half, :] = lower_t[:half, :]
    out_ref[half:, :half] = lower_t[half : half + half // 2, half:]
    out_ref[half:, half:] = lower_t[half + half // 2 :, half:]


def pick_kernel(span, moved_ref, held_ref, out_ref):
    child = lax.rem(lax.axis_index("prow"), 2 * span) == span

    @pl.when(child)
    def _():
        out_ref[...] = moved_ref[...]

    @pl.when(jnp.logical_not(child))
    def _():
        out_ref[...] = held_ref[...]


def invert_kernel(lower_ref, out_ref, lower_t):
    holds = lax.axis_index("prow") & 1 == 0

    @pl.when(jnp.logical_not(holds))
    def _():
        out_ref[...] = jnp.zeros_like(out_ref)

    @pl.when(holds)
    def _():
        width = lower_t.shape[0]
        half = width // 2
        lower_t[:half, :] = lower_ref[:half, :]
        lower_t[half:, :half] = jnp.zeros((half, half), F32)
        lower_t[half : half + half // 2, half:] = lower_ref[half:, :half]
        lower_t[half + half // 2 :, half:] = lower_ref[half:, half:]
        lower = lower_t[...].T
        blocks = block_inverses(lower)
        row = lax.broadcasted_iota(jnp.int32, (half, half), 0)
        col = lax.broadcasted_iota(jnp.int32, (half, half), 1)
        for h, strip in enumerate(blocks):
            corner = lower[h * half : (h + 1) * half, h * half : (h + 1) * half]
            inv = jnp.where(row // BLOCK == col // BLOCK, jnp.concatenate([strip] * (half // BLOCK), axis=0), 0.0)
            size = BLOCK
            while size < half:
                off = (row // (2 * size) == col // (2 * size)) & (row // size > col // size)
                inv = inv - dot_full(dot_full(inv, jnp.where(off, corner, 0.0)), inv)
                size *= 2
            out_ref[:half, h * half : (h + 1) * half] = inv
        first, second = out_ref[:half, :half], out_ref[:half, half:]
        quarter = -dot_full(dot_full(second, lower[half:, :half]), first)
        out_ref[half:, :half] = quarter[: half // 2]
        out_ref[half:, half:] = quarter[half // 2 :]


def solve_kernel(inverse_ref, pivot_rows_ref, x_ref):
    half = pivot_rows_ref.shape[0] // 2
    quarter = jnp.concatenate([inverse_ref[half:, :half], inverse_ref[half:, half:]], axis=0)
    lower_half = jnp.concatenate([quarter, inverse_ref[:half, half:]], axis=1)
    x_ref[:half, :] = dot_full(inverse_ref[:half, :half], pivot_rows_ref[:half, :])
    x_ref[half:, :] = dot_full(lower_half, pivot_rows_ref[...])


def product(pieces, upper):
    high, low = zip(*(split2(piece) for piece in pieces))
    high, low = jnp.concatenate(high, axis=0), jnp.concatenate(low, axis=0)
    upper_high, upper_low = upper
    width = upper_high.shape[1]

    def dot(a, b):
        return lax.dot_general(a, b, (((0,), (0,)), ((), ())), preferred_element_type=F32)

    both = dot(high, jnp.concatenate([upper_high, upper_low], axis=1))
    return both[:, :width] + (both[:, width:] + dot(low, upper_high))


def piece_rows(x_ref, m, d):
    piece = x_ref.shape[0] // m
    source = jnp.bitwise_xor(lax.axis_index("pcol"), d)
    return x_ref[pl.ds(pl.multiple_of(source * piece, piece), piece), :]


def update_kernel(m, local_ref, lead_ref, x_ref, slab_ref, *refs):
    *pieces, out_ref, result, swaps, sems = refs
    tops, rests = pieces[:m], pieces[m:]
    rows = slab_ref.shape[0]
    width = x_ref.shape[0]
    blocks = rows // width
    fetch = pltpu.make_async_copy(local_ref, swaps, sems.at[blocks])
    fetch.start()
    result[:rows, :] = slab_ref[...]
    top_upper = split2(jnp.concatenate([piece_rows(x_ref, m, d) for d in top_order(m)], axis=0))
    upper = split2(jnp.concatenate([piece_rows(x_ref, m, d) for d in range(m)], axis=0))
    copies = []
    for c in range(blocks):
        part = pl.ds(c * width, width)
        if c:
            total = product([rest[:, (c - 1) * width : c * width] for rest in rests], upper)
        else:
            total = product([top[...] for top in tops], top_upper)
            fetch.wait()
            for s in range(CAP):
                result[pl.ds(swaps[0, s], 1), :] = lead_ref[pl.ds(s, 1), :]
        result[part, :] = result[part, :] - total
        if c == 0:

            @pl.when(lax.axis_index("prow") == 0)
            def _():
                result[part, :] = x_ref[...]

        copy = pltpu.make_async_copy(result.at[part], out_ref.at[part], sems.at[c])
        copy.start()
        copies.append(copy)
    for copy in copies:
        copy.wait()


def unit(held, steps, *operands):
    shapes = jax.eval_shape(steps, *operands)
    return lax.cond(held, steps, lambda *_: jax.tree.map(lambda s: jnp.zeros(s.shape, s.dtype), shapes), *operands)


def call(kernel, outs, operands, in_specs=None, out_specs=None, scratch=()):
    return pl.pallas_call(
        kernel,
        out_shape=outs,
        in_specs=in_specs or [VMEM] * len(operands),
        out_specs=out_specs or jax.tree.map(lambda _: VMEM, outs),
        scratch_shapes=list(scratch),
        compiler_params=PARAMS,
        cost_estimate=pl.CostEstimate(flops=1, bytes_accessed=1, transcendentals=0),
    )(*operands)


def local(n, m, slab, panel, pivots):
    rows, cols = slab.shape
    width = pivots.shape[0]
    piece = panel.shape[1]
    me = lax.axis_index("prow")
    panel_t = panel.T
    pivot_row = pivots.reshape(1, width)

    def exchange(block, d):
        return lax.ppermute(block, "pcol", [(c, c ^ d) for c in range(m)])

    top, rest = call(
        cut_kernel,
        (jax.ShapeDtypeStruct((piece, width), F32), jax.ShapeDtypeStruct((piece, rows - width), F32)),
        (panel_t,),
        in_specs=[pl.BlockSpec(memory_space=pl.ANY)],
        scratch=[pltpu.SemaphoreType.DMA((rows // width,))],
    )
    tops = [top] + [exchange(top, d) for d in top_order(m)[1:]]
    rests = [rest] + [exchange(rest, d) for d in range(1, m)]

    gathered, leading, local_rows = call(
        pack_kernel,
        (
            jax.ShapeDtypeStruct((CAP, cols), F32),
            jax.ShapeDtypeStruct((n * CAP, cols), F32),
            jax.ShapeDtypeStruct((1, 128), jnp.int32),
        ),
        (pivot_row, slab),
    )
    lower = call(
        functools.partial(assemble_kernel, m),
        jax.ShapeDtypeStruct((width * 3 // 4, width), F32),
        tops,
        scratch=[pltpu.VMEM((width, width), F32)],
    )

    def split(leading):
        blocks = leading.reshape(2, -1, cols)
        return blocks[0], blocks[1]

    def levels(lower, gathered, leading, choice):
        span, other, held = n // 2, 2, lower
        while span > 1:
            moved = lax.ppermute(lower, "prow", [(r, tree_partner(r, span)) for r in range(n)])
            lower = call(
                functools.partial(pick_kernel, span),
                jax.ShapeDtypeStruct(lower.shape, F32),
                (moved, held),
            )
            kept, sent = split(leading)
            count = gathered.shape[0]
            message = jnp.concatenate([gathered, sent], axis=0)
            moved = lax.ppermute(message, "prow", [(r, r ^ other) for r in range(n)])
            moved, held = lax.optimization_barrier((moved, lower))
            gathered = jnp.concatenate([gathered, moved[:count]], axis=0)
            leading = jnp.where(me & other != 0, moved[count:], kept)
            span, other = span // 2, other * 2
        pivot_rows = call(order_kernel, jax.ShapeDtypeStruct((width, cols), F32), (choice, gathered))
        inverse = call(
            invert_kernel,
            jax.ShapeDtypeStruct(lower.shape, F32),
            (lower,),
            scratch=[pltpu.VMEM((width, width), F32)],
        )
        moved = lax.ppermute(inverse, "prow", [(r, r ^ 1) for r in range(n)])
        inverse = jnp.where(me & 1 != 0, moved, inverse)
        return leading, call(solve_kernel, jax.ShapeDtypeStruct((width, cols), F32), (inverse, pivot_rows))

    gathered, lower, pivot_row = lax.optimization_barrier((gathered, lower, pivot_row))
    choice = call(
        functools.partial(choice_kernel, n, rows), jax.ShapeDtypeStruct((width, n * CAP), BF16), (pivot_row,)
    )
    twins = [(r, r ^ 1) for r in range(n)]
    moved = lax.ppermute(gathered, "prow", twins)
    gathered = jnp.concatenate([gathered, moved], axis=0)
    kept, sent = split(leading)
    leading = jnp.where(me & 1 != 0, lax.ppermute(sent, "prow", twins), kept)
    leading, upper_rows = unit(me < n, levels, lower, gathered, leading, choice)
    return call(
        functools.partial(update_kernel, m),
        jax.ShapeDtypeStruct((rows, cols), F32),
        (local_rows, leading, upper_rows, slab, *tops, *rests),
        in_specs=[VMEM] * (2 * m + 4),
        out_specs=pl.BlockSpec(memory_space=pl.ANY),
        scratch=[
            pltpu.VMEM((rows + 8, cols), F32),
            pltpu.SMEM((1, 128), jnp.int32),
            pltpu.SemaphoreType.DMA((rows // width + 1,)),
        ],
    )


def solution(mesh):
    return jax.shard_map(
        functools.partial(local, mesh.shape["prow"], mesh.shape["pcol"]),
        mesh=mesh,
        in_specs=(P("prow", "pcol"), P("prow", "pcol"), P()),
        out_specs=P("prow", "pcol"),
        check_vma=False,
    )
```
